512 devices in a mesh: seq: 32 (over z, core), tp: 16 (over y, x).
Axes of the slice: x: 4, y: 4, z: 16, core: 2. Of those that a mesh axis runs over, the one named last changes fastest.
Arguments:
- inner_x: bfloat16 [12288, 8192], P('seq', 'tp'), may hold values from -9 to 9
- gate_z: bfloat16 [12288, 8192], P('seq', 'tp'), may hold values from -6 to 6
- bc_input: bfloat16 [12288, 256], P('seq'), may hold values from -3 to 3
- conv_inner: float32 [4, 8192], P(None, 'tp'), may hold values from -3 to 3
- conv_bc: float32 [4, 256], replicated, may hold values from -1.5 to 1.5
- step_size: float32 [128, 12288], P('tp', 'seq'), may hold values from 0 to 3
- log_decay: float32 [128, 12288], P('tp', 'seq'), may hold values from -0.8 to 0
- skip_gain: float32 [128], P('tp'), may hold values from 0.5 to 1.5
- norm_gain: float32 [8192], P('tp'), may hold values from 0.1 to 1.9
- out_weight: bfloat16 [8192, 2048], P('tp'), may hold values from -0.0625 to 0.0625
Outputs:
- mixed: bfloat16 [12288, 2048], P('seq', 'tp')
The draws below stay inside these ranges and needn't reach their ends.
All inputs are finite; a program needn't handle non-finite values.
Results may differ from the reference program's by a relative error of at most 0.015.
Values may be sent and summed in bfloat16 or wider, within the bound.
No kernel may reach another device: no remote copies, remote signals or barrier semaphores. Data moves between devices by JAX's collectives and lax.ppermute only.
A program may use at most 64 MiB of HBM per device.

```python
import jax
import jax.numpy as jnp
from jax import lax

HEADS = 128
P_SIZE = 64
N = 128
DOUT = 2048
TOK_DEV = 384
TOKENS = 12288
INNER = 8192


def decay_rates(key, fast_share):
    base_key = jax.random.fold_in(key, 7)
    key_fast, key_fbase, key_sbase, seed_segment, key_token = jax.random.split(base_key, 5)
    fast_heads = jax.random.bernoulli(key_fast, fast_share, (HEADS,))
    fast_base = jnp.exp(jax.random.uniform(key_fbase, (HEADS,), jnp.float32, jnp.log(1.0 / 50.0), jnp.log(1.0 / 30.0)))
    slow_base = jnp.exp(jax.random.uniform(key_sbase, (HEADS,), jnp.float32, jnp.log(0.05), jnp.log(0.15))) / TOKENS
    base_rate = jnp.where(fast_heads, fast_base, slow_base)
    block_factor = jnp.exp(jax.random.uniform(seed_segment, (HEADS, TOKENS // TOK_DEV), jnp.float32, jnp.log(0.5), jnp.log(2.0)))
    block_factor = jnp.repeat(block_factor, TOK_DEV, axis=1)
    token_factor = jnp.exp(jax.random.uniform(key_token, (HEADS, TOKENS), jnp.float32, jnp.log(0.7), jnp.log(1.4)))
    return base_rate[:, None] * block_factor * token_factor


def draw_log_decay(key, part):
    probability_levels = decay_rates(key, 0.5)
    own_key = jax.random.fold_in(key, 11)
    key_spots, key_loss = jax.random.split(own_key)
    chosen_locations = jax.random.randint(key_spots, (3,), 0, TOKENS)
    dropout_draws = jax.random.uniform(key_loss, (3,), jnp.float32, 0.22, 0.6)
    landing_offsets = jnp.arange(TOKENS)
    spike_happenings = jnp.sum((landing_offsets[None, :] == chosen_locations[:, None]).astype(jnp.float32) * dropout_draws[:, None], axis=0)
    return -(probability_levels + spike_happenings[None, :])


def draw_step_size(key, part):
    probability_levels = decay_rates(key, 0.5)
    own_key = jax.random.fold_in(key, 13)
    factor = jnp.exp(jax.random.uniform(own_key, (HEADS, TOKENS), jnp.float32, jnp.log(0.5), jnp.log(1.5)))
    return jnp.sqrt(40.0 * probability_levels) * factor


def draw_inner_x(key, part):
    own_key = jax.random.fold_in(key, 5)
    key_column_span, key_vals = jax.random.split(own_key, 2)
    ramp = 3.0 ** (jnp.arange(INNER).astype(jnp.float32) / INNER)
    column_scale = ramp * jnp.exp(jax.random.uniform(key_column_span, (INNER,), jnp.float32, jnp.log(0.6), jnp.log(2.0)))
    values = jnp.clip(jax.random.normal(key_vals, (TOKENS, INNER), jnp.float32), -3.0, 3.0)
    return (0.4 * values * column_scale[None, :]).astype(jnp.bfloat16)


def block_levels(rng, extent, pieces, low, high):
    def one(dim, blocks):
        heights = jax.random.uniform(jax.random.fold_in(jax.random.fold_in(rng, 6), dim), (blocks,), jnp.float32, low / len(pieces), high / len(pieces))
        return jnp.repeat(jnp.exp(heights), extent[dim] // blocks).reshape((-1,) + (1,) * (len(extent) - dim - 1))

    factor_of = one(*pieces[0])
    for cut in pieces[1:]:
        factor_of = factor_of * one(*cut)
    return factor_of


def scatter_about(stream_key, extent, scale, bound, pieces=(), dtype=jnp.bfloat16):
    entries = scale * jax.random.normal(stream_key, extent, jnp.float32)
    if pieces:
        entries = entries * block_levels(stream_key, extent, pieces, -0.22, 0.18)
    return jnp.clip(entries, -bound, bound).astype(dtype)


def setup_inputs(seed: int = 0) -> dict:
    key_of = jax.random.split(jax.random.key(seed), 11)
    return {
        "inner_x": draw_inner_x(jax.random.fold_in(key_of[10], 71), 0),
        "gate_z": scatter_about(key_of[1], (TOKENS, INNER), 1.0, 6.0, ((0, 32), (1, 16))),
        "bc_input": scatter_about(key_of[2], (TOKENS, 2 * N), 0.5, 3.0, ((0, 32),)),
        "conv_inner": scatter_about(key_of[3], (4, INNER), 4 ** -0.5, 3.0, ((1, 16),), jnp.float32),
        "conv_bc": scatter_about(key_of[4], (4, 2 * N), 0.25, 1.5, (), jnp.float32),
        "step_size": draw_step_size(jax.random.fold_in(key_of[10], 71), 0),
        "log_decay": draw_log_decay(jax.random.fold_in(key_of[10], 71), 0),
        "skip_gain": jnp.clip(0.5 + 1.0 * jax.random.uniform(key_of[7], (HEADS,), jnp.float32) ** block_levels(key_of[7], (HEADS,), ((0, 16),), -0.2, 0.2), 0.5, 1.5),
        "norm_gain": jnp.clip(1.0 + 0.18 * jax.random.normal(key_of[8], (INNER,), jnp.float32), 0.1, 1.9),
        "out_weight": scatter_about(key_of[9], (INNER, DOUT), INNER ** -0.5, 0.0625, ((0, 16),)),
    }


def filtered_sigmoid_linear(leading, block, weights):
    whole = jnp.concatenate([leading, block], axis=0).astype(jnp.float32)
    length = block.shape[0]
    summed = weights[0] * whole[0:length]
    for offset in range(1, 4):
        summed = summed + weights[offset] * whole[offset:offset + length]
    return jax.nn.silu(summed).astype(jnp.bfloat16)

def local_ssd(inner_act, b_rows, c_rows, step_size, log_decay, skip_gain):
    length = inner_act.shape[0]
    cumulative = jnp.cumsum(log_decay, axis=1)
    scaled = (inner_act.astype(jnp.float32) * step_size.T[:, :, None]).astype(jnp.bfloat16)
    scores = jnp.dot(c_rows.astype(jnp.float32), b_rows.astype(jnp.float32).T, preferred_element_type=jnp.float32)
    token_position = jnp.arange(length)
    causal_mask = token_position[:, None] >= token_position[None, :]
    spread = cumulative[:, :, None] - cumulative[:, None, :]
    decays = jnp.exp(jnp.where(causal_mask[None], spread, -jnp.inf))
    mixing = (scores[None] * decays).astype(jnp.bfloat16)
    within = jnp.einsum('hts,shp->thp', mixing.astype(jnp.float32), scaled.astype(jnp.float32))
    tail = jnp.exp(cumulative[:, -1:] - cumulative)
    weighted = (scaled.astype(jnp.float32) * tail.T[:, :, None]).astype(jnp.bfloat16)
    summary = jnp.einsum('shp,sn->hpn', weighted.astype(jnp.float32), b_rows.astype(jnp.float32))
    local_out = within + skip_gain[None, :, None] * inner_act.astype(jnp.float32)
    return (local_out, cumulative, summary, jnp.exp(cumulative[:, -1]))

def carried(cumulative, c_rows, incoming):
    product = jnp.einsum('tn,hpn->thp', c_rows.astype(jnp.float32), incoming, precision=lax.Precision.HIGHEST)
    return jnp.exp(cumulative).T[:, :, None] * product

def reference(inner_x, gate_z, bc_input, conv_inner, conv_bc, step_size, log_decay, skip_gain, norm_gain, out_weight):
    inner_all = filtered_sigmoid_linear(jnp.zeros((3, INNER), jnp.bfloat16), inner_x, conv_inner)
    bc_all = filtered_sigmoid_linear(jnp.zeros((3, 2 * N), jnp.bfloat16), bc_input, conv_bc)
    blocks_count = TOKENS // TOK_DEV
    items = (inner_all.reshape(blocks_count, TOK_DEV, INNER), bc_all.reshape(blocks_count, TOK_DEV, 2 * N), gate_z.reshape(blocks_count, TOK_DEV, INNER), step_size.reshape(HEADS, blocks_count, TOK_DEV).transpose(1, 0, 2), log_decay.reshape(HEADS, blocks_count, TOK_DEV).transpose(1, 0, 2))
    weight_f = out_weight.astype(jnp.float32)

    def march_forward(state, item):
        inner_blk, bc_blk, gate_blk, step_blk, decay_blk = item
        b_rows = bc_blk[:, :N]
        c_rows = bc_blk[:, N:]
        local_out, cumulative, summary, decay_total = local_ssd(inner_blk.reshape(TOK_DEV, HEADS, P_SIZE), b_rows, c_rows, step_blk, decay_blk, skip_gain)
        output = (local_out + carried(cumulative, c_rows, state)).reshape(TOK_DEV, INNER)
        gated = output * jax.nn.silu(gate_blk.astype(jnp.float32))
        meansq = lax.optimization_barrier(jnp.sum(gated * gated, axis=1)) / INNER
        normed = (gated * lax.rsqrt(meansq + 1e-05)[:, None] * norm_gain).astype(jnp.bfloat16)
        block_out = jnp.dot(normed.astype(jnp.float32), weight_f, preferred_element_type=jnp.float32).astype(jnp.bfloat16)
        new_state = decay_total[:, None, None] * state + summary
        return (new_state, block_out)
    _, mixed = lax.scan(march_forward, jnp.zeros((HEADS, P_SIZE, N), jnp.float32), items)
    return mixed.reshape(TOKENS, DOUT)
```

```python
import jax
import jax.numpy as jnp
from jax import lax
from jax.experimental import pallas as pl
from jax.experimental.pallas import tpu as pltpu
from jax.sharding import PartitionSpec as P

INNER = 8192
HEADS = 8
HEAD = 64
WIDTH = HEADS * HEAD
STATE = 128
LENGTH = 384
BLOCK = 128
BLOCKS = 32
GROUP = 8
SHARES = 16
EXTRA = 16

f32 = jnp.float32
bf16 = jnp.bfloat16


def parts3(a):
    high = a.astype(bf16)
    rest = a - high.astype(f32)
    middle = rest.astype(bf16)
    low = (rest - middle.astype(f32)).astype(bf16)
    return high, middle, low


def silu(a):
    return a * jax.nn.sigmoid(a)


def dot(a, b):
    return lax.dot_general(a, b, (((1,), (0,)), ((), ())), preferred_element_type=f32)


def columns_of(rows):
    padded = jnp.concatenate([rows, jnp.zeros((128 - rows.shape[0], LENGTH), f32)], axis=0)
    return padded.T


def spread_heads(columns):
    head = lax.broadcasted_iota(jnp.int32, (128, WIDTH), 0)
    channel = lax.broadcasted_iota(jnp.int32, (128, WIDTH), 1)
    chosen = jnp.where(channel // HEAD == head, 1.0, 0.0).astype(bf16)
    high, middle, low = parts3(columns)
    return dot(high, chosen) + (dot(middle, chosen) + dot(low, chosen))


def convolved(ext, weights):
    total = weights[0:1] * ext[5 : 5 + LENGTH]
    for k in range(1, 4):
        total = total + weights[k : k + 1] * ext[5 + k : 5 + k + LENGTH]
    return silu(total).astype(bf16)


def summary_kernel(
    x_ref, bc_ref, halo_ref, cx_ref, cbc_ref, step_ref, decay_ref,
    message_ref, act_ref, bc_act_ref, cum_ref, ext_x, ext_bc,
):
    halo = halo_ref[...].astype(f32)[8:16]
    ext_x[0:8] = halo[:, :WIDTH]
    ext_bc[0:8] = halo[:, WIDTH:]
    ext_x[8:] = x_ref[...].astype(f32)
    ext_bc[8:] = bc_ref[...].astype(f32)
    bc_act = convolved(ext_bc, cbc_ref)
    bc_act_ref[...] = bc_act
    act = convolved(ext_x, cx_ref)
    act_ref[...] = act

    s_at = lax.broadcasted_iota(jnp.int32, (LENGTH, LENGTH), 0)
    t_at = lax.broadcasted_iota(jnp.int32, (LENGTH, LENGTH), 1)
    upto = jnp.where(s_at <= t_at, 1.0, 0.0).astype(bf16)
    high, middle, low = parts3(decay_ref[...])
    cum = dot(high, upto) + (dot(middle, upto) + dot(low, upto))
    cum_ref[...] = cum
    last = cum[:, LENGTH - 1 : LENGTH]
    factor = step_ref[...] * jnp.exp(last - cum)
    weighted = (act.astype(f32) * spread_heads(columns_of(factor))).astype(bf16)
    b_rows = bc_act[:, :STATE].astype(f32)
    summary = dot(b_rows.T.astype(bf16), weighted)

    total = jnp.broadcast_to(jnp.exp(last), (HEADS, 128))
    low_lanes = lax.broadcasted_iota(jnp.int32, (HEAD, 128), 1) < HEAD
    row_at = lax.broadcasted_iota(jnp.int32, (EXTRA, 128), 0)
    for pair in range(HEADS // 2):
        top = summary[:HEAD, 128 * pair : 128 * (pair + 1)]
        bottom = summary[HEAD:, 128 * pair : 128 * (pair + 1)]
        even = jnp.where(low_lanes, top, pltpu.roll(bottom, HEAD, 1))
        odd = jnp.where(low_lanes, pltpu.roll(top, HEAD, 1), bottom)
        message_ref[2 * pair, 0:HEAD] = even.astype(bf16)
        message_ref[2 * pair + 1, 0:HEAD] = odd.astype(bf16)
    for h in range(HEADS):
        high, middle, low = (p.astype(f32) for p in parts3(total[h : h + 1]))
        rows = jnp.where(row_at == 0, high, jnp.where(row_at == 1, middle, jnp.where(row_at == 2, low, 0.0)))
        message_ref[h, HEAD:] = rows.astype(bf16)


def within_kernel(
    act_ref, bc_act_ref, cum_ref, step_ref, skip_ref, z_ref, local_ref, gate_ref
):
    cum = cum_ref[...]
    cum_columns = columns_of(cum)
    act = act_ref[...].astype(f32)
    scaled = (act * spread_heads(columns_of(step_ref[...]))).astype(bf16)
    gate = silu(z_ref[...].astype(f32))
    gate_ref[...] = gate * spread_heads(jnp.exp(cum_columns))
    b_rows = bc_act_ref[:, :STATE]
    c_rows = bc_act_ref[:, STATE:]
    skipped = skip_ref[...] * act
    t_at = lax.broadcasted_iota(jnp.int32, (BLOCK, BLOCK), 0)
    s_at = lax.broadcasted_iota(jnp.int32, (BLOCK, BLOCK), 1)
    causal = t_at >= s_at
    low_lanes = lax.broadcasted_iota(jnp.int32, (BLOCK, 128), 1) < HEAD
    for block in range(LENGTH // BLOCK):
        rows = slice(block * BLOCK, (block + 1) * BLOCK)
        scores = lax.dot_general(
            c_rows[rows], b_rows[: (block + 1) * BLOCK], (((1,), (1,)), ((), ())), preferred_element_type=f32
        )
        for pair in range(HEADS // 2):
            lanes = slice(128 * pair, 128 * (pair + 1))
            sums = []
            for h in (2 * pair, 2 * pair + 1):
                here = cum_columns[rows, h : h + 1]
                tiles = []
                for other in range(block + 1):
                    columns = slice(other * BLOCK, (other + 1) * BLOCK)
                    spread = here - cum[h : h + 1, columns]
                    if other == block:
                        spread = jnp.where(causal, spread, -jnp.inf)
                    tiles.append((scores[:, columns] * jnp.exp(spread)).astype(bf16))
                mixing = tiles[0] if block == 0 else jnp.concatenate(tiles, axis=1)
                sums.append(dot(mixing, scaled[: (block + 1) * BLOCK, lanes]))
            within = jnp.where(low_lanes, sums[0], sums[1])
            local_ref[rows, lanes] = (within + skipped[rows, lanes]) * gate[rows, lanes]


def prefix_kernel(message_ref, prefix_ref, scale_ref, total_ref):
    state = jnp.zeros((HEAD, 128), f32)
    scale = jnp.ones((8, 128), f32)
    for m in range(GROUP):
        prefix_ref[m] = state
        scale_ref[m] = scale
        rows = message_ref[m, HEAD:].astype(f32)
        decay = rows[0:1] + (rows[1:2] + rows[2:3])
        state = decay * state + message_ref[m, 0:HEAD].astype(f32)
        scale = decay * scale
    total_ref[0:HEAD] = state.astype(bf16)
    row_at = lax.broadcasted_iota(jnp.int32, (EXTRA, 128), 0)
    high, middle, low = (p.astype(f32)[0:1] for p in parts3(scale))
    rows = jnp.where(row_at == 0, high, jnp.where(row_at == 1, middle, jnp.where(row_at == 2, low, 0.0)))
    total_ref[HEAD:] = rows.astype(bf16)


def entering_kernel(prefix_ref, scale_ref, near_ref, next_ref, far_ref, state_ref):
    entering = far_ref[0:HEAD].astype(f32)
    for ref in (next_ref, near_ref):
        rows = ref[HEAD:].astype(f32)
        decay = rows[0:1] + (rows[1:2] + rows[2:3])
        entering = decay * entering + ref[0:HEAD].astype(f32)
    for m in range(GROUP):
        state_ref[m] = (prefix_ref[m] + scale_ref[m, 0:1] * entering).astype(bf16)


def output_kernel(state_ref, bc_act_ref, local_ref, gate_ref, gain_ref, weight_ref, share_ref):
    low_lanes = lax.broadcasted_iota(jnp.int32, (HEAD, 128), 1) < HEAD
    pairs = []
    for pair in range(HEADS // 2):
        even = state_ref[2 * pair].astype(f32)
        odd = state_ref[2 * pair + 1].astype(f32)
        top = jnp.where(low_lanes, even, pltpu.roll(odd, HEAD, 1))
        bottom = jnp.where(low_lanes, pltpu.roll(even, HEAD, 1), odd)
        pairs.append(jnp.concatenate([top, bottom], axis=0).astype(bf16))
    states = jnp.concatenate(pairs, axis=1)
    carried = dot(bc_act_ref[:, STATE:], states)
    gated = local_ref[...] + gate_ref[...] * carried
    squares = jnp.sum(gated * gated, axis=1, keepdims=True)
    scaled = (gated * gain_ref[...]).astype(bf16)
    wide = jnp.broadcast_to(squares, (LENGTH, 128))
    row_at = lax.broadcasted_iota(jnp.int32, (EXTRA, 128), 0)
    extra = jnp.zeros((EXTRA, 128), f32)
    for block in range(LENGTH // BLOCK):
        row = wide[block * BLOCK : (block + 1) * BLOCK].T[0:1]
        for k, part in enumerate(parts3(row)):
            extra = jnp.where(row_at == 3 * block + k, part.astype(f32), extra)
    extra = extra.astype(bf16)
    for pair in range(SHARES // 2):
        product = dot(scaled, weight_ref[:, 256 * pair : 256 * (pair + 1)]).astype(bf16)
        share_ref[2 * pair, 0:LENGTH] = product[:, :128]
        share_ref[2 * pair, LENGTH:] = extra
        share_ref[2 * pair + 1, 0:LENGTH] = product[:, 128:]
        share_ref[2 * pair + 1, LENGTH:] = extra


def sum_kernel(share_ref, out_ref):
    total = share_ref[0].astype(f32)
    for d in range(1, SHARES):
        total = total + share_ref[d].astype(f32)
    extra = total[LENGTH:]
    for block in range(LENGTH // BLOCK):
        rows = slice(block * BLOCK, (block + 1) * BLOCK)
        squares = extra[3 * block : 3 * block + 1] + (
            extra[3 * block + 1 : 3 * block + 2] + extra[3 * block + 2 : 3 * block + 3]
        )
        scale = lax.rsqrt(squares / INNER + 1e-05)
        column = jnp.broadcast_to(scale, (128, 128)).T
        out_ref[rows] = (total[rows] * column).astype(bf16)


def call(kernel, outs, *args, scratch=(), flops=1e8, transcendentals=0):
    whole = pl.BlockSpec(memory_space=pltpu.VMEM)
    return pl.pallas_call(
        kernel,
        out_shape=[jax.ShapeDtypeStruct(s, d) for s, d in outs],
        in_specs=[whole] * len(args),
        out_specs=[whole] * len(outs),
        scratch_shapes=list(scratch),
        compiler_params=pltpu.CompilerParams(vmem_limit_bytes=32 * 1024 * 1024),
        cost_estimate=pl.CostEstimate(
            flops=int(flops), bytes_accessed=2_000_000, transcendentals=int(transcendentals)
        ),
    )(*args)


def shards(
    inner_x, gate_z, bc_input, conv_inner, conv_bc, step_size, log_decay, skip_gain, norm_gain, out_weight
):
    tail = jnp.concatenate([inner_x[LENGTH - 16 :], bc_input[LENGTH - 16 :]], axis=1)
    halo = lax.ppermute(tail, "seq", [(i, i + 1) for i in range(BLOCKS - 1)])
    message, act, bc_act, cum = call(
        summary_kernel,
        [((HEADS, HEAD + EXTRA, 128), bf16), ((LENGTH, WIDTH), bf16), ((LENGTH, 2 * STATE), bf16), ((HEADS, LENGTH), f32)],
        inner_x, bc_input, halo, conv_inner, conv_bc, step_size, log_decay,
        scratch=[pltpu.VMEM((LENGTH + 8, WIDTH), f32), pltpu.VMEM((LENGTH + 8, 2 * STATE), f32)],
    )
    groups = [list(range(i, i + GROUP)) for i in range(0, BLOCKS, GROUP)]
    message = lax.all_to_all(message, "seq", 0, 0, tiled=True, axis_index_groups=groups)
    skip = jnp.repeat(skip_gain, HEAD)[None, :]
    local, gate = call(
        within_kernel,
        [((LENGTH, WIDTH), f32), ((LENGTH, WIDTH), f32)],
        act, bc_act, cum, step_size, skip, gate_z,
        flops=2e9, transcendentals=1.2e6,
    )
    prefix, scale, total = call(
        prefix_kernel,
        [((GROUP, HEAD, 128), f32), ((GROUP, 8, 128), f32), ((HEAD + EXTRA, 128), bf16)],
        message,
    )
    near, after, far = (
        lax.ppermute(total, "seq", [(i, i + d) for i in range(BLOCKS - d)]) for d in (GROUP, 2 * GROUP, 3 * GROUP)
    )
    (state,) = call(entering_kernel, [((GROUP, HEAD, 128), bf16)], prefix, scale, near, after, far)
    state = lax.all_to_all(state, "seq", 0, 0, tiled=True, axis_index_groups=groups)
    (share,) = call(
        output_kernel,
        [((SHARES, LENGTH + EXTRA, 128), bf16)],
        state, bc_act, local, gate, norm_gain[None, :], out_weight,
        flops=9e8,
    )
    share = lax.all_to_all(share, "tp", 0, 0, tiled=True)
    (mixed,) = call(sum_kernel, [((LENGTH, 128), bf16)], share)
    return mixed


def solution(mesh):
    in_specs = (
        P("seq", "tp"),
        P("seq", "tp"),
        P("seq", None),
        P(None, "tp"),
        P(),
        P("tp", "seq"),
        P("tp", "seq"),
        P("tp"),
        P("tp"),
        P("tp", None),
    )
    return jax.shard_map(shards, mesh=mesh, in_specs=in_specs, out_specs=P("seq", "tp"), check_vma=False)
```

```python
import jax
import jax.numpy as jnp
from jax import lax
from jax.experimental import pallas as pl
from jax.experimental.pallas import tpu as pltpu
from jax.sharding import PartitionSpec as P

INNER = 8192
HEADS = 8
HEAD = 64
WIDTH = HEADS * HEAD
STATE = 128
LENGTH = 384
BLOCK = 128
BLOCKS = 32
GROUP = 8
SHARES = 16
EXTRA = 16

f32 = jnp.float32
bf16 = jnp.bfloat16


def parts3(a):
    high = a.astype(bf16)
    rest = a - high.astype(f32)
    middle = rest.astype(bf16)
    low = (rest - middle.astype(f32)).astype(bf16)
    return high, middle, low


def silu(a):
    return a * jax.nn.sigmoid(a)


def dot(a, b):
    return lax.dot_general(a, b, (((1,), (0,)), ((), ())), preferred_element_type=f32)


def columns_of(rows):
    padded = jnp.concatenate([rows, jnp.zeros((128 - rows.shape[0], LENGTH), f32)], axis=0)
    return padded.T


def spread_heads(columns):
    head = lax.broadcasted_iota(jnp.int32, (128, WIDTH), 0)
    channel = lax.broadcasted_iota(jnp.int32, (128, WIDTH), 1)
    chosen = jnp.where(channel // HEAD == head, 1.0, 0.0).astype(bf16)
    high, middle, low = parts3(columns)
    return dot(high, chosen) + (dot(middle, chosen) + dot(low, chosen))


def convolved(ext, weights):
    total = weights[0:1] * ext[5 : 5 + LENGTH]
    for k in range(1, 4):
        total = total + weights[k : k + 1] * ext[5 + k : 5 + k + LENGTH]
    return silu(total).astype(bf16)


def fetch(pairs, sems):
    copies = [pltpu.make_async_copy(there, here, sems.at[i]) for i, (there, here) in enumerate(pairs)]
    for copy in copies:
        copy.start()
    return copies


def summary_kernel(
    x_at, bc_at, halo_ref, cx_at, cbc_at, step_at, decay_at,
    message_ref, act_ref, bc_act_ref, cum_ref,
    ext_x, ext_bc, x_ref, bc_ref, cx_ref, cbc_ref, step_ref, decay_ref, sems,
):
    for copy in fetch(
        [(decay_at, decay_ref), (step_at, step_ref), (cx_at, cx_ref), (cbc_at, cbc_ref), (bc_at, bc_ref), (x_at, x_ref)],
        sems,
    ):
        copy.wait()
    halo = halo_ref[...].astype(f32)[8:16]
    ext_x[0:8] = halo[:, :WIDTH]
    ext_bc[0:8] = halo[:, WIDTH:]
    ext_x[8:] = x_ref[...].astype(f32)
    ext_bc[8:] = bc_ref[...].astype(f32)
    bc_act = convolved(ext_bc, cbc_ref)
    bc_act_ref[...] = bc_act
    act = convolved(ext_x, cx_ref)
    act_ref[...] = act

    s_at = lax.broadcasted_iota(jnp.int32, (LENGTH, LENGTH), 0)
    t_at = lax.broadcasted_iota(jnp.int32, (LENGTH, LENGTH), 1)
    upto = jnp.where(s_at <= t_at, 1.0, 0.0).astype(bf16)
    high, middle, low = parts3(decay_ref[...])
    cum = dot(high, upto) + (dot(middle, upto) + dot(low, upto))
    cum_ref[...] = cum
    last = cum[:, LENGTH - 1 : LENGTH]
    factor = step_ref[...] * jnp.exp(last - cum)
    weighted = (act.astype(f32) * spread_heads(columns_of(factor))).astype(bf16)
    b_rows = bc_act[:, :STATE].astype(f32)
    summary = dot(b_rows.T.astype(bf16), weighted)

    total = jnp.broadcast_to(jnp.exp(last), (HEADS, 128))
    low_lanes = lax.broadcasted_iota(jnp.int32, (HEAD, 128), 1) < HEAD
    row_at = lax.broadcasted_iota(jnp.int32, (EXTRA, 128), 0)
    for pair in range(HEADS // 2):
        top = summary[:HEAD, 128 * pair : 128 * (pair + 1)]
        bottom = summary[HEAD:, 128 * pair : 128 * (pair + 1)]
        even = jnp.where(low_lanes, top, pltpu.roll(bottom, HEAD, 1))
        odd = jnp.where(low_lanes, pltpu.roll(top, HEAD, 1), bottom)
        message_ref[2 * pair, 0:HEAD] = even.astype(bf16)
        message_ref[2 * pair + 1, 0:HEAD] = odd.astype(bf16)
    for h in range(HEADS):
        high, middle, low = (p.astype(f32) for p in parts3(total[h : h + 1]))
        rows = jnp.where(row_at == 0, high, jnp.where(row_at == 1, middle, jnp.where(row_at == 2, low, 0.0)))
        message_ref[h, HEAD:] = rows.astype(bf16)


def within_kernel(
    act_ref, bc_act_ref, cum_ref, step_at, skip_ref, z_at, gain_at, local_ref, gate_ref, gain_ref,
    step_ref, z_ref, sems,
):
    for copy in fetch([(step_at, step_ref), (z_at, z_ref), (gain_at, gain_ref)], sems):
        copy.wait()
    head_at = lax.broadcasted_iota(jnp.int32, (1, WIDTH), 1) // HEAD
    skip = jnp.zeros((1, WIDTH), f32)
    for h in range(HEADS):
        skip = jnp.where(head_at == h, skip_ref[h], skip)
    cum = cum_ref[...]
    cum_columns = columns_of(cum)
    act = act_ref[...].astype(f32)
    scaled = (act * spread_heads(columns_of(step_ref[...]))).astype(bf16)
    gate = silu(z_ref[...].astype(f32))
    gate_ref[...] = gate * spread_heads(jnp.exp(cum_columns))
    b_rows = bc_act_ref[:, :STATE]
    c_rows = bc_act_ref[:, STATE:]
    skipped = skip * act
    t_at = lax.broadcasted_iota(jnp.int32, (BLOCK, BLOCK), 0)
    s_at = lax.broadcasted_iota(jnp.int32, (BLOCK, BLOCK), 1)
    causal = t_at >= s_at
    low_lanes = lax.broadcasted_iota(jnp.int32, (BLOCK, 128), 1) < HEAD
    for block in range(LENGTH // BLOCK):
        rows = slice(block * BLOCK, (block + 1) * BLOCK)
        scores = lax.dot_general(
            c_rows[rows], b_rows[: (block + 1) * BLOCK], (((1,), (1,)), ((), ())), preferred_element_type=f32
        )
        for pair in range(HEADS // 2):
            lanes = slice(128 * pair, 128 * (pair + 1))
            sums = []
            for h in (2 * pair, 2 * pair + 1):
                here = cum_columns[rows, h : h + 1]
                tiles = []
                for other in range(block + 1):
                    columns = slice(other * BLOCK, (other + 1) * BLOCK)
                    spread = here - cum[h : h + 1, columns]
                    if other == block:
                        spread = jnp.where(causal, spread, -jnp.inf)
                    tiles.append((scores[:, columns] * jnp.exp(spread)).astype(bf16))
                mixing = tiles[0] if block == 0 else jnp.concatenate(tiles, axis=1)
                sums.append(dot(mixing, scaled[: (block + 1) * BLOCK, lanes]))
            within = jnp.where(low_lanes, sums[0], sums[1])
            local_ref[rows, lanes] = (within + skipped[rows, lanes]) * gate[rows, lanes]


def prefix_kernel(message_ref, prefix_ref, scale_ref, total_ref):
    state = jnp.zeros((HEAD, 128), f32)
    scale = jnp.ones((8, 128), f32)
    for m in range(GROUP):
        prefix_ref[m] = state
        scale_ref[m] = scale
        rows = message_ref[m, HEAD:].astype(f32)
        decay = rows[0:1] + (rows[1:2] + rows[2:3])
        state = decay * state + message_ref[m, 0:HEAD].astype(f32)
        scale = decay * scale
    total_ref[0:HEAD] = state.astype(bf16)
    row_at = lax.broadcasted_iota(jnp.int32, (EXTRA, 128), 0)
    high, middle, low = (p.astype(f32)[0:1] for p in parts3(scale))
    rows = jnp.where(row_at == 0, high, jnp.where(row_at == 1, middle, jnp.where(row_at == 2, low, 0.0)))
    total_ref[HEAD:] = rows.astype(bf16)


def entering_kernel(prefix_ref, scale_ref, far_ref, near_ref, next_ref, state_ref):
    entering = far_ref[0:HEAD].astype(f32)
    for ref in (next_ref, near_ref):
        rows = ref[HEAD:].astype(f32)
        decay = rows[0:1] + (rows[1:2] + rows[2:3])
        entering = decay * entering + ref[0:HEAD].astype(f32)
    for m in range(GROUP):
        state_ref[m] = (prefix_ref[m] + scale_ref[m, 0:1] * entering).astype(bf16)


def output_kernel(state_ref, bc_act_ref, local_ref, gate_ref, gain_ref, weight_ref, share_ref):
    low_lanes = lax.broadcasted_iota(jnp.int32, (HEAD, 128), 1) < HEAD
    pairs = []
    for pair in range(HEADS // 2):
        even = state_ref[2 * pair].astype(f32)
        odd = state_ref[2 * pair + 1].astype(f32)
        top = jnp.where(low_lanes, even, pltpu.roll(odd, HEAD, 1))
        bottom = jnp.where(low_lanes, pltpu.roll(even, HEAD, 1), odd)
        pairs.append(jnp.concatenate([top, bottom], axis=0).astype(bf16))
    states = jnp.concatenate(pairs, axis=1)
    carried = dot(bc_act_ref[:, STATE:], states)
    gated = local_ref[...] + gate_ref[...] * carried
    squares = jnp.sum(gated * gated, axis=1, keepdims=True)
    scaled = (gated * gain_ref[...]).astype(bf16)
    wide = jnp.broadcast_to(squares, (LENGTH, 128))
    row_at = lax.broadcasted_iota(jnp.int32, (EXTRA, 128), 0)
    extra = jnp.zeros((EXTRA, 128), f32)
    for block in range(LENGTH // BLOCK):
        row = wide[block * BLOCK : (block + 1) * BLOCK].T[0:1]
        for k, part in enumerate(parts3(row)):
            extra = jnp.where(row_at == 3 * block + k, part.astype(f32), extra)
    extra = extra.astype(bf16)
    for pair in range(SHARES // 2):
        product = dot(scaled, weight_ref[:, 256 * pair : 256 * (pair + 1)]).astype(bf16)
        share_ref[2 * pair, 0:LENGTH] = product[:, :128]
        share_ref[2 * pair, LENGTH:] = extra
        share_ref[2 * pair + 1, 0:LENGTH] = product[:, 128:]
        share_ref[2 * pair + 1, LENGTH:] = extra


def sum_kernel(share_ref, out_ref):
    total = share_ref[0].astype(f32)
    for d in range(1, SHARES):
        total = total + share_ref[d].astype(f32)
    extra = total[LENGTH:]
    for block in range(LENGTH // BLOCK):
        rows = slice(block * BLOCK, (block + 1) * BLOCK)
        squares = extra[3 * block : 3 * block + 1] + (
            extra[3 * block + 1 : 3 * block + 2] + extra[3 * block + 2 : 3 * block + 3]
        )
        scale = lax.rsqrt(squares / INNER + 1e-05)
        column = jnp.broadcast_to(scale, (128, 128)).T
        out_ref[rows] = (total[rows] * column).astype(bf16)


HERE = pl.BlockSpec(memory_space=pltpu.VMEM)
SCALARS = pl.BlockSpec(memory_space=pltpu.SMEM)
THERE = pl.BlockSpec(memory_space=pltpu.HBM)


def stay(a):
    return pltpu.with_memory_space_constraint(a, pltpu.HBM)


def call(kernel, outs, *args, specs=None, scratch=(), flops=1e8, transcendentals=0):
    return pl.pallas_call(
        kernel,
        out_shape=[jax.ShapeDtypeStruct(s, d) for s, d in outs],
        in_specs=specs or [HERE] * len(args),
        out_specs=[HERE] * len(outs),
        scratch_shapes=list(scratch),
        compiler_params=pltpu.CompilerParams(vmem_limit_bytes=32 * 1024 * 1024),
        cost_estimate=pl.CostEstimate(
            flops=int(flops), bytes_accessed=2_000_000, transcendentals=int(transcendentals)
        ),
    )(*(stay(a) if spec is THERE else a for a, spec in zip(args, specs or [HERE] * len(args))))


def shards(
    inner_x, gate_z, bc_input, conv_inner, conv_bc, step_size, log_decay, skip_gain, norm_gain, out_weight
):
    tail = jnp.concatenate([inner_x[LENGTH - 16 :], bc_input[LENGTH - 16 :]], axis=1)
    halo = lax.ppermute(tail, "seq", [(i, i + 1) for i in range(BLOCKS - 1)])
    message, act, bc_act, cum = call(
        summary_kernel,
        [((HEADS, HEAD + EXTRA, 128), bf16), ((LENGTH, WIDTH), bf16), ((LENGTH, 2 * STATE), bf16), ((HEADS, LENGTH), f32)],
        inner_x, bc_input, halo, conv_inner, conv_bc, step_size, log_decay,
        specs=[THERE, THERE, HERE, THERE, THERE, THERE, THERE],
        scratch=[
            pltpu.VMEM((LENGTH + 8, WIDTH), f32), pltpu.VMEM((LENGTH + 8, 2 * STATE), f32),
            pltpu.VMEM((LENGTH, WIDTH), bf16), pltpu.VMEM((LENGTH, 2 * STATE), bf16),
            pltpu.VMEM((4, WIDTH), f32), pltpu.VMEM((4, 2 * STATE), f32),
            pltpu.VMEM((HEADS, LENGTH), f32), pltpu.VMEM((HEADS, LENGTH), f32),
            pltpu.SemaphoreType.DMA((6,)),
        ],
    )
    groups = [list(range(i, i + GROUP)) for i in range(0, BLOCKS, GROUP)]
    message = lax.all_to_all(message, "seq", 0, 0, tiled=True, axis_index_groups=groups)
    prefix, scale, total = call(
        prefix_kernel,
        [((GROUP, HEAD, 128), f32), ((GROUP, 8, 128), f32), ((HEAD + EXTRA, 128), bf16)],
        message,
    )
    local, gate, gain = call(
        within_kernel,
        [((LENGTH, WIDTH), f32), ((LENGTH, WIDTH), f32), ((1, WIDTH), f32)],
        act, bc_act, cum, step_size, skip_gain, gate_z, norm_gain[None, :],
        specs=[HERE, HERE, HERE, THERE, SCALARS, THERE, THERE],
        scratch=[pltpu.VMEM((HEADS, LENGTH), f32), pltpu.VMEM((LENGTH, WIDTH), bf16), pltpu.SemaphoreType.DMA((3,))],
        flops=2e9, transcendentals=1.2e6,
    )

    def later(distance):
        return lax.ppermute(total, "seq", [(i, i + distance) for i in range(BLOCKS - distance)])

    far, near, after = later(3 * GROUP), later(GROUP), later(2 * GROUP)
    (state,) = call(entering_kernel, [((GROUP, HEAD, 128), bf16)], prefix, scale, far, near, after)
    state = lax.all_to_all(state, "seq", 0, 0, tiled=True, axis_index_groups=groups)
    (share,) = call(
        output_kernel,
        [((SHARES, LENGTH + EXTRA, 128), bf16)],
        state, bc_act, local, gate, gain, out_weight,
        flops=9e8,
    )
    share = lax.all_to_all(share, "tp", 0, 0, tiled=True)
    (mixed,) = call(sum_kernel, [((LENGTH, 128), bf16)], share)
    return mixed


def solution(mesh):
    in_specs = (
        P("seq", "tp"),
        P("seq", "tp"),
        P("seq", None),
        P(None, "tp"),
        P(),
        P("tp", "seq"),
        P("tp", "seq"),
        P("tp"),
        P("tp"),
        P("tp", None),
    )
    return jax.shard_map(shards, mesh=mesh, in_specs=in_specs, out_specs=P("seq", "tp"), check_vma=False)
```

```python
import jax
import jax.numpy as jnp
from jax import lax
from jax.experimental import pallas as pl
from jax.experimental.pallas import tpu as pltpu
from jax.sharding import PartitionSpec as P

INNER = 8192
HEADS = 8
HEAD = 64
WIDTH = HEADS * HEAD
STATE = 128
LENGTH = 384
BLOCK = 128
BLOCKS = 32
GROUP = 8
SHARES = 16
EDGE = 3
EXTRA = 16

f32 = jnp.float32
bf16 = jnp.bfloat16


def parts3(a):
    high = a.astype(bf16)
    rest = a - high.astype(f32)
    middle = rest.astype(bf16)
    low = (rest - middle.astype(f32)).astype(bf16)
    return high, middle, low


def silu(a):
    return a * jax.nn.sigmoid(a)


def dot(a, b):
    return lax.dot_general(a, b, (((1,), (0,)), ((), ())), preferred_element_type=f32)


def columns_of(rows):
    padded = jnp.concatenate([rows, jnp.zeros((128 - rows.shape[0], LENGTH), f32)], axis=0)
    return padded.T


def spread_heads(columns):
    head = lax.broadcasted_iota(jnp.int32, (128, WIDTH), 0)
    channel = lax.broadcasted_iota(jnp.int32, (128, WIDTH), 1)
    chosen = jnp.where(channel // HEAD == head, 1.0, 0.0).astype(bf16)
    high, middle, low = parts3(columns)
    return dot(high, chosen) + (dot(middle, chosen) + dot(low, chosen))


def rolled(a, distance, axis):
    return pltpu.roll(a, distance % a.shape[axis], axis)


def iota(shape, axis):
    return lax.broadcasted_iota(jnp.int32, shape, axis)


def before_taps(ext, weights):
    total = weights[0:1] * ext[5 : 5 + LENGTH]
    for k in range(1, 4):
        total = total + weights[k : k + 1] * ext[5 + k : 5 + k + LENGTH]
    return total


def earlier_taps(last, taps):
    total = taps[0] * last + taps[1] * rolled(last, -1, 0) + taps[2] * rolled(last, -2, 0)
    return jnp.where(iota(last.shape, 0) < EDGE, total, 0.0)


def own_taps(first, taps):
    return taps[3] * first + taps[2] * rolled(first, 1, 0) + taps[1] * rolled(first, 2, 0)


def rounded(a):
    return a.astype(bf16).astype(f32)


def fetch(pairs, sems):
    copies = [pltpu.make_async_copy(there, here, sems.at[i]) for i, (there, here) in enumerate(pairs)]
    for copy in copies:
        copy.start()
    return copies


def summary_kernel(
    x_at, bc_at, cx_at, cbc_at, step_at, decay_at,
    message_ref, act_ref, bc_act_ref, cum_ref, first_x_ref, first_bc_ref, taps_x_ref, taps_bc_ref,
    ext_x, ext_bc, x_ref, bc_ref, step_ref, decay_ref, sems,
):
    for copy in fetch(
        [
            (decay_at, decay_ref), (step_at, step_ref), (cx_at, taps_x_ref),
            (cbc_at, taps_bc_ref), (bc_at, bc_ref), (x_at, x_ref),
        ],
        sems,
    ):
        copy.wait()
    ext_x[0:8] = jnp.zeros((8, WIDTH), f32)
    ext_bc[0:8] = jnp.zeros((8, 2 * STATE), f32)
    ext_x[8:] = x_ref[...].astype(f32)
    ext_bc[8:] = bc_ref[...].astype(f32)
    sums = before_taps(ext_bc, taps_bc_ref)
    first_bc_ref[...] = sums[0:8]
    bc_act = silu(sums).astype(bf16)
    bc_act_ref[...] = bc_act
    sums = before_taps(ext_x, taps_x_ref)
    first_x_ref[...] = sums[0:8]
    act = silu(sums).astype(bf16)
    act_ref[...] = act

    upto = jnp.where(iota((LENGTH, LENGTH), 0) <= iota((LENGTH, LENGTH), 1), 1.0, 0.0).astype(bf16)
    high, middle, low = parts3(decay_ref[...])
    cum = dot(high, upto) + (dot(middle, upto) + dot(low, upto))
    cum_ref[...] = cum
    last = cum[:, LENGTH - 1 : LENGTH]
    factor = step_ref[...] * jnp.exp(last - cum)
    inside = jnp.where(iota((HEADS, LENGTH), 1) < EDGE, 0.0, factor)
    weighted = (act.astype(f32) * spread_heads(columns_of(inside))).astype(bf16)
    b_rows = bc_act[:, :STATE].astype(f32)
    summary = dot(b_rows.T.astype(bf16), weighted)

    total = jnp.broadcast_to(jnp.exp(last), (HEADS, 128))
    scalars = jnp.where(iota((HEADS, 128), 1) < HEAD, factor[:, :128], total)
    high, middle, _ = (p.astype(f32) for p in parts3(scalars))
    tap_high, tap_middle, _ = (p.astype(f32) for p in parts3(taps_x_ref[...]))
    low_lanes = iota((HEAD, 128), 1) < HEAD
    few = iota((8, 128), 1) < HEAD
    row = iota((8, 128), 0)
    b_first = rolled(ext_bc[8:16, :STATE], 3, 0)
    bc_last = rolled(ext_bc[LENGTH : LENGTH + 8], 3, 0)
    for h in range(HEADS):
        lanes = slice(128 * (h // 2), 128 * (h // 2 + 1))
        even = h % 2 == 0

        def side_by_side(left, right, where):
            if even:
                return jnp.where(where, left, rolled(right, HEAD, 1))
            return jnp.where(where, rolled(left, HEAD, 1), right)

        message_ref[h, 0:HEAD] = side_by_side(summary[:HEAD, lanes], summary[HEAD:, lanes], low_lanes).astype(bf16)
        x_edges = side_by_side(ext_x[8:16, lanes], rolled(ext_x[LENGTH : LENGTH + 8, lanes], 3, 0), few)
        tile = jnp.where(row < 3, x_edges, b_first)
        tile = jnp.where(row == 6, high[h : h + 1], jnp.where(row == 7, middle[h : h + 1], tile))
        other = bc_last[:, :STATE]
        for at, (part, k) in enumerate(((tap_high, 0), (tap_high, 2), (tap_middle, 0), (tap_middle, 2))):
            pair = side_by_side(part[k : k + 1, lanes], part[k + 1 : k + 2, lanes], few[0:1])
            other = jnp.where(row == 3 + at, pair, other)
        c_row = bc_last[h : h + 1, STATE:] if h < EDGE else jnp.zeros((1, STATE), f32)
        other = jnp.where(row == 7, c_row, other)
        message_ref[h, HEAD:] = jnp.concatenate([tile, other], axis=0).astype(bf16)


def within_kernel(
    act_ref, bc_act_ref, cum_ref, step_at, skip_ref, z_at, gain_at, after_ref,
    local_ref, gate_ref, gain_ref, lead_ref, gate_first_ref,
    step_ref, z_ref, sems,
):
    for copy in fetch([(step_at, step_ref), (z_at, z_ref), (gain_at, gain_ref)], sems):
        copy.wait()
    head_at = lax.broadcasted_iota(jnp.int32, (1, WIDTH), 1) // HEAD
    skip = jnp.zeros((1, WIDTH), f32)
    for h in range(HEADS):
        skip = jnp.where(head_at == h, skip_ref[h], skip)
    cum = cum_ref[...]
    cum_columns = columns_of(cum)
    act = act_ref[...].astype(f32)
    step = step_ref[...]
    inside = jnp.where(iota((HEADS, LENGTH), 1) < EDGE, 0.0, step)
    scaled = (act * spread_heads(columns_of(inside))).astype(bf16)
    lead_ref[...] = spread_heads(columns_of(step)[0:8] * jnp.exp(-cum_columns[0:8]))
    gate = silu(z_ref[...].astype(f32))
    gate_first_ref[...] = gate[0:8] * skip
    gate_ref[...] = gate * spread_heads(jnp.exp(cum_columns))
    b_rows = bc_act_ref[:, :STATE]
    c_rows = bc_act_ref[:, STATE:]
    skipped = jnp.where(iota((LENGTH, WIDTH), 0) < EDGE, 0.0, skip * act)
    t_at = lax.broadcasted_iota(jnp.int32, (BLOCK, BLOCK), 0)
    s_at = lax.broadcasted_iota(jnp.int32, (BLOCK, BLOCK), 1)
    causal = t_at >= s_at
    low_lanes = lax.broadcasted_iota(jnp.int32, (BLOCK, 128), 1) < HEAD
    for block in range(LENGTH // BLOCK):
        rows = slice(block * BLOCK, (block + 1) * BLOCK)
        scores = lax.dot_general(
            c_rows[rows], b_rows[: (block + 1) * BLOCK], (((1,), (1,)), ((), ())), preferred_element_type=f32
        )
        for pair in range(HEADS // 2):
            lanes = slice(128 * pair, 128 * (pair + 1))
            sums = []
            for h in (2 * pair, 2 * pair + 1):
                here = cum_columns[rows, h : h + 1]
                tiles = []
                for other in range(block + 1):
                    columns = slice(other * BLOCK, (other + 1) * BLOCK)
                    spread = here - cum[h : h + 1, columns]
                    if other == block:
                        spread = jnp.where(causal, spread, -jnp.inf)
                    tiles.append((scores[:, columns] * jnp.exp(spread)).astype(bf16))
                mixing = tiles[0] if block == 0 else jnp.concatenate(tiles, axis=1)
                sums.append(dot(mixing, scaled[: (block + 1) * BLOCK, lanes]))
            within = jnp.where(low_lanes, sums[0], sums[1])
            local_ref[rows, lanes] = (within + skipped[rows, lanes]) * gate[rows, lanes]


def all_lanes(row):
    return jnp.where(iota((1, 128), 1) < HEAD, rolled(row, HEAD, 1), row)


def taps_of(tile):
    pairs = tile[3:5] + tile[5:7]
    return [pairs[0:1], rolled(pairs[0:1], HEAD, 1), pairs[1:2], rolled(pairs[1:2], HEAD, 1)]


def edge_rows(tile, before, before_last, scalars, taps_x, taps_b):
    row = iota((8, 128), 0)
    lane = iota((8, 128), 1)
    sums = own_taps(jnp.where(row < EDGE, tile, 0.0), taps_x)
    sums_b = own_taps(jnp.where(row < EDGE, rolled(tile, -EDGE, 0), 0.0), taps_b)
    if before is not None:
        sums = sums + earlier_taps(jnp.where(row < EDGE, rolled(before, HEAD, 1), 0.0), taps_x)
        sums_b = sums_b + earlier_taps(jnp.where(row < EDGE, before_last, 0.0), taps_b)
    factor = jnp.sum(jnp.where(lane == row, scalars, 0.0), axis=1, keepdims=True)
    weighted = rounded(silu(sums)) * factor
    weighted = jnp.where((row < EDGE) & (lane < HEAD), weighted, 0.0)
    return weighted, jnp.where(row < EDGE, rounded(silu(sums_b)), 0.0)


def edge_states(entries):
    zeros = jnp.zeros((HEAD - 8 * len(entries), 128), f32)
    pad = [zeros] if zeros.shape[0] else []
    weighted = jnp.concatenate([e[0] for e in entries] + pad, axis=0)
    weighted = jnp.concatenate([weighted, rolled(weighted, HEAD, 1)], axis=0)
    b_rows = jnp.concatenate([e[1] for e in entries] + pad + [jnp.zeros((HEAD, 128), f32)], axis=0).T
    left = jnp.where(iota((HEAD, 128), 1) < HEAD, b_rows[:HEAD], rolled(b_rows[HEAD:], HEAD, 1)).astype(bf16)
    owner = (iota((128, 128), 0) % HEAD) // 8
    return [dot(left, jnp.where(owner == e, weighted, 0.0).astype(bf16)) for e in range(len(entries))]


def prefix_kernel(message_ref, taps_ref, prefix_ref, scale_ref, total_ref):
    tiles = [message_ref[m, HEAD:].astype(f32) for m in range(GROUP)]
    scalars = [t[6:7] + t[7:8] for t in tiles]
    decays = [all_lanes(s) for s in scalars]
    taps_x = taps_of(tiles[0][8:])
    taps_b = [taps_ref[k : k + 1, :STATE] for k in range(4)]
    entries = [
        edge_rows(tiles[m][:8], tiles[m - 1][:8], tiles[m - 1][8:], scalars[m], taps_x, taps_b) for m in range(1, GROUP)
    ]
    edges = edge_states(entries)
    state = message_ref[0, 0:HEAD].astype(f32)
    scale = jnp.ones((1, 128), f32)
    for m in range(1, GROUP):
        prefix_ref[m] = state
        scale_ref[m] = jnp.broadcast_to(scale, (8, 128))
        state = decays[m] * state + (message_ref[m, 0:HEAD].astype(f32) + edges[m - 1])
        scale = decays[m] * scale
    total_ref[0:HEAD] = state.astype(bf16)
    lane = iota((1, 128), 1)
    high, middle, _ = (p.astype(f32) for p in parts3(jnp.where(lane < HEAD, scalars[0] * scale, decays[0] * scale)))
    row = iota((8, 128), 0)
    first, last = tiles[0][:8], tiles[GROUP - 1]
    tile = jnp.where((row < EDGE) & (iota((8, 128), 1) >= HEAD), last[:8], first)
    tile = jnp.where(row == 6, high, jnp.where(row == 7, middle, tile))
    total_ref[HEAD:] = jnp.concatenate([tile, last[8:]], axis=0).astype(bf16)


def entering_kernel(gain_ref, message_ref, taps_ref, prefix_ref, scale_ref, far_ref, near_ref, next_ref, state_ref):
    own = message_ref[0, HEAD:].astype(f32)
    taps_x = taps_of(own[8:])
    taps_b = [taps_ref[k : k + 1, :STATE] for k in range(4)]
    refs = [far_ref, next_ref, near_ref]
    tiles = [r[HEAD:].astype(f32) for r in refs] + [own]
    scalars = [t[6:7] + t[7:8] for t in tiles]
    entries = [edge_rows(tiles[0][:8], None, None, scalars[0], taps_x, taps_b)]
    for e in range(1, 4):
        entries.append(edge_rows(tiles[e][:8], tiles[e - 1][:8], tiles[e - 1][8:], scalars[e], taps_x, taps_b))
    edges = edge_states(entries)
    entering = far_ref[0:HEAD].astype(f32) + edges[0]
    for e in range(1, 3):
        entering = all_lanes(scalars[e]) * entering + (refs[e][0:HEAD].astype(f32) + edges[e])
    state_ref[0, 0:HEAD] = entering.astype(bf16)
    state_ref[0, HEAD:] = near_ref[HEAD:]
    after_first = all_lanes(scalars[3]) * entering + edges[3]
    for m in range(1, GROUP):
        state_ref[m, 0:HEAD] = (prefix_ref[m] + scale_ref[m, 0:1] * after_first).astype(bf16)
        state_ref[m, HEAD:] = message_ref[m - 1, HEAD:]


def output_kernel(
    state_ref, bc_act_ref, first_x_ref, first_bc_ref, taps_x_ref, taps_bc_ref, lead_ref, gate_first_ref,
    local_ref, gate_ref, gain_ref, weight_ref, share_ref,
):
    row = iota((8, 128), 0)
    few = iota((8, 128), 1) < HEAD
    low_lanes = iota((HEAD, 128), 1) < HEAD
    tiles = [state_ref[h, HEAD:].astype(f32) for h in range(HEADS)]

    last_x = jnp.concatenate(
        [jnp.where(few, rolled(tiles[h][:8], HEAD, 1), tiles[h + 1][:8]) for h in range(0, HEADS, 2)], axis=1
    )
    last_c = jnp.zeros((8, 128), f32)
    for h in range(EDGE):
        last_c = jnp.where(row == h, tiles[h][15:16], last_c)
    last_bc = jnp.concatenate([tiles[0][8:], last_c], axis=1)
    last_x = jnp.where(iota((8, WIDTH), 0) < EDGE, last_x, 0.0)
    last_bc = jnp.where(iota((8, 2 * STATE), 0) < EDGE, last_bc, 0.0)
    taps_x = [taps_x_ref[k : k + 1] for k in range(4)]
    taps_bc = [taps_bc_ref[k : k + 1] for k in range(4)]
    act = rounded(silu(first_x_ref[...] + earlier_taps(last_x, taps_x)))
    bc_act = rounded(silu(first_bc_ref[...] + earlier_taps(last_bc, taps_bc)))
    b_first, c_first = bc_act[:, :STATE], bc_act[:, STATE:]
    lead = rounded(jnp.where(iota((8, WIDTH), 0) < EDGE, act * lead_ref[...], 0.0))

    pairs = []
    for pair in range(HEADS // 2):
        even = state_ref[2 * pair, 0:HEAD].astype(f32)
        odd = state_ref[2 * pair + 1, 0:HEAD].astype(f32)
        top = jnp.where(low_lanes, even, rolled(odd, HEAD, 1))
        bottom = jnp.where(low_lanes, rolled(even, HEAD, 1), odd)
        pairs.append(jnp.concatenate([top, bottom], axis=0))
    states = jnp.concatenate(pairs, axis=1)
    b_columns = jnp.concatenate([b_first, jnp.zeros((120, STATE), f32)], axis=0).T.astype(bf16)
    lead_rows = jnp.concatenate([lead, jnp.zeros((120, WIDTH), f32)], axis=0).astype(bf16)
    states = (states + dot(b_columns, lead_rows)).astype(bf16)
    c_rows = jnp.concatenate([c_first, bc_act_ref[:, STATE:].astype(f32)[8:]], axis=0).astype(bf16)
    gated = local_ref[...] + gate_ref[...] * dot(c_rows, states)
    ahead = jnp.zeros((8, WIDTH), f32)
    for s in range(1, EDGE):
        score = jnp.sum(c_first * b_first[s : s + 1], axis=1, keepdims=True)
        ahead = ahead + jnp.where(iota((8, WIDTH), 0) < s, score * lead[s : s + 1], 0.0)
    skipped = jnp.where(iota((8, WIDTH), 0) < EDGE, gate_first_ref[...] * act, 0.0)
    gated = jnp.concatenate([gated[0:8] + (skipped - gate_ref[0:8] * ahead), gated[8:]], axis=0)

    squares = jnp.sum(gated * gated, axis=1, keepdims=True)
    scaled = (gated * gain_ref[...]).astype(bf16)
    wide = jnp.broadcast_to(squares, (LENGTH, 128))
    row_at = lax.broadcasted_iota(jnp.int32, (EXTRA, 128), 0)
    extra = jnp.zeros((EXTRA, 128), f32)
    for block in range(LENGTH // BLOCK):
        row = wide[block * BLOCK : (block + 1) * BLOCK].T[0:1]
        for k, part in enumerate(parts3(row)):
            extra = jnp.where(row_at == 3 * block + k, part.astype(f32), extra)
    extra = extra.astype(bf16)
    for pair in range(SHARES // 2):
        product = dot(scaled, weight_ref[:, 256 * pair : 256 * (pair + 1)]).astype(bf16)
        share_ref[2 * pair, 0:LENGTH] = product[:, :128]
        share_ref[2 * pair, LENGTH:] = extra
        share_ref[2 * pair + 1, 0:LENGTH] = product[:, 128:]
        share_ref[2 * pair + 1, LENGTH:] = extra


def sum_kernel(share_ref, out_ref):
    total = share_ref[0].astype(f32)
    for d in range(1, SHARES):
        total = total + share_ref[d].astype(f32)
    extra = total[LENGTH:]
    for block in range(LENGTH // BLOCK):
        rows = slice(block * BLOCK, (block + 1) * BLOCK)
        squares = extra[3 * block : 3 * block + 1] + (
            extra[3 * block + 1 : 3 * block + 2] + extra[3 * block + 2 : 3 * block + 3]
        )
        scale = lax.rsqrt(squares / INNER + 1e-05)
        column = jnp.broadcast_to(scale, (128, 128)).T
        out_ref[rows] = (total[rows] * column).astype(bf16)


HERE = pl.BlockSpec(memory_space=pltpu.VMEM)
SCALARS = pl.BlockSpec(memory_space=pltpu.SMEM)
THERE = pl.BlockSpec(memory_space=pltpu.HBM)


def stay(a):
    return pltpu.with_memory_space_constraint(a, pltpu.HBM)


def call(kernel, outs, *args, specs=None, scratch=(), flops=1e8, transcendentals=0):
    return pl.pallas_call(
        kernel,
        out_shape=[jax.ShapeDtypeStruct(s, d) for s, d in outs],
        in_specs=specs or [HERE] * len(args),
        out_specs=[HERE] * len(outs),
        scratch_shapes=list(scratch),
        compiler_params=pltpu.CompilerParams(vmem_limit_bytes=32 * 1024 * 1024),
        cost_estimate=pl.CostEstimate(
            flops=int(flops), bytes_accessed=2_000_000, transcendentals=int(transcendentals)
        ),
    )(*(stay(a) if spec is THERE else a for a, spec in zip(args, specs or [HERE] * len(args))))


def shards(
    inner_x, gate_z, bc_input, conv_inner, conv_bc, step_size, log_decay, skip_gain, norm_gain, out_weight
):
    message, act, bc_act, cum, first_x, first_bc, taps_x, taps_bc = call(
        summary_kernel,
        [
            ((HEADS, HEAD + EXTRA, 128), bf16), ((LENGTH, WIDTH), bf16), ((LENGTH, 2 * STATE), bf16),
            ((HEADS, LENGTH), f32), ((8, WIDTH), f32), ((8, 2 * STATE), f32), ((4, WIDTH), f32), ((4, 2 * STATE), f32),
        ],
        inner_x, bc_input, conv_inner, conv_bc, step_size, log_decay,
        specs=[THERE] * 6,
        scratch=[
            pltpu.VMEM((LENGTH + 8, WIDTH), f32), pltpu.VMEM((LENGTH + 8, 2 * STATE), f32),
            pltpu.VMEM((LENGTH, WIDTH), bf16), pltpu.VMEM((LENGTH, 2 * STATE), bf16),
            pltpu.VMEM((HEADS, LENGTH), f32), pltpu.VMEM((HEADS, LENGTH), f32),
            pltpu.SemaphoreType.DMA((6,)),
        ],
    )
    groups = [list(range(i, i + GROUP)) for i in range(0, BLOCKS, GROUP)]
    message = lax.all_to_all(message, "seq", 0, 0, tiled=True, axis_index_groups=groups)
    prefix, scale, total = call(
        prefix_kernel,
        [((GROUP, HEAD, 128), f32), ((GROUP, 8, 128), f32), ((HEAD + EXTRA, 128), bf16)],
        message, taps_bc,
    )
    local, gate, gain, lead, gate_first = call(
        within_kernel,
        [((LENGTH, WIDTH), f32), ((LENGTH, WIDTH), f32), ((1, WIDTH), f32), ((8, WIDTH), f32), ((8, WIDTH), f32)],
        act, bc_act, cum, step_size, skip_gain, gate_z, norm_gain[None, :], total,
        specs=[HERE, HERE, HERE, THERE, SCALARS, THERE, THERE, HERE],
        scratch=[pltpu.VMEM((HEADS, LENGTH), f32), pltpu.VMEM((LENGTH, WIDTH), bf16), pltpu.SemaphoreType.DMA((3,))],
        flops=2e9, transcendentals=1.2e6,
    )

    def later(distance):
        return lax.ppermute(total, "seq", [(i, i + distance) for i in range(BLOCKS - distance)])

    far, near, after = later(3 * GROUP), later(GROUP), later(2 * GROUP)
    (state,) = call(
        entering_kernel,
        [((GROUP, HEAD + EXTRA, 128), bf16)],
        gain, message, taps_bc, prefix, scale, far, near, after,
    )
    state = lax.all_to_all(state, "seq", 0, 0, tiled=True, axis_index_groups=groups)
    (share,) = call(
        output_kernel,
        [((SHARES, LENGTH + EXTRA, 128), bf16)],
        state, bc_act, first_x, first_bc, taps_x, taps_bc, lead, gate_first, local, gate, gain, out_weight,
        flops=9e8,
    )
    share = lax.all_to_all(share, "tp", 0, 0, tiled=True)
    (mixed,) = call(sum_kernel, [((LENGTH, 128), bf16)], share)
    return mixed


def solution(mesh):
    in_specs = (
        P("seq", "tp"),
        P("seq", "tp"),
        P("seq", None),
        P(None, "tp"),
        P(),
        P("tp", "seq"),
        P("tp", "seq"),
        P("tp"),
        P("tp"),
        P("tp", None),
    )
    return jax.shard_map(shards, mesh=mesh, in_specs=in_specs, out_specs=P("seq", "tp"), check_vma=False)
```

```python
import jax
import jax.numpy as jnp
from jax import lax
from jax.experimental import pallas as pl
from jax.experimental.pallas import tpu as pltpu
from jax.sharding import PartitionSpec as P

INNER = 8192
HEADS = 8
HEAD = 64
WIDTH = HEADS * HEAD
STATE = 128
LENGTH = 384
BLOCK = 128
BLOCKS = 32
GROUP = 8
SHARES = 16
EDGE = 3
EXTRA = 16

f32 = jnp.float32
bf16 = jnp.bfloat16


def parts3(a):
    high = a.astype(bf16)
    rest = a - high.astype(f32)
    middle = rest.astype(bf16)
    low = (rest - middle.astype(f32)).astype(bf16)
    return high, middle, low


def silu(a):
    return a * jax.nn.sigmoid(a)


def dot(a, b):
    return lax.dot_general(a, b, (((1,), (0,)), ((), ())), preferred_element_type=f32)


def columns_of(rows):
    padded = jnp.concatenate([rows, jnp.zeros((128 - rows.shape[0], rows.shape[1]), f32)], axis=0)
    return padded.T


def part_columns(rows):
    return columns_of(jnp.concatenate([p.astype(f32) for p in parts3(rows)], axis=0)).astype(bf16)


def spread_heads(columns):
    part = iota((128, WIDTH), 0)
    chosen = (part < 3 * HEADS) & (part % HEADS == iota((128, WIDTH), 1) // HEAD)
    return dot(columns, jnp.where(chosen, 1.0, 0.0).astype(bf16))


def rolled(a, distance, axis):
    return pltpu.roll(a, distance % a.shape[axis], axis)


def iota(shape, axis):
    return lax.broadcasted_iota(jnp.int32, shape, axis)


def before_taps(ext, weights):
    total = weights[0:1] * ext[5 : 5 + LENGTH]
    for k in range(1, 4):
        total = total + weights[k : k + 1] * ext[5 + k : 5 + k + LENGTH]
    return total


def earlier_taps(last, taps):
    total = taps[0] * last + taps[1] * rolled(last, -1, 0) + taps[2] * rolled(last, -2, 0)
    return jnp.where(iota(last.shape, 0) < EDGE, total, 0.0)


def own_taps(first, taps):
    return taps[3] * first + taps[2] * rolled(first, 1, 0) + taps[1] * rolled(first, 2, 0)


def rounded(a):
    return a.astype(bf16).astype(f32)


def fetch(pairs, sems):
    copies = [pltpu.make_async_copy(there, here, sems.at[i]) for i, (there, here) in enumerate(pairs)]
    for copy in copies:
        copy.start()
    return copies


def summary_kernel(
    x_at, bc_at, cx_at, cbc_at, step_at, decay_at,
    message_ref, act_ref, bc_act_ref, cum_ref, first_x_ref, first_bc_ref, taps_x_ref, taps_bc_ref,
    ext_x, ext_bc, x_ref, bc_ref, step_ref, decay_ref, sems,
):
    copies = fetch(
        [
            (decay_at, decay_ref), (step_at, step_ref), (cx_at, taps_x_ref),
            (cbc_at, taps_bc_ref), (bc_at, bc_ref), (x_at, x_ref),
        ],
        sems,
    )
    copies[0].wait()
    copies[1].wait()
    upto = jnp.where(iota((LENGTH, LENGTH), 0) <= iota((LENGTH, LENGTH), 1), 1.0, 0.0).astype(bf16)
    sums = dot(jnp.concatenate([p.astype(f32) for p in parts3(decay_ref[...])], axis=0).astype(bf16), upto)
    cum = sums[0:8] + (sums[8:16] + sums[16:24])
    cum_ref[...] = cum
    last = cum[:, LENGTH - 1 : LENGTH]
    factor = step_ref[...] * jnp.exp(last - cum)
    inside = jnp.where(iota((HEADS, LENGTH), 1) < EDGE, 0.0, factor)
    factor_spread = spread_heads(part_columns(inside))
    for copy in copies[2:]:
        copy.wait()
    ext_x[0:8] = jnp.zeros((8, WIDTH), f32)
    ext_bc[0:8] = jnp.zeros((8, 2 * STATE), f32)
    ext_x[8:] = x_ref[...].astype(f32)
    ext_bc[8:] = bc_ref[...].astype(f32)
    sums = before_taps(ext_bc, taps_bc_ref)
    first_bc_ref[...] = sums[0:8]
    bc_act = silu(sums).astype(bf16)
    bc_act_ref[...] = bc_act
    sums = before_taps(ext_x, taps_x_ref)
    first_x_ref[...] = sums[0:8]
    act = silu(sums).astype(bf16)
    act_ref[...] = act

    weighted = (act.astype(f32) * factor_spread).astype(bf16)
    b_rows = bc_act[:, :STATE].astype(f32)
    summary = dot(b_rows.T.astype(bf16), weighted)

    total = jnp.broadcast_to(jnp.exp(last), (HEADS, 128))
    scalars = jnp.where(iota((HEADS, 128), 1) < HEAD, factor[:, :128], total)
    high, middle, _ = (p.astype(f32) for p in parts3(scalars))
    tap_high, tap_middle, _ = (p.astype(f32) for p in parts3(taps_x_ref[...]))
    low_lanes = iota((HEAD, 128), 1) < HEAD
    few = iota((8, 128), 1) < HEAD
    row = iota((8, 128), 0)
    b_first = rolled(ext_bc[8:16, :STATE], 3, 0)
    bc_last = rolled(ext_bc[LENGTH : LENGTH + 8], 3, 0)
    for h in range(HEADS):
        lanes = slice(128 * (h // 2), 128 * (h // 2 + 1))
        even = h % 2 == 0

        def side_by_side(left, right, where):
            if even:
                return jnp.where(where, left, rolled(right, HEAD, 1))
            return jnp.where(where, rolled(left, HEAD, 1), right)

        message_ref[h, 0:HEAD] = side_by_side(summary[:HEAD, lanes], summary[HEAD:, lanes], low_lanes).astype(bf16)
        x_edges = side_by_side(ext_x[8:16, lanes], rolled(ext_x[LENGTH : LENGTH + 8, lanes], 3, 0), few)
        tile = jnp.where(row < 3, x_edges, b_first)
        tile = jnp.where(row == 6, high[h : h + 1], jnp.where(row == 7, middle[h : h + 1], tile))
        other = bc_last[:, :STATE]
        for at, (part, k) in enumerate(((tap_high, 0), (tap_high, 2), (tap_middle, 0), (tap_middle, 2))):
            pair = side_by_side(part[k : k + 1, lanes], part[k + 1 : k + 2, lanes], few[0:1])
            other = jnp.where(row == 3 + at, pair, other)
        c_row = bc_last[h : h + 1, STATE:] if h < EDGE else jnp.zeros((1, STATE), f32)
        other = jnp.where(row == 7, c_row, other)
        message_ref[h, HEAD:] = jnp.concatenate([tile, other], axis=0).astype(bf16)


def within_kernel(
    act_ref, bc_act_ref, cum_ref, step_at, skip_at, z_at, gain_at, after_ref,
    local_ref, gate_ref, gain_ref, lead_ref, gate_first_ref,
    step_ref, z_ref, skip_ref, sems,
):
    copies = fetch([(step_at, step_ref), (skip_at, skip_ref), (gain_at, gain_ref), (z_at, z_ref)], sems)
    copies[0].wait()
    copies[1].wait()
    head_at = iota((1, WIDTH), 1) // HEAD
    skip = jnp.zeros((1, WIDTH), f32)
    for h in range(HEADS):
        skip = jnp.where(head_at == h, skip_ref[h], skip)
    cum = cum_ref[...]
    cum_columns = columns_of(cum)
    act = act_ref[...].astype(f32)
    step = step_ref[...]
    inside = jnp.where(iota((HEADS, LENGTH), 1) < EDGE, 0.0, step)
    scaled = (act * spread_heads(part_columns(inside))).astype(bf16)
    early = iota((HEADS, 128), 1) < 8
    lead = jnp.where(early, step[:, :128] * jnp.exp(jnp.where(early, -cum[:, :128], 0.0)), 0.0)
    lead_ref[...] = spread_heads(part_columns(lead)[0:16])[0:8]
    cum_spread = spread_heads(part_columns(jnp.exp(cum)))
    copies[2].wait()
    copies[3].wait()
    gate = silu(z_ref[...].astype(f32))
    gate_first_ref[...] = gate[0:8] * skip
    gate_ref[...] = gate * cum_spread
    b_rows = bc_act_ref[:, :STATE]
    c_rows = bc_act_ref[:, STATE:]
    skipped = jnp.where(iota((LENGTH, WIDTH), 0) < EDGE, 0.0, skip * act)
    t_at = lax.broadcasted_iota(jnp.int32, (BLOCK, BLOCK), 0)
    s_at = lax.broadcasted_iota(jnp.int32, (BLOCK, BLOCK), 1)
    causal = t_at >= s_at
    low_lanes = lax.broadcasted_iota(jnp.int32, (BLOCK, 128), 1) < HEAD
    for block in range(LENGTH // BLOCK):
        rows = slice(block * BLOCK, (block + 1) * BLOCK)
        scores = lax.dot_general(
            c_rows[rows], b_rows[: (block + 1) * BLOCK], (((1,), (1,)), ((), ())), preferred_element_type=f32
        )
        for pair in range(HEADS // 2):
            lanes = slice(128 * pair, 128 * (pair + 1))
            mixing = []
            for h in (2 * pair, 2 * pair + 1):
                here = cum_columns[rows, h : h + 1]
                tiles = []
                for other in range(block + 1):
                    columns = slice(other * BLOCK, (other + 1) * BLOCK)
                    spread = here - cum[h : h + 1, columns]
                    if other == block:
                        spread = jnp.where(causal, spread, -jnp.inf)
                    tiles.append((scores[:, columns] * jnp.exp(spread)).astype(bf16))
                mixing.append(tiles[0] if block == 0 else jnp.concatenate(tiles, axis=1))
            sums = dot(jnp.concatenate(mixing, axis=0), scaled[: (block + 1) * BLOCK, lanes])
            within = jnp.where(low_lanes, sums[:BLOCK], sums[BLOCK:])
            local_ref[rows, lanes] = (within + skipped[rows, lanes]) * gate[rows, lanes]


def all_lanes(row):
    return jnp.where(iota((1, 128), 1) < HEAD, rolled(row, HEAD, 1), row)


def taps_of(tile):
    pairs = tile[3:5] + tile[5:7]
    return [pairs[0:1], rolled(pairs[0:1], HEAD, 1), pairs[1:2], rolled(pairs[1:2], HEAD, 1)]


def edge_rows(tile, before, before_last, scalars, taps_x, taps_b):
    row = iota((8, 128), 0)
    lane = iota((8, 128), 1)
    sums = own_taps(jnp.where(row < EDGE, tile, 0.0), taps_x)
    sums_b = own_taps(jnp.where(row < EDGE, rolled(tile, -EDGE, 0), 0.0), taps_b)
    if before is not None:
        sums = sums + earlier_taps(jnp.where(row < EDGE, rolled(before, HEAD, 1), 0.0), taps_x)
        sums_b = sums_b + earlier_taps(jnp.where(row < EDGE, before_last, 0.0), taps_b)
    factor = jnp.sum(jnp.where(lane == row, scalars, 0.0), axis=1, keepdims=True)
    weighted = rounded(silu(sums)) * factor
    weighted = jnp.where((row < EDGE) & (lane < HEAD), weighted, 0.0)
    return weighted, jnp.where(row < EDGE, rounded(silu(sums_b)), 0.0)


def edge_states(entries):
    zeros = jnp.zeros((HEAD - 8 * len(entries), 128), f32)
    pad = [zeros] if zeros.shape[0] else []
    weighted = jnp.concatenate([e[0] for e in entries] + pad, axis=0)
    weighted = jnp.concatenate([weighted, rolled(weighted, HEAD, 1)], axis=0)
    b_rows = jnp.concatenate([e[1] for e in entries] + pad + [jnp.zeros((HEAD, 128), f32)], axis=0).T
    left = jnp.where(iota((HEAD, 128), 1) < HEAD, b_rows[:HEAD], rolled(b_rows[HEAD:], HEAD, 1)).astype(bf16)
    owner = (iota((128, 128), 0) % HEAD) // 8
    return [dot(left, jnp.where(owner == e, weighted, 0.0).astype(bf16)) for e in range(len(entries))]


def prefix_kernel(message_ref, taps_ref, prefix_ref, scale_ref, total_ref):
    tiles = [message_ref[m, HEAD:].astype(f32) for m in range(GROUP)]
    scalars = [t[6:7] + t[7:8] for t in tiles]
    decays = [all_lanes(s) for s in scalars]
    taps_x = taps_of(tiles[0][8:])
    taps_b = [taps_ref[k : k + 1, :STATE] for k in range(4)]
    entries = [
        edge_rows(tiles[m][:8], tiles[m - 1][:8], tiles[m - 1][8:], scalars[m], taps_x, taps_b) for m in range(1, GROUP)
    ]
    edges = edge_states(entries)
    state = message_ref[0, 0:HEAD].astype(f32)
    scale = jnp.ones((1, 128), f32)
    for m in range(1, GROUP):
        prefix_ref[m] = state
        scale_ref[m] = jnp.broadcast_to(scale, (8, 128))
        state = decays[m] * state + (message_ref[m, 0:HEAD].astype(f32) + edges[m - 1])
        scale = decays[m] * scale
    total_ref[0:HEAD] = state.astype(bf16)
    lane = iota((1, 128), 1)
    high, middle, _ = (p.astype(f32) for p in parts3(jnp.where(lane < HEAD, scalars[0] * scale, decays[0] * scale)))
    row = iota((8, 128), 0)
    first, last = tiles[0][:8], tiles[GROUP - 1]
    tile = jnp.where((row < EDGE) & (iota((8, 128), 1) >= HEAD), last[:8], first)
    tile = jnp.where(row == 6, high, jnp.where(row == 7, middle, tile))
    total_ref[HEAD:] = jnp.concatenate([tile, last[8:]], axis=0).astype(bf16)


def entering_kernel(
    gain_ref, message_ref, taps_ref, prefix_ref, scale_ref,
    other_ref, relayed_ref, skipped_ref, near_ref, far_ref, state_ref,
):
    own = message_ref[0, HEAD:].astype(f32)
    taps_x = taps_of(own[8:])
    taps_b = [taps_ref[k : k + 1, :STATE] for k in range(4)]
    totals = [far_ref[...].astype(f32), relayed_ref[...].astype(f32) + skipped_ref[...].astype(f32), near_ref[...].astype(f32) + other_ref[...].astype(f32)]
    tiles = [t[HEAD:] for t in totals] + [own]
    scalars = [t[6:7] + t[7:8] for t in tiles]
    entries = [edge_rows(tiles[0][:8], None, None, scalars[0], taps_x, taps_b)]
    for e in range(1, 4):
        entries.append(edge_rows(tiles[e][:8], tiles[e - 1][:8], tiles[e - 1][8:], scalars[e], taps_x, taps_b))
    edges = edge_states(entries)
    entering = totals[0][0:HEAD] + edges[0]
    for e in range(1, 3):
        entering = all_lanes(scalars[e]) * entering + (totals[e][0:HEAD] + edges[e])
    state_ref[0, 0:HEAD] = entering.astype(bf16)
    state_ref[0, HEAD:] = tiles[2].astype(bf16)
    after_first = all_lanes(scalars[3]) * entering + edges[3]
    for m in range(1, GROUP):
        state_ref[m, 0:HEAD] = (prefix_ref[m] + scale_ref[m, 0:1] * after_first).astype(bf16)
        state_ref[m, HEAD:] = message_ref[m - 1, HEAD:]


def output_kernel(
    state_ref, bc_act_ref, first_x_ref, first_bc_ref, taps_x_ref, taps_bc_ref, lead_ref, gate_first_ref,
    local_ref, gate_ref, gain_ref, weight_ref, share_ref,
):
    row = iota((8, 128), 0)
    few = iota((8, 128), 1) < HEAD
    low_lanes = iota((HEAD, 128), 1) < HEAD
    tiles = [state_ref[h, HEAD:].astype(f32) for h in range(HEADS)]

    last_x = jnp.concatenate(
        [jnp.where(few, rolled(tiles[h][:8], HEAD, 1), tiles[h + 1][:8]) for h in range(0, HEADS, 2)], axis=1
    )
    last_c = jnp.zeros((8, 128), f32)
    for h in range(EDGE):
        last_c = jnp.where(row == h, tiles[h][15:16], last_c)
    last_bc = jnp.concatenate([tiles[0][8:], last_c], axis=1)
    last_x = jnp.where(iota((8, WIDTH), 0) < EDGE, last_x, 0.0)
    last_bc = jnp.where(iota((8, 2 * STATE), 0) < EDGE, last_bc, 0.0)
    taps_x = [taps_x_ref[k : k + 1] for k in range(4)]
    taps_bc = [taps_bc_ref[k : k + 1] for k in range(4)]
    act = rounded(silu(first_x_ref[...] + earlier_taps(last_x, taps_x)))
    bc_act = rounded(silu(first_bc_ref[...] + earlier_taps(last_bc, taps_bc)))
    b_first, c_first = bc_act[:, :STATE], bc_act[:, STATE:]
    lead = rounded(jnp.where(iota((8, WIDTH), 0) < EDGE, act * lead_ref[...], 0.0))

    pairs = []
    for pair in range(HEADS // 2):
        even = state_ref[2 * pair, 0:HEAD].astype(f32)
        odd = state_ref[2 * pair + 1, 0:HEAD].astype(f32)
        top = jnp.where(low_lanes, even, rolled(odd, HEAD, 1))
        bottom = jnp.where(low_lanes, rolled(even, HEAD, 1), odd)
        pairs.append(jnp.concatenate([top, bottom], axis=0))
    states = jnp.concatenate(pairs, axis=1)
    b_columns = jnp.concatenate([b_first, jnp.zeros((120, STATE), f32)], axis=0).T.astype(bf16)
    lead_rows = jnp.concatenate([lead, jnp.zeros((120, WIDTH), f32)], axis=0).astype(bf16)
    states = (states + dot(b_columns, lead_rows)).astype(bf16)
    c_rows = jnp.concatenate([c_first, bc_act_ref[:, STATE:].astype(f32)[8:]], axis=0).astype(bf16)
    gated = local_ref[...] + gate_ref[...] * dot(c_rows, states)
    ahead = jnp.zeros((8, WIDTH), f32)
    for s in range(1, EDGE):
        score = jnp.sum(c_first * b_first[s : s + 1], axis=1, keepdims=True)
        ahead = ahead + jnp.where(iota((8, WIDTH), 0) < s, score * lead[s : s + 1], 0.0)
    skipped = jnp.where(iota((8, WIDTH), 0) < EDGE, gate_first_ref[...] * act, 0.0)
    gated = jnp.concatenate([gated[0:8] + (skipped - gate_ref[0:8] * ahead), gated[8:]], axis=0)

    squares = jnp.sum(gated * gated, axis=1, keepdims=True)
    scaled = (gated * gain_ref[...]).astype(bf16)
    wide = jnp.broadcast_to(squares, (LENGTH, 128))
    row_at = lax.broadcasted_iota(jnp.int32, (EXTRA, 128), 0)
    extra = jnp.zeros((EXTRA, 128), f32)
    for block in range(LENGTH // BLOCK):
        row = wide[block * BLOCK : (block + 1) * BLOCK].T[0:1]
        for k, part in enumerate(parts3(row)):
            extra = jnp.where(row_at == 3 * block + k, part.astype(f32), extra)
    extra = extra.astype(bf16)
    for pair in range(SHARES // 2):
        product = dot(scaled, weight_ref[:, 256 * pair : 256 * (pair + 1)]).astype(bf16)
        share_ref[2 * pair, 0:LENGTH] = product[:, :128]
        share_ref[2 * pair, LENGTH:] = extra
        share_ref[2 * pair + 1, 0:LENGTH] = product[:, 128:]
        share_ref[2 * pair + 1, LENGTH:] = extra


def sum_kernel(share_ref, out_ref):
    total = share_ref[0].astype(f32)
    for d in range(1, SHARES):
        total = total + share_ref[d].astype(f32)
    extra = total[LENGTH:]
    for block in range(LENGTH // BLOCK):
        rows = slice(block * BLOCK, (block + 1) * BLOCK)
        squares = extra[3 * block : 3 * block + 1] + (
            extra[3 * block + 1 : 3 * block + 2] + extra[3 * block + 2 : 3 * block + 3]
        )
        scale = lax.rsqrt(squares / INNER + 1e-05)
        column = jnp.broadcast_to(scale, (128, 128)).T
        out_ref[rows] = (total[rows] * column).astype(bf16)


HERE = pl.BlockSpec(memory_space=pltpu.VMEM)
THERE = pl.BlockSpec(memory_space=pltpu.HBM)


def stay(a):
    return pltpu.with_memory_space_constraint(a, pltpu.HBM)


def call(kernel, outs, *args, specs=None, scratch=(), flops=1e8, transcendentals=0):
    return pl.pallas_call(
        kernel,
        out_shape=[jax.ShapeDtypeStruct(s, d) for s, d in outs],
        in_specs=specs or [HERE] * len(args),
        out_specs=[HERE] * len(outs),
        scratch_shapes=list(scratch),
        compiler_params=pltpu.CompilerParams(vmem_limit_bytes=32 * 1024 * 1024),
        cost_estimate=pl.CostEstimate(
            flops=int(flops), bytes_accessed=2_000_000, transcendentals=int(transcendentals)
        ),
    )(*(stay(a) if spec is THERE else a for a, spec in zip(args, specs or [HERE] * len(args))))


def shards(
    inner_x, gate_z, bc_input, conv_inner, conv_bc, step_size, log_decay, skip_gain, norm_gain, out_weight
):
    message, act, bc_act, cum, first_x, first_bc, taps_x, taps_bc = call(
        summary_kernel,
        [
            ((HEADS, HEAD + EXTRA, 128), bf16), ((LENGTH, WIDTH), bf16), ((LENGTH, 2 * STATE), bf16),
            ((HEADS, LENGTH), f32), ((8, WIDTH), f32), ((8, 2 * STATE), f32), ((4, WIDTH), f32), ((4, 2 * STATE), f32),
        ],
        inner_x, bc_input, conv_inner, conv_bc, step_size, log_decay,
        specs=[THERE] * 6,
        scratch=[
            pltpu.VMEM((LENGTH + 8, WIDTH), f32), pltpu.VMEM((LENGTH + 8, 2 * STATE), f32),
            pltpu.VMEM((LENGTH, WIDTH), bf16), pltpu.VMEM((LENGTH, 2 * STATE), bf16),
            pltpu.VMEM((HEADS, LENGTH), f32), pltpu.VMEM((HEADS, LENGTH), f32),
            pltpu.SemaphoreType.DMA((6,)),
        ],
    )
    groups = [list(range(i, i + GROUP)) for i in range(0, BLOCKS, GROUP)]
    message = lax.all_to_all(message, "seq", 0, 0, tiled=True, axis_index_groups=groups)
    prefix, scale, total = call(
        prefix_kernel,
        [((GROUP, HEAD, 128), f32), ((GROUP, 8, 128), f32), ((HEAD + EXTRA, 128), bf16)],
        message, taps_bc,
    )
    def later(a, distance, first, last):
        return lax.ppermute(a, "seq", [(i, i + distance * GROUP) for i in range(first * GROUP, (last + 1) * GROUP)])

    pairs = [(i, i + GROUP) for i in (*range(GROUP), *range(2 * GROUP, 3 * GROUP))]
    near, far, skipped = lax.ppermute(total, "seq", pairs), later(total, 3, 0, 0), later(total, 2, 1, 1)
    relayed, other = later(near, 1, 1, 1), later(total, 1, 1, 1)
    local, gate, gain, lead, gate_first = call(
        within_kernel,
        [((LENGTH, WIDTH), f32), ((LENGTH, WIDTH), f32), ((1, WIDTH), f32), ((8, WIDTH), f32), ((8, WIDTH), f32)],
        act, bc_act, cum, step_size, skip_gain, gate_z, norm_gain[None, :], near,
        specs=[HERE, HERE, HERE, THERE, THERE, THERE, THERE, HERE],
        scratch=[
            pltpu.VMEM((HEADS, LENGTH), f32), pltpu.VMEM((LENGTH, WIDTH), bf16), pltpu.SMEM((HEADS,), f32),
            pltpu.SemaphoreType.DMA((4,)),
        ],
        flops=2e9, transcendentals=1.2e6,
    )

    (state,) = call(
        entering_kernel,
        [((GROUP, HEAD + EXTRA, 128), bf16)],
        gain, message, taps_bc, prefix, scale, other, relayed, skipped, near, far,
    )
    state = lax.all_to_all(state, "seq", 0, 0, tiled=True, axis_index_groups=groups)
    (share,) = call(
        output_kernel,
        [((SHARES, LENGTH + EXTRA, 128), bf16)],
        state, bc_act, first_x, first_bc, taps_x, taps_bc, lead, gate_first, local, gate, gain, out_weight,
        flops=9e8,
    )
    share = lax.all_to_all(share, "tp", 0, 0, tiled=True)
    (mixed,) = call(sum_kernel, [((LENGTH, 128), bf16)], share)
    return mixed


def solution(mesh):
    in_specs = (
        P("seq", "tp"),
        P("seq", "tp"),
        P("seq", None),
        P(None, "tp"),
        P(),
        P("tp", "seq"),
        P("tp", "seq"),
        P("tp"),
        P("tp"),
        P("tp", None),
    )
    return jax.shard_map(shards, mesh=mesh, in_specs=in_specs, out_specs=P("seq", "tp"), check_vma=False)
```

```python
import jax
import jax.numpy as jnp
from jax import lax
from jax.experimental import pallas as pl
from jax.experimental.pallas import tpu as pltpu
from jax.sharding import PartitionSpec as P

INNER = 8192
HEADS = 8
HEAD = 64
WIDTH = HEADS * HEAD
STATE = 128
LENGTH = 384
BLOCK = 128
BLOCKS = 32
GROUP = 8
SHARES = 16
EDGE = 3
EXTRA = 16

f32 = jnp.float32
bf16 = jnp.bfloat16


def parts3(a):
    high = a.astype(bf16)
    rest = a - high.astype(f32)
    middle = rest.astype(bf16)
    low = (rest - middle.astype(f32)).astype(bf16)
    return high, middle, low


def silu(a):
    return a * jax.nn.sigmoid(a)


def dot(a, b):
    return lax.dot_general(a, b, (((1,), (0,)), ((), ())), preferred_element_type=f32)


def columns_of(rows):
    padded = jnp.concatenate([rows, jnp.zeros((128 - rows.shape[0], rows.shape[1]), f32)], axis=0)
    return padded.T


def part_columns(rows):
    return columns_of(jnp.concatenate([p.astype(f32) for p in parts3(rows)], axis=0)).astype(bf16)


def spread_heads(columns):
    part = iota((128, WIDTH), 0)
    chosen = (part < 3 * HEADS) & (part % HEADS == iota((128, WIDTH), 1) // HEAD)
    return dot(columns, jnp.where(chosen, 1.0, 0.0).astype(bf16))


def rolled(a, distance, axis):
    return pltpu.roll(a, distance % a.shape[axis], axis)


def iota(shape, axis):
    return lax.broadcasted_iota(jnp.int32, shape, axis)


def before_taps(ext, weights):
    total = weights[0:1] * ext[5 : 5 + LENGTH]
    for k in range(1, 4):
        total = total + weights[k : k + 1] * ext[5 + k : 5 + k + LENGTH]
    return total


def earlier_taps(last, taps):
    total = taps[0] * last + taps[1] * rolled(last, -1, 0) + taps[2] * rolled(last, -2, 0)
    return jnp.where(iota(last.shape, 0) < EDGE, total, 0.0)


def own_taps(first, taps):
    return taps[3] * first + taps[2] * rolled(first, 1, 0) + taps[1] * rolled(first, 2, 0)


def rounded(a):
    return a.astype(bf16).astype(f32)


def fetch(pairs, sems):
    copies = [pltpu.make_async_copy(there, here, sems.at[i]) for i, (there, here) in enumerate(pairs)]
    for copy in copies:
        copy.start()
    return copies


def summary_kernel(
    x_at, bc_at, cx_at, cbc_at, step_at, decay_at, z_at, gain_at, skip_at,
    message_ref, act_ref, bc_act_ref, cum_ref, first_x_ref, first_bc_ref, taps_x_ref, taps_bc_ref,
    step_ref, z_ref, gain_ref, skip_row_ref,
    ext_x, ext_bc, x_ref, bc_ref, decay_ref, skip_ref, sems,
):
    copies = fetch(
        [
            (decay_at, decay_ref), (step_at, step_ref), (cx_at, taps_x_ref),
            (cbc_at, taps_bc_ref), (bc_at, bc_ref), (x_at, x_ref),
            (z_at, z_ref), (gain_at, gain_ref), (skip_at, skip_ref),
        ],
        sems,
    )
    copies[0].wait()
    copies[1].wait()
    upto = jnp.where(iota((LENGTH, LENGTH), 0) <= iota((LENGTH, LENGTH), 1), 1.0, 0.0).astype(bf16)
    sums = dot(jnp.concatenate([p.astype(f32) for p in parts3(decay_ref[...])], axis=0).astype(bf16), upto)
    cum = sums[0:8] + (sums[8:16] + sums[16:24])
    cum_ref[...] = cum
    last = cum[:, LENGTH - 1 : LENGTH]
    factor = step_ref[...] * jnp.exp(last - cum)
    inside = jnp.where(iota((HEADS, LENGTH), 1) < EDGE, 0.0, factor)
    factor_spread = spread_heads(part_columns(inside))
    for copy in copies[2:6]:
        copy.wait()
    ext_x[0:8] = jnp.zeros((8, WIDTH), f32)
    ext_bc[0:8] = jnp.zeros((8, 2 * STATE), f32)
    ext_x[8:] = x_ref[...].astype(f32)
    ext_bc[8:] = bc_ref[...].astype(f32)
    sums = before_taps(ext_bc, taps_bc_ref)
    first_bc_ref[...] = sums[0:8]
    bc_act = silu(sums).astype(bf16)
    bc_act_ref[...] = bc_act
    sums = before_taps(ext_x, taps_x_ref)
    first_x_ref[...] = sums[0:8]
    act = silu(sums).astype(bf16)
    act_ref[...] = act

    weighted = (act.astype(f32) * factor_spread).astype(bf16)
    b_rows = bc_act[:, :STATE].astype(f32)
    summary = dot(b_rows.T.astype(bf16), weighted)

    total = jnp.broadcast_to(jnp.exp(last), (HEADS, 128))
    scalars = jnp.where(iota((HEADS, 128), 1) < HEAD, factor[:, :128], total)
    high, middle, _ = (p.astype(f32) for p in parts3(scalars))
    tap_high, tap_middle, _ = (p.astype(f32) for p in parts3(taps_x_ref[...]))
    low_lanes = iota((HEAD, 128), 1) < HEAD
    few = iota((8, 128), 1) < HEAD
    row = iota((8, 128), 0)
    b_first = rolled(ext_bc[8:16, :STATE], 3, 0)
    bc_last = rolled(ext_bc[LENGTH : LENGTH + 8], 3, 0)
    for h in range(HEADS):
        lanes = slice(128 * (h // 2), 128 * (h // 2 + 1))
        even = h % 2 == 0

        def side_by_side(left, right, where):
            if even:
                return jnp.where(where, left, rolled(right, HEAD, 1))
            return jnp.where(where, rolled(left, HEAD, 1), right)

        message_ref[h, 0:HEAD] = side_by_side(summary[:HEAD, lanes], summary[HEAD:, lanes], low_lanes).astype(bf16)
        x_edges = side_by_side(ext_x[8:16, lanes], rolled(ext_x[LENGTH : LENGTH + 8, lanes], 3, 0), few)
        tile = jnp.where(row < 3, x_edges, b_first)
        tile = jnp.where(row == 6, high[h : h + 1], jnp.where(row == 7, middle[h : h + 1], tile))
        other = bc_last[:, :STATE]
        for at, (part, k) in enumerate(((tap_high, 0), (tap_high, 2), (tap_middle, 0), (tap_middle, 2))):
            pair = side_by_side(part[k : k + 1, lanes], part[k + 1 : k + 2, lanes], few[0:1])
            other = jnp.where(row == 3 + at, pair, other)
        c_row = bc_last[h : h + 1, STATE:] if h < EDGE else jnp.zeros((1, STATE), f32)
        other = jnp.where(row == 7, c_row, other)
        message_ref[h, HEAD:] = jnp.concatenate([tile, other], axis=0).astype(bf16)

    for copy in copies[6:]:
        copy.wait()
    head_at = iota((1, WIDTH), 1) // HEAD
    skip = jnp.zeros((1, WIDTH), f32)
    for h in range(HEADS):
        skip = jnp.where(head_at == h, skip_ref[h], skip)
    skip_row_ref[...] = skip


def within_kernel(
    act_ref, bc_act_ref, cum_ref, step_ref, skip_row_ref, z_ref, after_ref,
    local_ref, gate_ref, lead_ref, gate_first_ref,
):
    skip = skip_row_ref[...]
    cum = cum_ref[...]
    cum_columns = columns_of(cum)
    act = act_ref[...].astype(f32)
    step = step_ref[...]
    inside = jnp.where(iota((HEADS, LENGTH), 1) < EDGE, 0.0, step)
    scaled = (act * spread_heads(part_columns(inside))).astype(bf16)
    early = iota((HEADS, 128), 1) < 8
    lead = jnp.where(early, step[:, :128] * jnp.exp(jnp.where(early, -cum[:, :128], 0.0)), 0.0)
    lead_ref[...] = spread_heads(part_columns(lead)[0:16])[0:8]
    cum_spread = spread_heads(part_columns(jnp.exp(cum)))
    gate = silu(z_ref[...].astype(f32))
    gate_first_ref[...] = gate[0:8] * skip
    gate_ref[...] = gate * cum_spread
    b_rows = bc_act_ref[:, :STATE]
    c_rows = bc_act_ref[:, STATE:]
    skipped = jnp.where(iota((LENGTH, WIDTH), 0) < EDGE, 0.0, skip * act)
    t_at = lax.broadcasted_iota(jnp.int32, (BLOCK, BLOCK), 0)
    s_at = lax.broadcasted_iota(jnp.int32, (BLOCK, BLOCK), 1)
    causal = t_at >= s_at
    low_lanes = lax.broadcasted_iota(jnp.int32, (BLOCK, 128), 1) < HEAD
    for block in range(LENGTH // BLOCK):
        rows = slice(block * BLOCK, (block + 1) * BLOCK)
        scores = lax.dot_general(
            c_rows[rows], b_rows[: (block + 1) * BLOCK], (((1,), (1,)), ((), ())), preferred_element_type=f32
        )
        for pair in range(HEADS // 2):
            lanes = slice(128 * pair, 128 * (pair + 1))
            mixing = []
            for h in (2 * pair, 2 * pair + 1):
                here = cum_columns[rows, h : h + 1]
                tiles = []
                for other in range(block + 1):
                    columns = slice(other * BLOCK, (other + 1) * BLOCK)
                    spread = here - cum[h : h + 1, columns]
                    if other == block:
                        spread = jnp.where(causal, spread, -jnp.inf)
                    tiles.append((scores[:, columns] * jnp.exp(spread)).astype(bf16))
                mixing.append(tiles[0] if block == 0 else jnp.concatenate(tiles, axis=1))
            sums = dot(jnp.concatenate(mixing, axis=0), scaled[: (block + 1) * BLOCK, lanes])
            within = jnp.where(low_lanes, sums[:BLOCK], sums[BLOCK:])
            local_ref[rows, lanes] = (within + skipped[rows, lanes]) * gate[rows, lanes]


def all_lanes(row):
    return jnp.where(iota((1, 128), 1) < HEAD, rolled(row, HEAD, 1), row)


def taps_of(tile):
    pairs = tile[3:5] + tile[5:7]
    return [pairs[0:1], rolled(pairs[0:1], HEAD, 1), pairs[1:2], rolled(pairs[1:2], HEAD, 1)]


def edge_rows(tile, before, before_last, scalars, taps_x, taps_b):
    row = iota((8, 128), 0)
    lane = iota((8, 128), 1)
    sums = own_taps(jnp.where(row < EDGE, tile, 0.0), taps_x)
    sums_b = own_taps(jnp.where(row < EDGE, rolled(tile, -EDGE, 0), 0.0), taps_b)
    if before is not None:
        sums = sums + earlier_taps(jnp.where(row < EDGE, rolled(before, HEAD, 1), 0.0), taps_x)
        sums_b = sums_b + earlier_taps(jnp.where(row < EDGE, before_last, 0.0), taps_b)
    factor = jnp.sum(jnp.where(lane == row, scalars, 0.0), axis=1, keepdims=True)
    weighted = rounded(silu(sums)) * factor
    weighted = jnp.where((row < EDGE) & (lane < HEAD), weighted, 0.0)
    return weighted, jnp.where(row < EDGE, rounded(silu(sums_b)), 0.0)


def edge_states(entries):
    zeros = jnp.zeros((HEAD - 8 * len(entries), 128), f32)
    pad = [zeros] if zeros.shape[0] else []
    weighted = jnp.concatenate([e[0] for e in entries] + pad, axis=0)
    weighted = jnp.concatenate([weighted, rolled(weighted, HEAD, 1)], axis=0)
    b_rows = jnp.concatenate([e[1] for e in entries] + pad + [jnp.zeros((HEAD, 128), f32)], axis=0).T
    left = jnp.where(iota((HEAD, 128), 1) < HEAD, b_rows[:HEAD], rolled(b_rows[HEAD:], HEAD, 1)).astype(bf16)
    owner = (iota((128, 128), 0) % HEAD) // 8
    return [dot(left, jnp.where(owner == e, weighted, 0.0).astype(bf16)) for e in range(len(entries))]


def prefix_kernel(message_ref, taps_ref, prefix_ref, scale_ref, total_ref):
    tiles = [message_ref[m, HEAD:].astype(f32) for m in range(GROUP)]
    scalars = [t[6:7] + t[7:8] for t in tiles]
    decays = [all_lanes(s) for s in scalars]
    taps_x = taps_of(tiles[0][8:])
    taps_b = [taps_ref[k : k + 1, :STATE] for k in range(4)]
    entries = [
        edge_rows(tiles[m][:8], tiles[m - 1][:8], tiles[m - 1][8:], scalars[m], taps_x, taps_b) for m in range(1, GROUP)
    ]
    edges = edge_states(entries)
    state = message_ref[0, 0:HEAD].astype(f32)
    scale = jnp.ones((1, 128), f32)
    for m in range(1, GROUP):
        prefix_ref[m] = state
        scale_ref[m] = jnp.broadcast_to(scale, (8, 128))
        state = decays[m] * state + (message_ref[m, 0:HEAD].astype(f32) + edges[m - 1])
        scale = decays[m] * scale
    total_ref[0:HEAD] = state.astype(bf16)
    lane = iota((1, 128), 1)
    high, middle, _ = (p.astype(f32) for p in parts3(jnp.where(lane < HEAD, scalars[0] * scale, decays[0] * scale)))
    row = iota((8, 128), 0)
    first, last = tiles[0][:8], tiles[GROUP - 1]
    tile = jnp.where((row < EDGE) & (iota((8, 128), 1) >= HEAD), last[:8], first)
    tile = jnp.where(row == 6, high, jnp.where(row == 7, middle, tile))
    total_ref[HEAD:] = jnp.concatenate([tile, last[8:]], axis=0).astype(bf16)


def entering_kernel(
    lead_ref, message_ref, taps_ref, prefix_ref, scale_ref,
    relayed_ref, other_ref, skipped_ref, near_ref, state_ref,
):
    own = message_ref[0, HEAD:].astype(f32)
    taps_x = taps_of(own[8:])
    taps_b = [taps_ref[k : k + 1, :STATE] for k in range(4)]
    third = lax.axis_index("seq") // GROUP == 2
    other = other_ref[...].astype(f32)
    totals = [
        jnp.where(third, 0.0, other),
        relayed_ref[...].astype(f32) + skipped_ref[...].astype(f32),
        near_ref[...].astype(f32) + jnp.where(third, other, 0.0),
    ]
    tiles = [t[HEAD:] for t in totals] + [own]
    scalars = [t[6:7] + t[7:8] for t in tiles]
    entries = [edge_rows(tiles[0][:8], None, None, scalars[0], taps_x, taps_b)]
    for e in range(1, 4):
        entries.append(edge_rows(tiles[e][:8], tiles[e - 1][:8], tiles[e - 1][8:], scalars[e], taps_x, taps_b))
    edges = edge_states(entries)
    entering = totals[0][0:HEAD] + edges[0]
    for e in range(1, 3):
        entering = all_lanes(scalars[e]) * entering + (totals[e][0:HEAD] + edges[e])
    state_ref[0, 0:HEAD] = entering.astype(bf16)
    state_ref[0, HEAD:] = tiles[2].astype(bf16)
    after_first = all_lanes(scalars[3]) * entering + edges[3]
    for m in range(1, GROUP):
        state_ref[m, 0:HEAD] = (prefix_ref[m] + scale_ref[m, 0:1] * after_first).astype(bf16)
        state_ref[m, HEAD:] = message_ref[m - 1, HEAD:]


def output_kernel(
    state_ref, bc_act_ref, first_x_ref, first_bc_ref, taps_x_ref, taps_bc_ref, lead_ref, gate_first_ref,
    local_ref, gate_ref, gain_ref, weight_ref, share_ref,
):
    row = iota((8, 128), 0)
    few = iota((8, 128), 1) < HEAD
    low_lanes = iota((HEAD, 128), 1) < HEAD
    tiles = [state_ref[h, HEAD:].astype(f32) for h in range(HEADS)]

    last_x = jnp.concatenate(
        [jnp.where(few, rolled(tiles[h][:8], HEAD, 1), tiles[h + 1][:8]) for h in range(0, HEADS, 2)], axis=1
    )
    last_c = jnp.zeros((8, 128), f32)
    for h in range(EDGE):
        last_c = jnp.where(row == h, tiles[h][15:16], last_c)
    last_bc = jnp.concatenate([tiles[0][8:], last_c], axis=1)
    last_x = jnp.where(iota((8, WIDTH), 0) < EDGE, last_x, 0.0)
    last_bc = jnp.where(iota((8, 2 * STATE), 0) < EDGE, last_bc, 0.0)
    taps_x = [taps_x_ref[k : k + 1] for k in range(4)]
    taps_bc = [taps_bc_ref[k : k + 1] for k in range(4)]
    act = rounded(silu(first_x_ref[...] + earlier_taps(last_x, taps_x)))
    bc_act = rounded(silu(first_bc_ref[...] + earlier_taps(last_bc, taps_bc)))
    b_first, c_first = bc_act[:, :STATE], bc_act[:, STATE:]
    lead = rounded(jnp.where(iota((8, WIDTH), 0) < EDGE, act * lead_ref[...], 0.0))

    pairs = []
    for pair in range(HEADS // 2):
        even = state_ref[2 * pair, 0:HEAD].astype(f32)
        odd = state_ref[2 * pair + 1, 0:HEAD].astype(f32)
        top = jnp.where(low_lanes, even, rolled(odd, HEAD, 1))
        bottom = jnp.where(low_lanes, rolled(even, HEAD, 1), odd)
        pairs.append(jnp.concatenate([top, bottom], axis=0))
    states = jnp.concatenate(pairs, axis=1)
    b_columns = jnp.concatenate([b_first, jnp.zeros((120, STATE), f32)], axis=0).T.astype(bf16)
    lead_rows = jnp.concatenate([lead, jnp.zeros((120, WIDTH), f32)], axis=0).astype(bf16)
    states = (states + dot(b_columns, lead_rows)).astype(bf16)
    c_rows = jnp.concatenate([c_first, bc_act_ref[:, STATE:].astype(f32)[8:]], axis=0).astype(bf16)
    gated = local_ref[...] + gate_ref[...] * dot(c_rows, states)
    ahead = jnp.zeros((8, WIDTH), f32)
    for s in range(1, EDGE):
        score = jnp.sum(c_first * b_first[s : s + 1], axis=1, keepdims=True)
        ahead = ahead + jnp.where(iota((8, WIDTH), 0) < s, score * lead[s : s + 1], 0.0)
    skipped = jnp.where(iota((8, WIDTH), 0) < EDGE, gate_first_ref[...] * act, 0.0)
    gated = jnp.concatenate([gated[0:8] + (skipped - gate_ref[0:8] * ahead), gated[8:]], axis=0)

    squares = jnp.sum(gated * gated, axis=1, keepdims=True)
    scaled = (gated * gain_ref[...]).astype(bf16)
    wide = jnp.broadcast_to(squares, (LENGTH, 128))
    row_at = lax.broadcasted_iota(jnp.int32, (EXTRA, 128), 0)
    extra = jnp.zeros((EXTRA, 128), f32)
    for block in range(LENGTH // BLOCK):
        row = wide[block * BLOCK : (block + 1) * BLOCK].T[0:1]
        for k, part in enumerate(parts3(row)):
            extra = jnp.where(row_at == 3 * block + k, part.astype(f32), extra)
    extra = extra.astype(bf16)
    for pair in range(SHARES // 2):
        product = dot(scaled, weight_ref[:, 256 * pair : 256 * (pair + 1)]).astype(bf16)
        share_ref[2 * pair, 0:LENGTH] = product[:, :128]
        share_ref[2 * pair, LENGTH:] = extra
        share_ref[2 * pair + 1, 0:LENGTH] = product[:, 128:]
        share_ref[2 * pair + 1, LENGTH:] = extra


def sum_kernel(share_ref, out_ref):
    total = share_ref[0].astype(f32)
    for d in range(1, SHARES):
        total = total + share_ref[d].astype(f32)
    extra = total[LENGTH:]
    for block in range(LENGTH // BLOCK):
        rows = slice(block * BLOCK, (block + 1) * BLOCK)
        squares = extra[3 * block : 3 * block + 1] + (
            extra[3 * block + 1 : 3 * block + 2] + extra[3 * block + 2 : 3 * block + 3]
        )
        scale = lax.rsqrt(squares / INNER + 1e-05)
        column = jnp.broadcast_to(scale, (128, 128)).T
        out_ref[rows] = (total[rows] * column).astype(bf16)


HERE = pl.BlockSpec(memory_space=pltpu.VMEM)
THERE = pl.BlockSpec(memory_space=pltpu.HBM)


def stay(a):
    return pltpu.with_memory_space_constraint(a, pltpu.HBM)


def call(kernel, outs, *args, specs=None, scratch=(), flops=1e8, transcendentals=0):
    return pl.pallas_call(
        kernel,
        out_shape=[jax.ShapeDtypeStruct(s, d) for s, d in outs],
        in_specs=specs or [HERE] * len(args),
        out_specs=[HERE] * len(outs),
        scratch_shapes=list(scratch),
        compiler_params=pltpu.CompilerParams(vmem_limit_bytes=32 * 1024 * 1024),
        cost_estimate=pl.CostEstimate(
            flops=int(flops), bytes_accessed=2_000_000, transcendentals=int(transcendentals)
        ),
    )(*(stay(a) if spec is THERE else a for a, spec in zip(args, specs or [HERE] * len(args))))


def shards(
    inner_x, gate_z, bc_input, conv_inner, conv_bc, step_size, log_decay, skip_gain, norm_gain, out_weight
):
    message, act, bc_act, cum, first_x, first_bc, taps_x, taps_bc, step, z, gain, skip = call(
        summary_kernel,
        [
            ((HEADS, HEAD + EXTRA, 128), bf16), ((LENGTH, WIDTH), bf16), ((LENGTH, 2 * STATE), bf16),
            ((HEADS, LENGTH), f32), ((8, WIDTH), f32), ((8, 2 * STATE), f32), ((4, WIDTH), f32), ((4, 2 * STATE), f32),
            ((HEADS, LENGTH), f32), ((LENGTH, WIDTH), bf16), ((1, WIDTH), f32), ((1, WIDTH), f32),
        ],
        inner_x, bc_input, conv_inner, conv_bc, step_size, log_decay, gate_z, norm_gain[None, :], skip_gain,
        specs=[THERE] * 9,
        scratch=[
            pltpu.VMEM((LENGTH + 8, WIDTH), f32), pltpu.VMEM((LENGTH + 8, 2 * STATE), f32),
            pltpu.VMEM((LENGTH, WIDTH), bf16), pltpu.VMEM((LENGTH, 2 * STATE), bf16),
            pltpu.VMEM((HEADS, LENGTH), f32), pltpu.SMEM((HEADS,), f32),
            pltpu.SemaphoreType.DMA((9,)),
        ],
    )
    groups = [list(range(i, i + GROUP)) for i in range(0, BLOCKS, GROUP)]
    message = lax.all_to_all(message, "seq", 0, 0, tiled=True, axis_index_groups=groups)
    prefix, scale, total = call(
        prefix_kernel,
        [((GROUP, HEAD, 128), f32), ((GROUP, 8, 128), f32), ((HEAD + EXTRA, 128), bf16)],
        message, taps_bc,
    )
    def later(a, distance, first, last):
        return lax.ppermute(a, "seq", [(i, i + distance * GROUP) for i in range(first * GROUP, (last + 1) * GROUP)])

    def permuted(a, *ways):
        return lax.ppermute(a, "seq", [(i + f * GROUP, i + t * GROUP) for f, t in ways for i in range(GROUP)])

    near, skipped, other = permuted(total, (0, 1), (2, 3)), permuted(total, (1, 3)), permuted(total, (0, 3), (1, 2))
    relayed = permuted(near, (1, 2))
    local, gate, lead, gate_first = call(
        within_kernel,
        [((LENGTH, WIDTH), f32), ((LENGTH, WIDTH), f32), ((8, WIDTH), f32), ((8, WIDTH), f32)],
        act, bc_act, cum, step, skip, z, near,
        flops=2e9, transcendentals=1.2e6,
    )
    (state,) = call(
        entering_kernel,
        [((GROUP, HEAD + EXTRA, 128), bf16)],
        lead, message, taps_bc, prefix, scale, relayed, other, skipped, near,
    )
    state = lax.all_to_all(state, "seq", 0, 0, tiled=True, axis_index_groups=groups)
    (share,) = call(
        output_kernel,
        [((SHARES, LENGTH + EXTRA, 128), bf16)],
        state, bc_act, first_x, first_bc, taps_x, taps_bc, lead, gate_first, local, gate, gain, out_weight,
        flops=9e8,
    )
    share = lax.all_to_all(share, "tp", 0, 0, tiled=True)
    (mixed,) = call(sum_kernel, [((LENGTH, 128), bf16)], share)
    return mixed


def solution(mesh):
    in_specs = (
        P("seq", "tp"),
        P("seq", "tp"),
        P("seq", None),
        P(None, "tp"),
        P(),
        P("tp", "seq"),
        P("tp", "seq"),
        P("tp"),
        P("tp"),
        P("tp", None),
    )
    return jax.shard_map(shards, mesh=mesh, in_specs=in_specs, out_specs=P("seq", "tp"), check_vma=False)
```

```python
import jax
import jax.numpy as jnp
from jax import lax
from jax.experimental import pallas as pl
from jax.experimental.pallas import tpu as pltpu
from jax.sharding import PartitionSpec as P

INNER = 8192
HEADS = 8
HEAD = 64
WIDTH = HEADS * HEAD
STATE = 128
LENGTH = 384
BLOCK = 128
BLOCKS = 32
GROUP = 8
SHARES = 16
EDGE = 3
EXTRA = 16

f32 = jnp.float32
bf16 = jnp.bfloat16


def parts3(a):
    high = a.astype(bf16)
    rest = a - high.astype(f32)
    middle = rest.astype(bf16)
    low = (rest - middle.astype(f32)).astype(bf16)
    return high, middle, low


def silu(a):
    return a * jax.nn.sigmoid(a)


def dot(a, b):
    return lax.dot_general(a, b, (((1,), (0,)), ((), ())), preferred_element_type=f32)


def columns_of(rows):
    padded = jnp.concatenate([rows, jnp.zeros((128 - rows.shape[0], rows.shape[1]), f32)], axis=0)
    return padded.T


def part_columns(rows):
    return columns_of(jnp.concatenate([p.astype(f32) for p in parts3(rows)], axis=0)).astype(bf16)


def spread_heads(columns):
    part = iota((128, WIDTH), 0)
    chosen = (part < 3 * HEADS) & (part % HEADS == iota((128, WIDTH), 1) // HEAD)
    return dot(columns, jnp.where(chosen, 1.0, 0.0).astype(bf16))


def rolled(a, distance, axis):
    return pltpu.roll(a, distance % a.shape[axis], axis)


def iota(shape, axis):
    return lax.broadcasted_iota(jnp.int32, shape, axis)


def before_taps(ext, late, weights):
    here, back = ext[8 : 8 + LENGTH], ext[7 : 7 + LENGTH]
    late[8:] = weights[1:2] * here + weights[0:1] * back
    return weights[3:4] * here + weights[2:3] * back + late[6 : 6 + LENGTH]


def earlier_taps(last, taps):
    total = taps[0] * last + taps[1] * rolled(last, -1, 0) + taps[2] * rolled(last, -2, 0)
    return jnp.where(iota(last.shape, 0) < EDGE, total, 0.0)


def own_taps(first, taps):
    return taps[3] * first + taps[2] * rolled(first, 1, 0) + taps[1] * rolled(first, 2, 0)


def rounded(a):
    return a.astype(bf16).astype(f32)


def fetch(pairs, sems):
    copies = [pltpu.make_async_copy(there, here, sems.at[i]) for i, (there, here) in enumerate(pairs)]
    for copy in copies:
        copy.start()
    return copies


def summary_kernel(
    x_at, bc_at, cx_at, cbc_at, step_at, decay_at, z_at, gain_at, skip_at,
    message_ref, act_ref, bc_act_ref, cum_ref, first_x_ref, first_bc_ref, taps_x_ref, taps_bc_ref,
    step_ref, z_ref, gain_ref, skip_row_ref,
    ext_x, ext_bc, late_x, late_bc, x_ref, bc_ref, decay_ref, skip_ref, sems,
):
    copies = fetch(
        [
            (decay_at, decay_ref), (step_at, step_ref), (cx_at, taps_x_ref),
            (cbc_at, taps_bc_ref), (bc_at, bc_ref), (x_at, x_ref),
            (z_at, z_ref), (gain_at, gain_ref), (skip_at, skip_ref),
        ],
        sems,
    )
    copies[0].wait()
    copies[1].wait()
    upto = jnp.where(iota((LENGTH, LENGTH), 0) <= iota((LENGTH, LENGTH), 1), 1.0, 0.0).astype(bf16)
    sums = dot(jnp.concatenate([p.astype(f32) for p in parts3(decay_ref[...])], axis=0).astype(bf16), upto)
    cum = sums[0:8] + (sums[8:16] + sums[16:24])
    cum_ref[...] = cum
    last = cum[:, LENGTH - 1 : LENGTH]
    factor = step_ref[...] * jnp.exp(last - cum)
    inside = jnp.where(iota((HEADS, LENGTH), 1) < EDGE, 0.0, factor)
    factor_spread = spread_heads(part_columns(inside))
    for copy in copies[2:6]:
        copy.wait()
    ext_x[0:8] = jnp.zeros((8, WIDTH), f32)
    ext_bc[0:8] = jnp.zeros((8, 2 * STATE), f32)
    ext_x[8:] = x_ref[...].astype(f32)
    ext_bc[8:] = bc_ref[...].astype(f32)
    late_bc[0:8] = jnp.zeros((8, 2 * STATE), f32)
    late_x[0:8] = jnp.zeros((8, WIDTH), f32)
    sums = before_taps(ext_bc, late_bc, taps_bc_ref)
    first_bc_ref[...] = sums[0:8]
    bc_act = silu(sums).astype(bf16)
    bc_act_ref[...] = bc_act
    sums = before_taps(ext_x, late_x, taps_x_ref)
    first_x_ref[...] = sums[0:8]
    act = silu(sums).astype(bf16)
    act_ref[...] = act

    weighted = (act.astype(f32) * factor_spread).astype(bf16)
    b_rows = bc_act[:, :STATE].astype(f32)
    summary = dot(b_rows.T.astype(bf16), weighted)

    total = jnp.broadcast_to(jnp.exp(last), (HEADS, 128))
    scalars = jnp.where(iota((HEADS, 128), 1) < HEAD, factor[:, :128], total)
    high, middle, _ = (p.astype(f32) for p in parts3(scalars))
    tap_high, tap_middle, _ = (p.astype(f32) for p in parts3(taps_x_ref[...]))
    low_lanes = iota((HEAD, 128), 1) < HEAD
    few = iota((8, 128), 1) < HEAD
    row = iota((8, 128), 0)
    b_first = rolled(ext_bc[8:16, :STATE], 3, 0)
    bc_last = rolled(ext_bc[LENGTH : LENGTH + 8], 3, 0)
    for h in range(HEADS):
        lanes = slice(128 * (h // 2), 128 * (h // 2 + 1))
        even = h % 2 == 0

        def side_by_side(left, right, where):
            if even:
                return jnp.where(where, left, rolled(right, HEAD, 1))
            return jnp.where(where, rolled(left, HEAD, 1), right)

        message_ref[h, 0:HEAD] = side_by_side(summary[:HEAD, lanes], summary[HEAD:, lanes], low_lanes).astype(bf16)
        x_edges = side_by_side(ext_x[8:16, lanes], rolled(ext_x[LENGTH : LENGTH + 8, lanes], 3, 0), few)
        tile = jnp.where(row < 3, x_edges, b_first)
        tile = jnp.where(row == 6, high[h : h + 1], jnp.where(row == 7, middle[h : h + 1], tile))
        other = bc_last[:, :STATE]
        for at, (part, k) in enumerate(((tap_high, 0), (tap_high, 2), (tap_middle, 0), (tap_middle, 2))):
            pair = side_by_side(part[k : k + 1, lanes], part[k + 1 : k + 2, lanes], few[0:1])
            other = jnp.where(row == 3 + at, pair, other)
        c_row = bc_last[h : h + 1, STATE:] if h < EDGE else jnp.zeros((1, STATE), f32)
        other = jnp.where(row == 7, c_row, other)
        message_ref[h, HEAD:] = jnp.concatenate([tile, other], axis=0).astype(bf16)

    for copy in copies[6:]:
        copy.wait()
    head_at = iota((1, WIDTH), 1) // HEAD
    skip = jnp.zeros((1, WIDTH), f32)
    for h in range(HEADS):
        skip = jnp.where(head_at == h, skip_ref[h], skip)
    skip_row_ref[...] = skip


def within_kernel(
    act_ref, bc_act_ref, cum_ref, step_ref, skip_row_ref, z_ref, after_ref,
    local_ref, gate_ref, lead_ref, gate_first_ref,
):
    skip = skip_row_ref[...]
    cum = cum_ref[...]
    cum_columns = columns_of(cum)
    act = act_ref[...].astype(f32)
    step = step_ref[...]
    inside = jnp.where(iota((HEADS, LENGTH), 1) < EDGE, 0.0, step)
    scaled = (act * spread_heads(part_columns(inside))).astype(bf16)
    early = iota((HEADS, 128), 1) < 8
    lead = jnp.where(early, step[:, :128] * jnp.exp(jnp.where(early, -cum[:, :128], 0.0)), 0.0)
    lead_ref[...] = spread_heads(part_columns(lead)[0:16])[0:8]
    cum_spread = spread_heads(part_columns(jnp.exp(cum)))
    gate = silu(z_ref[...].astype(f32))
    gate_first_ref[...] = gate[0:8] * skip
    gate_ref[...] = gate * cum_spread
    b_rows = bc_act_ref[:, :STATE]
    c_rows = bc_act_ref[:, STATE:]
    skipped = jnp.where(iota((LENGTH, WIDTH), 0) < EDGE, 0.0, skip * act)
    t_at = lax.broadcasted_iota(jnp.int32, (BLOCK, BLOCK), 0)
    s_at = lax.broadcasted_iota(jnp.int32, (BLOCK, BLOCK), 1)
    causal = t_at >= s_at
    low_lanes = lax.broadcasted_iota(jnp.int32, (BLOCK, 128), 1) < HEAD
    for block in range(LENGTH // BLOCK):
        rows = slice(block * BLOCK, (block + 1) * BLOCK)
        scores = lax.dot_general(
            c_rows[rows], b_rows[: (block + 1) * BLOCK], (((1,), (1,)), ((), ())), preferred_element_type=f32
        )
        for pair in range(HEADS // 2):
            lanes = slice(128 * pair, 128 * (pair + 1))
            mixing = []
            for h in (2 * pair, 2 * pair + 1):
                here = cum_columns[rows, h : h + 1]
                tiles = []
                for other in range(block + 1):
                    columns = slice(other * BLOCK, (other + 1) * BLOCK)
                    spread = here - cum[h : h + 1, columns]
                    if other == block:
                        spread = jnp.where(causal, spread, -jnp.inf)
                    tiles.append((scores[:, columns] * jnp.exp(spread)).astype(bf16))
                mixing.append(tiles[0] if block == 0 else jnp.concatenate(tiles, axis=1))
            sums = dot(jnp.concatenate(mixing, axis=0), scaled[: (block + 1) * BLOCK, lanes])
            within = jnp.where(low_lanes, sums[:BLOCK], sums[BLOCK:])
            local_ref[rows, lanes] = (within + skipped[rows, lanes]) * gate[rows, lanes]


def all_lanes(row):
    return jnp.where(iota((1, 128), 1) < HEAD, rolled(row, HEAD, 1), row)


def taps_of(tile):
    pairs = tile[3:5] + tile[5:7]
    return [pairs[0:1], rolled(pairs[0:1], HEAD, 1), pairs[1:2], rolled(pairs[1:2], HEAD, 1)]


def edge_rows(tile, before, before_last, scalars, taps_x, taps_b):
    row = iota((8, 128), 0)
    lane = iota((8, 128), 1)
    sums = own_taps(jnp.where(row < EDGE, tile, 0.0), taps_x)
    sums_b = own_taps(jnp.where(row < EDGE, rolled(tile, -EDGE, 0), 0.0), taps_b)
    if before is not None:
        sums = sums + earlier_taps(jnp.where(row < EDGE, rolled(before, HEAD, 1), 0.0), taps_x)
        sums_b = sums_b + earlier_taps(jnp.where(row < EDGE, before_last, 0.0), taps_b)
    factor = jnp.sum(jnp.where(lane == row, scalars, 0.0), axis=1, keepdims=True)
    weighted = rounded(silu(sums)) * factor
    weighted = jnp.where((row < EDGE) & (lane < HEAD), weighted, 0.0)
    return weighted, jnp.where(row < EDGE, rounded(silu(sums_b)), 0.0)


def edge_states(entries):
    zeros = jnp.zeros((HEAD - 8 * len(entries), 128), f32)
    pad = [zeros] if zeros.shape[0] else []
    weighted = jnp.concatenate([e[0] for e in entries] + pad, axis=0)
    weighted = jnp.concatenate([weighted, rolled(weighted, HEAD, 1)], axis=0)
    b_rows = jnp.concatenate([e[1] for e in entries] + pad + [jnp.zeros((HEAD, 128), f32)], axis=0).T
    left = jnp.where(iota((HEAD, 128), 1) < HEAD, b_rows[:HEAD], rolled(b_rows[HEAD:], HEAD, 1)).astype(bf16)
    owner = (iota((128, 128), 0) % HEAD) // 8
    return [dot(left, jnp.where(owner == e, weighted, 0.0).astype(bf16)) for e in range(len(entries))]


def prefix_kernel(message_ref, taps_ref, prefix_ref, scale_ref, total_ref):
    tiles = [message_ref[m, HEAD:].astype(f32) for m in range(GROUP)]
    scalars = [t[6:7] + t[7:8] for t in tiles]
    decays = [all_lanes(s) for s in scalars]
    taps_x = taps_of(tiles[0][8:])
    taps_b = [taps_ref[k : k + 1, :STATE] for k in range(4)]
    entries = [
        edge_rows(tiles[m][:8], tiles[m - 1][:8], tiles[m - 1][8:], scalars[m], taps_x, taps_b) for m in range(1, GROUP)
    ]
    edges = edge_states(entries)
    state = message_ref[0, 0:HEAD].astype(f32)
    scale = jnp.ones((1, 128), f32)
    for m in range(1, GROUP):
        prefix_ref[m] = state
        scale_ref[m] = jnp.broadcast_to(scale, (8, 128))
        state = decays[m] * state + (message_ref[m, 0:HEAD].astype(f32) + edges[m - 1])
        scale = decays[m] * scale
    total_ref[0:HEAD] = state.astype(bf16)
    lane = iota((1, 128), 1)
    high, middle, _ = (p.astype(f32) for p in parts3(jnp.where(lane < HEAD, scalars[0] * scale, decays[0] * scale)))
    row = iota((8, 128), 0)
    first, last = tiles[0][:8], tiles[GROUP - 1]
    tile = jnp.where((row < EDGE) & (iota((8, 128), 1) >= HEAD), last[:8], first)
    tile = jnp.where(row == 6, high, jnp.where(row == 7, middle, tile))
    total_ref[HEAD:] = jnp.concatenate([tile, last[8:]], axis=0).astype(bf16)


def joined_kernel(lead_ref, total_ref, swapped_ref, taps_ref, joined_ref, own_ref):
    zeroth = lax.axis_index("seq") // GROUP == 0
    total, swapped = total_ref[...].astype(f32), swapped_ref[...].astype(f32)
    first, second = jnp.where(zeroth, total, swapped), jnp.where(zeroth, swapped, total)
    taps_x = taps_of(total[HEAD + 8 :])
    taps_b = [taps_ref[k : k + 1, :STATE] for k in range(4)]
    tiles = [first[HEAD:], second[HEAD:]]
    scalars = [t[6:7] + t[7:8] for t in tiles]
    edges = edge_states(
        [
            edge_rows(tiles[0][:8], None, None, scalars[0], taps_x, taps_b),
            edge_rows(tiles[1][:8], tiles[0][:8], tiles[0][8:], scalars[1], taps_x, taps_b),
        ]
    )
    state = all_lanes(scalars[1]) * (first[:HEAD] + edges[0]) + (second[:HEAD] + edges[1])
    joined_ref[0:HEAD] = state.astype(bf16)
    joined_ref[HEAD:] = tiles[1].astype(bf16)
    own_ref[...] = total_ref[...]


def entering_kernel(
    message_ref, taps_ref, prefix_ref, scale_ref, swapped_ref, crossed_ref, passed_ref, state_ref
):
    group = lax.axis_index("seq") // GROUP
    crossed = crossed_ref[...].astype(f32)
    near = jnp.where(group == 1, swapped_ref[...].astype(f32), passed_ref[...].astype(f32))
    own = message_ref[0, HEAD:].astype(f32)
    before = jnp.where(group == 2, crossed[HEAD:], near[HEAD:])
    taps_x = taps_of(own[8:])
    taps_b = [taps_ref[k : k + 1, :STATE] for k in range(4)]
    scalars = [t[6:7] + t[7:8] for t in (near[HEAD:], own)]
    edges = edge_states(
        [
            edge_rows(near[HEAD : HEAD + 8], crossed[HEAD : HEAD + 8], crossed[HEAD + 8 :], scalars[0], taps_x, taps_b),
            edge_rows(own[:8], before[:8], before[8:], scalars[1], taps_x, taps_b),
        ]
    )
    entering = all_lanes(scalars[0]) * crossed[:HEAD] + (near[:HEAD] + edges[0])
    entering = jnp.where(group == 2, crossed[:HEAD], entering)
    state_ref[0, 0:HEAD] = entering.astype(bf16)
    state_ref[0, HEAD:] = before.astype(bf16)
    after_first = all_lanes(scalars[1]) * entering + edges[1]
    for m in range(1, GROUP):
        state_ref[m, 0:HEAD] = (prefix_ref[m] + scale_ref[m, 0:1] * after_first).astype(bf16)
        state_ref[m, HEAD:] = message_ref[m - 1, HEAD:]


def output_kernel(
    state_ref, bc_act_ref, first_x_ref, first_bc_ref, taps_x_ref, taps_bc_ref, lead_ref, gate_first_ref,
    local_ref, gate_ref, gain_ref, weight_ref, share_ref,
):
    row = iota((8, 128), 0)
    few = iota((8, 128), 1) < HEAD
    low_lanes = iota((HEAD, 128), 1) < HEAD
    tiles = [state_ref[h, HEAD:].astype(f32) for h in range(HEADS)]

    last_x = jnp.concatenate(
        [jnp.where(few, rolled(tiles[h][:8], HEAD, 1), tiles[h + 1][:8]) for h in range(0, HEADS, 2)], axis=1
    )
    last_c = jnp.zeros((8, 128), f32)
    for h in range(EDGE):
        last_c = jnp.where(row == h, tiles[h][15:16], last_c)
    last_bc = jnp.concatenate([tiles[0][8:], last_c], axis=1)
    last_x = jnp.where(iota((8, WIDTH), 0) < EDGE, last_x, 0.0)
    last_bc = jnp.where(iota((8, 2 * STATE), 0) < EDGE, last_bc, 0.0)
    taps_x = [taps_x_ref[k : k + 1] for k in range(4)]
    taps_bc = [taps_bc_ref[k : k + 1] for k in range(4)]
    act = rounded(silu(first_x_ref[...] + earlier_taps(last_x, taps_x)))
    bc_act = rounded(silu(first_bc_ref[...] + earlier_taps(last_bc, taps_bc)))
    b_first, c_first = bc_act[:, :STATE], bc_act[:, STATE:]
    lead = rounded(jnp.where(iota((8, WIDTH), 0) < EDGE, act * lead_ref[...], 0.0))

    pairs = []
    for pair in range(HEADS // 2):
        even = state_ref[2 * pair, 0:HEAD].astype(f32)
        odd = state_ref[2 * pair + 1, 0:HEAD].astype(f32)
        top = jnp.where(low_lanes, even, rolled(odd, HEAD, 1))
        bottom = jnp.where(low_lanes, rolled(even, HEAD, 1), odd)
        pairs.append(jnp.concatenate([top, bottom], axis=0))
    states = jnp.concatenate(pairs, axis=1)
    b_columns = jnp.concatenate([b_first, jnp.zeros((120, STATE), f32)], axis=0).T.astype(bf16)
    lead_rows = jnp.concatenate([lead, jnp.zeros((120, WIDTH), f32)], axis=0).astype(bf16)
    states = (states + dot(b_columns, lead_rows)).astype(bf16)
    c_rows = jnp.concatenate([c_first, bc_act_ref[:, STATE:].astype(f32)[8:]], axis=0).astype(bf16)
    gated = local_ref[...] + gate_ref[...] * dot(c_rows, states)
    ahead = jnp.zeros((8, WIDTH), f32)
    for s in range(1, EDGE):
        score = jnp.sum(c_first * b_first[s : s + 1], axis=1, keepdims=True)
        ahead = ahead + jnp.where(iota((8, WIDTH), 0) < s, score * lead[s : s + 1], 0.0)
    skipped = jnp.where(iota((8, WIDTH), 0) < EDGE, gate_first_ref[...] * act, 0.0)
    gated = jnp.concatenate([gated[0:8] + (skipped - gate_ref[0:8] * ahead), gated[8:]], axis=0)

    squares = jnp.sum(gated * gated, axis=1, keepdims=True)
    scaled = (gated * gain_ref[...]).astype(bf16)
    wide = jnp.broadcast_to(squares, (LENGTH, 128))
    row_at = lax.broadcasted_iota(jnp.int32, (EXTRA, 128), 0)
    extra = jnp.zeros((EXTRA, 128), f32)
    for block in range(LENGTH // BLOCK):
        row = wide[block * BLOCK : (block + 1) * BLOCK].T[0:1]
        for k, part in enumerate(parts3(row)):
            extra = jnp.where(row_at == 3 * block + k, part.astype(f32), extra)
    extra = extra.astype(bf16)
    for pair in range(SHARES // 2):
        product = dot(scaled, weight_ref[:, 256 * pair : 256 * (pair + 1)]).astype(bf16)
        share_ref[2 * pair, 0:LENGTH] = product[:, :128]
        share_ref[2 * pair, LENGTH:] = extra
        share_ref[2 * pair + 1, 0:LENGTH] = product[:, 128:]
        share_ref[2 * pair + 1, LENGTH:] = extra


def sum_kernel(share_ref, out_ref):
    total = share_ref[0].astype(f32)
    for d in range(1, SHARES):
        total = total + share_ref[d].astype(f32)
    extra = total[LENGTH:]
    for block in range(LENGTH // BLOCK):
        rows = slice(block * BLOCK, (block + 1) * BLOCK)
        squares = extra[3 * block : 3 * block + 1] + (
            extra[3 * block + 1 : 3 * block + 2] + extra[3 * block + 2 : 3 * block + 3]
        )
        scale = lax.rsqrt(squares / INNER + 1e-05)
        column = jnp.broadcast_to(scale, (128, 128)).T
        out_ref[rows] = (total[rows] * column).astype(bf16)


HERE = pl.BlockSpec(memory_space=pltpu.VMEM)
THERE = pl.BlockSpec(memory_space=pltpu.HBM)


def stay(a):
    return pltpu.with_memory_space_constraint(a, pltpu.HBM)


def call(kernel, outs, *args, specs=None, scratch=(), flops=1e8, transcendentals=0):
    return pl.pallas_call(
        kernel,
        out_shape=[jax.ShapeDtypeStruct(s, d) for s, d in outs],
        in_specs=specs or [HERE] * len(args),
        out_specs=[HERE] * len(outs),
        scratch_shapes=list(scratch),
        compiler_params=pltpu.CompilerParams(vmem_limit_bytes=32 * 1024 * 1024),
        cost_estimate=pl.CostEstimate(
            flops=int(flops), bytes_accessed=2_000_000, transcendentals=int(transcendentals)
        ),
    )(*(stay(a) if spec is THERE else a for a, spec in zip(args, specs or [HERE] * len(args))))


def shards(
    inner_x, gate_z, bc_input, conv_inner, conv_bc, step_size, log_decay, skip_gain, norm_gain, out_weight
):
    message, act, bc_act, cum, first_x, first_bc, taps_x, taps_bc, step, z, gain, skip = call(
        summary_kernel,
        [
            ((HEADS, HEAD + EXTRA, 128), bf16), ((LENGTH, WIDTH), bf16), ((LENGTH, 2 * STATE), bf16),
            ((HEADS, LENGTH), f32), ((8, WIDTH), f32), ((8, 2 * STATE), f32), ((4, WIDTH), f32), ((4, 2 * STATE), f32),
            ((HEADS, LENGTH), f32), ((LENGTH, WIDTH), bf16), ((1, WIDTH), f32), ((1, WIDTH), f32),
        ],
        inner_x, bc_input, conv_inner, conv_bc, step_size, log_decay, gate_z, norm_gain[None, :], skip_gain,
        specs=[THERE] * 9,
        scratch=[
            pltpu.VMEM((LENGTH + 8, WIDTH), f32), pltpu.VMEM((LENGTH + 8, 2 * STATE), f32),
            pltpu.VMEM((LENGTH + 8, WIDTH), f32), pltpu.VMEM((LENGTH + 8, 2 * STATE), f32),
            pltpu.VMEM((LENGTH, WIDTH), bf16), pltpu.VMEM((LENGTH, 2 * STATE), bf16),
            pltpu.VMEM((HEADS, LENGTH), f32), pltpu.SMEM((HEADS,), f32),
            pltpu.SemaphoreType.DMA((9,)),
        ],
    )
    groups = [list(range(i, i + GROUP)) for i in range(0, BLOCKS, GROUP)]
    message = lax.all_to_all(message, "seq", 0, 0, tiled=True, axis_index_groups=groups)
    prefix, scale, total = call(
        prefix_kernel,
        [((GROUP, HEAD, 128), f32), ((GROUP, 8, 128), f32), ((HEAD + EXTRA, 128), bf16)],
        message, taps_bc,
    )
    def later(a, distance, first, last):
        return lax.ppermute(a, "seq", [(i, i + distance * GROUP) for i in range(first * GROUP, (last + 1) * GROUP)])

    def permuted(a, *ways):
        return lax.ppermute(a, "seq", [(i + f * GROUP, i + t * GROUP) for f, t in ways for i in range(GROUP)])

    swapped = permuted(total, (0, 1), (1, 0))
    local, gate, lead, gate_first = call(
        within_kernel,
        [((LENGTH, WIDTH), f32), ((LENGTH, WIDTH), f32), ((8, WIDTH), f32), ((8, WIDTH), f32)],
        act, bc_act, cum, step, skip, z, total,
        flops=2e9, transcendentals=1.2e6,
    )
    joined, own = call(
        joined_kernel,
        [((HEAD + EXTRA, 128), bf16), ((HEAD + EXTRA, 128), bf16)],
        lead, total, swapped, taps_bc,
    )
    crossed, passed = permuted(joined, (1, 2), (0, 3)), permuted(own, (2, 3))
    (state,) = call(
        entering_kernel,
        [((GROUP, HEAD + EXTRA, 128), bf16)],
        message, taps_bc, prefix, scale, swapped, crossed, passed,
    )
    state = lax.all_to_all(state, "seq", 0, 0, tiled=True, axis_index_groups=groups)
    (share,) = call(
        output_kernel,
        [((SHARES, LENGTH + EXTRA, 128), bf16)],
        state, bc_act, first_x, first_bc, taps_x, taps_bc, lead, gate_first, local, gate, gain, out_weight,
        flops=9e8,
    )
    share = lax.all_to_all(share, "tp", 0, 0, tiled=True)
    (mixed,) = call(sum_kernel, [((LENGTH, 128), bf16)], share)
    return mixed


def solution(mesh):
    in_specs = (
        P("seq", "tp"),
        P("seq", "tp"),
        P("seq", None),
        P(None, "tp"),
        P(),
        P("tp", "seq"),
        P("tp", "seq"),
        P("tp"),
        P("tp"),
        P("tp", None),
    )
    return jax.shard_map(shards, mesh=mesh, in_specs=in_specs, out_specs=P("seq", "tp"), check_vma=False)
```

```python
import jax
import jax.numpy as jnp
from jax import lax
from jax.experimental import pallas as pl
from jax.experimental.pallas import tpu as pltpu
from jax.sharding import PartitionSpec as P

INNER = 8192
HEADS = 8
HEAD = 64
WIDTH = HEADS * HEAD
STATE = 128
LENGTH = 384
BLOCK = 128
BLOCKS = 32
GROUP = 8
SHARES = 16
EDGE = 3
EXTRA = 16

f32 = jnp.float32
bf16 = jnp.bfloat16


def parts3(a):
    high = a.astype(bf16)
    rest = a - high.astype(f32)
    middle = rest.astype(bf16)
    low = (rest - middle.astype(f32)).astype(bf16)
    return high, middle, low


def silu(a):
    return a * jax.nn.sigmoid(a)


def dot(a, b):
    return lax.dot_general(a, b, (((1,), (0,)), ((), ())), preferred_element_type=f32)


def columns_of(rows):
    padded = jnp.concatenate([rows, jnp.zeros((128 - rows.shape[0], rows.shape[1]), f32)], axis=0)
    return padded.T


def part_columns(rows):
    return columns_of(jnp.concatenate([p.astype(f32) for p in parts3(rows)], axis=0)).astype(bf16)


def spread_heads(columns):
    part = iota((128, WIDTH), 0)
    chosen = (part < 3 * HEADS) & (part % HEADS == iota((128, WIDTH), 1) // HEAD)
    return dot(columns, jnp.where(chosen, 1.0, 0.0).astype(bf16))


def rolled(a, distance, axis):
    return pltpu.roll(a, distance % a.shape[axis], axis)


def iota(shape, axis):
    return lax.broadcasted_iota(jnp.int32, shape, axis)


def before_taps(ext, late, weights):
    here, back = ext[8 : 8 + LENGTH], ext[7 : 7 + LENGTH]
    late[8:] = weights[1:2] * here + weights[0:1] * back
    return weights[3:4] * here + weights[2:3] * back + late[6 : 6 + LENGTH]


def earlier_taps(last, taps):
    total = taps[0] * last + taps[1] * rolled(last, -1, 0) + taps[2] * rolled(last, -2, 0)
    return jnp.where(iota(last.shape, 0) < EDGE, total, 0.0)


def own_taps(first, taps):
    return taps[3] * first + taps[2] * rolled(first, 1, 0) + taps[1] * rolled(first, 2, 0)


def rounded(a):
    return a.astype(bf16).astype(f32)


def fetch(pairs, sems):
    copies = [pltpu.make_async_copy(there, here, sems.at[i]) for i, (there, here) in enumerate(pairs)]
    for copy in copies:
        copy.start()
    return copies


def summary_kernel(
    x_at, bc_at, cx_at, cbc_at, step_at, decay_at, z_at, gain_at, skip_at,
    message_ref, act_ref, bc_act_ref, cum_ref, first_x_ref, first_bc_ref, taps_x_ref, taps_bc_ref,
    step_ref, z_ref, gain_ref, skip_row_ref,
    ext_x, ext_bc, late_x, late_bc, x_ref, bc_ref, decay_ref, skip_ref, sems,
):
    copies = fetch(
        [
            (decay_at, decay_ref), (step_at, step_ref), (cx_at, taps_x_ref),
            (cbc_at, taps_bc_ref), (bc_at, bc_ref), (x_at, x_ref),
            (z_at, z_ref), (gain_at, gain_ref), (skip_at, skip_ref),
        ],
        sems,
    )
    copies[0].wait()
    copies[1].wait()
    upto = jnp.where(iota((LENGTH, LENGTH), 0) <= iota((LENGTH, LENGTH), 1), 1.0, 0.0).astype(bf16)
    sums = dot(jnp.concatenate([p.astype(f32) for p in parts3(decay_ref[...])], axis=0).astype(bf16), upto)
    cum = sums[0:8] + (sums[8:16] + sums[16:24])
    cum_ref[...] = cum
    last = cum[:, LENGTH - 1 : LENGTH]
    factor = step_ref[...] * jnp.exp(last - cum)
    inside = jnp.where(iota((HEADS, LENGTH), 1) < EDGE, 0.0, factor)
    factor_spread = spread_heads(part_columns(inside))
    for copy in copies[2:6]:
        copy.wait()
    ext_x[0:8] = jnp.zeros((8, WIDTH), f32)
    ext_bc[0:8] = jnp.zeros((8, 2 * STATE), f32)
    ext_x[8:] = x_ref[...].astype(f32)
    ext_bc[8:] = bc_ref[...].astype(f32)
    late_bc[0:8] = jnp.zeros((8, 2 * STATE), f32)
    late_x[0:8] = jnp.zeros((8, WIDTH), f32)
    sums = before_taps(ext_bc, late_bc, taps_bc_ref)
    first_bc_ref[...] = sums[0:8]
    bc_act = silu(sums).astype(bf16)
    bc_act_ref[...] = bc_act
    sums = before_taps(ext_x, late_x, taps_x_ref)
    first_x_ref[...] = sums[0:8]
    act = silu(sums).astype(bf16)
    act_ref[...] = act

    weighted = (act.astype(f32) * factor_spread).astype(bf16)
    b_rows = bc_act[:, :STATE].astype(f32)
    summary = dot(b_rows.T.astype(bf16), weighted)

    total = jnp.broadcast_to(jnp.exp(last), (HEADS, 128))
    lane = iota((HEADS, 128), 1)
    lead = step_ref[:, :128] * jnp.exp(jnp.where(lane < EDGE, -cum[:, :128], 0.0))
    scalars = jnp.where(lane < HEAD, lead, total)
    high, middle, _ = (p.astype(f32) for p in parts3(scalars))
    tap_high, tap_middle, _ = (p.astype(f32) for p in parts3(taps_x_ref[...]))
    low_lanes = iota((HEAD, 128), 1) < HEAD
    few = iota((8, 128), 1) < HEAD
    row = iota((8, 128), 0)
    b_first = rolled(ext_bc[8:16, :STATE], 3, 0)
    bc_last = rolled(ext_bc[LENGTH : LENGTH + 8], 3, 0)
    for h in range(HEADS):
        lanes = slice(128 * (h // 2), 128 * (h // 2 + 1))
        even = h % 2 == 0

        def side_by_side(left, right, where):
            if even:
                return jnp.where(where, left, rolled(right, HEAD, 1))
            return jnp.where(where, rolled(left, HEAD, 1), right)

        message_ref[h, 0:HEAD] = side_by_side(summary[:HEAD, lanes], summary[HEAD:, lanes], low_lanes).astype(bf16)
        x_edges = side_by_side(ext_x[8:16, lanes], rolled(ext_x[LENGTH : LENGTH + 8, lanes], 3, 0), few)
        tile = jnp.where(row < 3, x_edges, b_first)
        tile = jnp.where(row == 6, high[h : h + 1], jnp.where(row == 7, middle[h : h + 1], tile))
        other = bc_last[:, :STATE]
        for at, (part, k) in enumerate(((tap_high, 0), (tap_high, 2), (tap_middle, 0), (tap_middle, 2))):
            pair = side_by_side(part[k : k + 1, lanes], part[k + 1 : k + 2, lanes], few[0:1])
            other = jnp.where(row == 3 + at, pair, other)
        c_row = bc_last[h : h + 1, STATE:] if h < EDGE else jnp.zeros((1, STATE), f32)
        other = jnp.where(row == 7, c_row, other)
        message_ref[h, HEAD:] = jnp.concatenate([tile, other], axis=0).astype(bf16)

    for copy in copies[6:]:
        copy.wait()
    head_at = iota((1, WIDTH), 1) // HEAD
    skip = jnp.zeros((1, WIDTH), f32)
    for h in range(HEADS):
        skip = jnp.where(head_at == h, skip_ref[h], skip)
    skip_row_ref[...] = skip


def within_kernel(
    act_ref, bc_act_ref, cum_ref, step_ref, skip_row_ref, z_ref, after_ref,
    local_ref, gate_ref, lead_ref, gate_first_ref,
):
    skip = skip_row_ref[...]
    cum = cum_ref[...]
    cum_columns = columns_of(cum)
    act = act_ref[...].astype(f32)
    step = step_ref[...]
    inside = jnp.where(iota((HEADS, LENGTH), 1) < EDGE, 0.0, step)
    scaled = (act * spread_heads(part_columns(inside))).astype(bf16)
    early = iota((HEADS, 128), 1) < 8
    lead = jnp.where(early, step[:, :128] * jnp.exp(jnp.where(early, -cum[:, :128], 0.0)), 0.0)
    lead_ref[...] = spread_heads(part_columns(lead)[0:16])[0:8]
    cum_spread = spread_heads(part_columns(jnp.exp(cum)))
    gate = silu(z_ref[...].astype(f32))
    gate_first_ref[...] = gate[0:8] * skip
    gate_ref[...] = gate * cum_spread
    b_rows = bc_act_ref[:, :STATE]
    c_rows = bc_act_ref[:, STATE:]
    skipped = jnp.where(iota((LENGTH, WIDTH), 0) < EDGE, 0.0, skip * act)
    t_at = lax.broadcasted_iota(jnp.int32, (BLOCK, BLOCK), 0)
    s_at = lax.broadcasted_iota(jnp.int32, (BLOCK, BLOCK), 1)
    causal = t_at >= s_at
    low_lanes = lax.broadcasted_iota(jnp.int32, (BLOCK, 128), 1) < HEAD
    for block in range(LENGTH // BLOCK):
        rows = slice(block * BLOCK, (block + 1) * BLOCK)
        scores = lax.dot_general(
            c_rows[rows], b_rows[: (block + 1) * BLOCK], (((1,), (1,)), ((), ())), preferred_element_type=f32
        )
        for pair in range(HEADS // 2):
            lanes = slice(128 * pair, 128 * (pair + 1))
            mixing = []
            for h in (2 * pair, 2 * pair + 1):
                here = cum_columns[rows, h : h + 1]
                tiles = []
                for other in range(block + 1):
                    columns = slice(other * BLOCK, (other + 1) * BLOCK)
                    spread = here - cum[h : h + 1, columns]
                    if other == block:
                        spread = jnp.where(causal, spread, -jnp.inf)
                    tiles.append((scores[:, columns] * jnp.exp(spread)).astype(bf16))
                mixing.append(tiles[0] if block == 0 else jnp.concatenate(tiles, axis=1))
            sums = dot(jnp.concatenate(mixing, axis=0), scaled[: (block + 1) * BLOCK, lanes])
            within = jnp.where(low_lanes, sums[:BLOCK], sums[BLOCK:])
            local_ref[rows, lanes] = (within + skipped[rows, lanes]) * gate[rows, lanes]


def all_lanes(row):
    return jnp.where(iota((1, 128), 1) < HEAD, rolled(row, HEAD, 1), row)


def taps_of(tile):
    pairs = tile[3:5] + tile[5:7]
    return [pairs[0:1], rolled(pairs[0:1], HEAD, 1), pairs[1:2], rolled(pairs[1:2], HEAD, 1)]


def edge_rows(tile, before, before_last, scalars, taps_x, taps_b):
    row = iota((8, 128), 0)
    lane = iota((8, 128), 1)
    sums = own_taps(jnp.where(row < EDGE, tile, 0.0), taps_x)
    sums_b = own_taps(jnp.where(row < EDGE, rolled(tile, -EDGE, 0), 0.0), taps_b)
    if before is not None:
        sums = sums + earlier_taps(jnp.where(row < EDGE, rolled(before, HEAD, 1), 0.0), taps_x)
        sums_b = sums_b + earlier_taps(jnp.where(row < EDGE, before_last, 0.0), taps_b)
    factor = jnp.sum(jnp.where(lane == row, scalars, 0.0), axis=1, keepdims=True)
    weighted = rounded(silu(sums)) * factor
    weighted = jnp.where((row < EDGE) & (lane < HEAD), weighted, 0.0)
    return weighted, jnp.where(row < EDGE, rounded(silu(sums_b)), 0.0)


def edge_states(entries):
    zeros = jnp.zeros((HEAD - 8 * len(entries), 128), f32)
    pad = [zeros] if zeros.shape[0] else []
    weighted = jnp.concatenate([e[0] for e in entries] + pad, axis=0)
    weighted = jnp.concatenate([weighted, rolled(weighted, HEAD, 1)], axis=0)
    b_rows = jnp.concatenate([e[1] for e in entries] + pad + [jnp.zeros((HEAD, 128), f32)], axis=0).T
    left = jnp.where(iota((HEAD, 128), 1) < HEAD, b_rows[:HEAD], rolled(b_rows[HEAD:], HEAD, 1)).astype(bf16)
    owner = (iota((128, 128), 0) % HEAD) // 8
    return [dot(left, jnp.where(owner == e, weighted, 0.0).astype(bf16)) for e in range(len(entries))]


def prefix_kernel(message_ref, taps_ref, prefix_ref, scale_ref, edge_ref, total_ref):
    tiles = [message_ref[m, HEAD:].astype(f32) for m in range(GROUP)]
    scalars = [t[6:7] + t[7:8] for t in tiles]
    decays = [all_lanes(s) for s in scalars]
    taps_x = taps_of(tiles[0][8:])
    taps_b = [taps_ref[k : k + 1, :STATE] for k in range(4)]
    entries = [
        edge_rows(tiles[m][:8], tiles[m - 1][:8], tiles[m - 1][8:], scalars[m], taps_x, taps_b) for m in range(1, GROUP)
    ]
    edges = edge_states(entries)
    state = message_ref[0, 0:HEAD].astype(f32)
    scale = jnp.ones((1, 128), f32)
    for m in range(1, GROUP):
        prefix_ref[m] = state
        scale_ref[m] = jnp.broadcast_to(scale, (8, 128))
        edge_ref[m] = edges[m - 1]
        state = decays[m] * (state + edges[m - 1]) + message_ref[m, 0:HEAD].astype(f32)
        scale = decays[m] * scale
    total_ref[0:HEAD] = state.astype(bf16)
    lane = iota((1, 128), 1)
    high, middle, _ = (p.astype(f32) for p in parts3(jnp.where(lane < HEAD, scalars[0], decays[0] * scale)))
    row = iota((8, 128), 0)
    first, last = tiles[0][:8], tiles[GROUP - 1]
    tile = jnp.where((row < EDGE) & (iota((8, 128), 1) >= HEAD), last[:8], first)
    tile = jnp.where(row == 6, high, jnp.where(row == 7, middle, tile))
    total_ref[HEAD:] = jnp.concatenate([tile, last[8:]], axis=0).astype(bf16)


def joined_kernel(lead_ref, total_ref, swapped_ref, taps_ref, joined_ref, own_ref):
    zeroth = lax.axis_index("seq") // GROUP == 0
    total, swapped = total_ref[...].astype(f32), swapped_ref[...].astype(f32)
    first, second = jnp.where(zeroth, total, swapped), jnp.where(zeroth, swapped, total)
    taps_x = taps_of(total[HEAD + 8 :])
    taps_b = [taps_ref[k : k + 1, :STATE] for k in range(4)]
    tiles = [first[HEAD:], second[HEAD:]]
    scalars = [t[6:7] + t[7:8] for t in tiles]
    edges = edge_states(
        [
            edge_rows(tiles[0][:8], None, None, scalars[0], taps_x, taps_b),
            edge_rows(tiles[1][:8], tiles[0][:8], tiles[0][8:], scalars[1], taps_x, taps_b),
        ]
    )
    state = all_lanes(scalars[0]) * edges[0] + first[:HEAD]
    state = all_lanes(scalars[1]) * (state + edges[1]) + second[:HEAD]
    joined_ref[0:HEAD] = state.astype(bf16)
    joined_ref[HEAD:] = tiles[1].astype(bf16)
    own_ref[...] = total_ref[...]


def entering_kernel(
    message_ref, taps_ref, prefix_ref, scale_ref, edge_ref, swapped_ref, crossed_ref, passed_ref, state_ref
):
    group = lax.axis_index("seq") // GROUP
    crossed = crossed_ref[...].astype(f32)
    near = jnp.where(group == 1, swapped_ref[...].astype(f32), passed_ref[...].astype(f32))
    own = message_ref[0, HEAD:].astype(f32)
    before = jnp.where(group == 2, crossed[HEAD:], near[HEAD:])
    taps_x = taps_of(own[8:])
    taps_b = [taps_ref[k : k + 1, :STATE] for k in range(4)]
    scalars = [t[6:7] + t[7:8] for t in (near[HEAD:], own)]
    edges = edge_states(
        [
            edge_rows(near[HEAD : HEAD + 8], crossed[HEAD : HEAD + 8], crossed[HEAD + 8 :], scalars[0], taps_x, taps_b),
            edge_rows(own[:8], before[:8], before[8:], scalars[1], taps_x, taps_b),
        ]
    )
    entering = all_lanes(scalars[0]) * (crossed[:HEAD] + edges[0]) + near[:HEAD]
    entering = jnp.where(group == 2, crossed[:HEAD], entering)
    entering = entering + edges[1]
    state_ref[0, 0:HEAD] = entering.astype(bf16)
    state_ref[0, HEAD:] = before.astype(bf16)
    after_first = all_lanes(scalars[1]) * entering
    for m in range(1, GROUP):
        state = prefix_ref[m] + scale_ref[m, 0:1] * after_first + edge_ref[m]
        state_ref[m, 0:HEAD] = state.astype(bf16)
        state_ref[m, HEAD:] = message_ref[m - 1, HEAD:]


def output_kernel(
    state_ref, bc_act_ref, first_x_ref, first_bc_ref, taps_x_ref, taps_bc_ref, lead_ref, gate_first_ref,
    local_ref, gate_ref, gain_ref, weight_ref, share_ref,
):
    row = iota((8, 128), 0)
    few = iota((8, 128), 1) < HEAD
    low_lanes = iota((HEAD, 128), 1) < HEAD
    tiles = [state_ref[h, HEAD:].astype(f32) for h in range(HEADS)]

    last_x = jnp.concatenate(
        [jnp.where(few, rolled(tiles[h][:8], HEAD, 1), tiles[h + 1][:8]) for h in range(0, HEADS, 2)], axis=1
    )
    last_c = jnp.zeros((8, 128), f32)
    for h in range(EDGE):
        last_c = jnp.where(row == h, tiles[h][15:16], last_c)
    last_bc = jnp.concatenate([tiles[0][8:], last_c], axis=1)
    last_x = jnp.where(iota((8, WIDTH), 0) < EDGE, last_x, 0.0)
    last_bc = jnp.where(iota((8, 2 * STATE), 0) < EDGE, last_bc, 0.0)
    taps_x = [taps_x_ref[k : k + 1] for k in range(4)]
    taps_bc = [taps_bc_ref[k : k + 1] for k in range(4)]
    act = rounded(silu(first_x_ref[...] + earlier_taps(last_x, taps_x)))
    bc_act = rounded(silu(first_bc_ref[...] + earlier_taps(last_bc, taps_bc)))
    b_first, c_first = bc_act[:, :STATE], bc_act[:, STATE:]
    lead = rounded(jnp.where(iota((8, WIDTH), 0) < EDGE, act * lead_ref[...], 0.0))

    pairs = []
    for pair in range(HEADS // 2):
        even = state_ref[2 * pair, 0:HEAD].astype(f32)
        odd = state_ref[2 * pair + 1, 0:HEAD].astype(f32)
        top = jnp.where(low_lanes, even, rolled(odd, HEAD, 1))
        bottom = jnp.where(low_lanes, rolled(even, HEAD, 1), odd)
        pairs.append(jnp.concatenate([top, bottom], axis=0))
    states = jnp.concatenate(pairs, axis=1)
    states = states.astype(bf16)
    c_rows = jnp.concatenate([c_first, bc_act_ref[:, STATE:].astype(f32)[8:]], axis=0).astype(bf16)
    gated = local_ref[...] + gate_ref[...] * dot(c_rows, states)
    ahead = jnp.zeros((8, WIDTH), f32)
    for s in range(1, EDGE):
        score = jnp.sum(c_first * b_first[s : s + 1], axis=1, keepdims=True)
        ahead = ahead + jnp.where(iota((8, WIDTH), 0) < s, score * lead[s : s + 1], 0.0)
    skipped = jnp.where(iota((8, WIDTH), 0) < EDGE, gate_first_ref[...] * act, 0.0)
    gated = jnp.concatenate([gated[0:8] + (skipped - gate_ref[0:8] * ahead), gated[8:]], axis=0)

    squares = jnp.sum(gated * gated, axis=1, keepdims=True)
    scaled = (gated * gain_ref[...]).astype(bf16)
    lane = iota((BLOCK, 128), 1)
    wide = jnp.zeros((BLOCK, 128), f32)
    for block in range(LENGTH // BLOCK):
        wide = jnp.where(lane == block, squares[block * BLOCK : (block + 1) * BLOCK], wide)
    high, middle, low = (p.astype(f32) for p in parts3(wide.T[0:8]))
    extra = jnp.where(row < 3, high, jnp.where(row < 6, rolled(middle, 3, 0), 0.0))
    extra = jnp.concatenate([extra, jnp.where(row < 3, low, 0.0)], axis=0).astype(bf16)
    for pair in range(SHARES // 2):
        product = dot(scaled, weight_ref[:, 256 * pair : 256 * (pair + 1)]).astype(bf16)
        share_ref[2 * pair, 0:LENGTH] = product[:, :128]
        share_ref[2 * pair, LENGTH:] = extra
        share_ref[2 * pair + 1, 0:LENGTH] = product[:, 128:]
        share_ref[2 * pair + 1, LENGTH:] = extra


def sum_kernel(share_ref, out_ref):
    total = share_ref[0].astype(f32)
    for d in range(1, SHARES):
        total = total + share_ref[d].astype(f32)
    extra = total[LENGTH:]
    for block in range(LENGTH // BLOCK):
        rows = slice(block * BLOCK, (block + 1) * BLOCK)
        squares = extra[block : block + 1] + (extra[block + 3 : block + 4] + extra[block + 8 : block + 9])
        scale = lax.rsqrt(squares / INNER + 1e-05)
        column = jnp.broadcast_to(scale, (128, 128)).T
        out_ref[rows] = (total[rows] * column).astype(bf16)


HERE = pl.BlockSpec(memory_space=pltpu.VMEM)
THERE = pl.BlockSpec(memory_space=pltpu.HBM)


def stay(a):
    return pltpu.with_memory_space_constraint(a, pltpu.HBM)


def call(kernel, outs, *args, specs=None, scratch=(), flops=1e8, transcendentals=0):
    return pl.pallas_call(
        kernel,
        out_shape=[jax.ShapeDtypeStruct(s, d) for s, d in outs],
        in_specs=specs or [HERE] * len(args),
        out_specs=[HERE] * len(outs),
        scratch_shapes=list(scratch),
        compiler_params=pltpu.CompilerParams(vmem_limit_bytes=32 * 1024 * 1024),
        cost_estimate=pl.CostEstimate(
            flops=int(flops), bytes_accessed=2_000_000, transcendentals=int(transcendentals)
        ),
    )(*(stay(a) if spec is THERE else a for a, spec in zip(args, specs or [HERE] * len(args))))


def shards(
    inner_x, gate_z, bc_input, conv_inner, conv_bc, step_size, log_decay, skip_gain, norm_gain, out_weight
):
    message, act, bc_act, cum, first_x, first_bc, taps_x, taps_bc, step, z, gain, skip = call(
        summary_kernel,
        [
            ((HEADS, HEAD + EXTRA, 128), bf16), ((LENGTH, WIDTH), bf16), ((LENGTH, 2 * STATE), bf16),
            ((HEADS, LENGTH), f32), ((8, WIDTH), f32), ((8, 2 * STATE), f32), ((4, WIDTH), f32), ((4, 2 * STATE), f32),
            ((HEADS, LENGTH), f32), ((LENGTH, WIDTH), bf16), ((1, WIDTH), f32), ((1, WIDTH), f32),
        ],
        inner_x, bc_input, conv_inner, conv_bc, step_size, log_decay, gate_z, norm_gain[None, :], skip_gain,
        specs=[THERE] * 9,
        scratch=[
            pltpu.VMEM((LENGTH + 8, WIDTH), f32), pltpu.VMEM((LENGTH + 8, 2 * STATE), f32),
            pltpu.VMEM((LENGTH + 8, WIDTH), f32), pltpu.VMEM((LENGTH + 8, 2 * STATE), f32),
            pltpu.VMEM((LENGTH, WIDTH), bf16), pltpu.VMEM((LENGTH, 2 * STATE), bf16),
            pltpu.VMEM((HEADS, LENGTH), f32), pltpu.SMEM((HEADS,), f32),
            pltpu.SemaphoreType.DMA((9,)),
        ],
    )
    groups = [list(range(i, i + GROUP)) for i in range(0, BLOCKS, GROUP)]
    message = lax.all_to_all(message, "seq", 0, 0, tiled=True, axis_index_groups=groups)
    prefix, scale, edge, total = call(
        prefix_kernel,
        [((GROUP, HEAD, 128), f32), ((GROUP, 8, 128), f32), ((GROUP, HEAD, 128), f32), ((HEAD + EXTRA, 128), bf16)],
        message, taps_bc,
    )
    def later(a, distance, first, last):
        return lax.ppermute(a, "seq", [(i, i + distance * GROUP) for i in range(first * GROUP, (last + 1) * GROUP)])

    def permuted(a, *ways):
        return lax.ppermute(a, "seq", [(i + f * GROUP, i + t * GROUP) for f, t in ways for i in range(GROUP)])

    swapped = permuted(total, (0, 1), (1, 0))
    local, gate, lead, gate_first = call(
        within_kernel,
        [((LENGTH, WIDTH), f32), ((LENGTH, WIDTH), f32), ((8, WIDTH), f32), ((8, WIDTH), f32)],
        act, bc_act, cum, step, skip, z, total,
        flops=2e9, transcendentals=1.2e6,
    )
    joined, own = call(
        joined_kernel,
        [((HEAD + EXTRA, 128), bf16), ((HEAD + EXTRA, 128), bf16)],
        lead, total, swapped, taps_bc,
    )
    crossed, passed = permuted(joined, (1, 2), (0, 3)), permuted(own, (2, 3))
    (state,) = call(
        entering_kernel,
        [((GROUP, HEAD + EXTRA, 128), bf16)],
        message, taps_bc, prefix, scale, edge, swapped, crossed, passed,
    )
    state = lax.all_to_all(state, "seq", 0, 0, tiled=True, axis_index_groups=groups)
    (share,) = call(
        output_kernel,
        [((SHARES, LENGTH + EXTRA, 128), bf16)],
        state, bc_act, first_x, first_bc, taps_x, taps_bc, lead, gate_first, local, gate, gain, out_weight,
        flops=9e8,
    )
    share = lax.all_to_all(share, "tp", 0, 0, tiled=True)
    (mixed,) = call(sum_kernel, [((LENGTH, 128), bf16)], share)
    return mixed


def solution(mesh):
    in_specs = (
        P("seq", "tp"),
        P("seq", "tp"),
        P("seq", None),
        P(None, "tp"),
        P(),
        P("tp", "seq"),
        P("tp", "seq"),
        P("tp"),
        P("tp"),
        P("tp", None),
    )
    return jax.shard_map(shards, mesh=mesh, in_specs=in_specs, out_specs=P("seq", "tp"), check_vma=False)
```

```python
import jax
import jax.numpy as jnp
from jax import lax
from jax.experimental import pallas as pl
from jax.experimental.pallas import tpu as pltpu
from jax.sharding import PartitionSpec as P

INNER = 8192
HEADS = 8
HEAD = 64
WIDTH = HEADS * HEAD
STATE = 128
LENGTH = 384
BLOCK = 128
BLOCKS = 32
GROUP = 8
SHARES = 16
EDGE = 3
EXTRA = 16

f32 = jnp.float32
bf16 = jnp.bfloat16


def parts3(a):
    high = a.astype(bf16)
    rest = a - high.astype(f32)
    middle = rest.astype(bf16)
    low = (rest - middle.astype(f32)).astype(bf16)
    return high, middle, low


def silu(a):
    return a * jax.nn.sigmoid(a)


def dot(a, b):
    return lax.dot_general(a, b, (((1,), (0,)), ((), ())), preferred_element_type=f32)


def columns_of(rows):
    padded = jnp.concatenate([rows, jnp.zeros((128 - rows.shape[0], rows.shape[1]), f32)], axis=0)
    return padded.T


def part_columns(rows):
    return columns_of(jnp.concatenate([p.astype(f32) for p in parts3(rows)], axis=0)).astype(bf16)


def spread_heads(columns):
    part = iota((128, WIDTH), 0)
    chosen = (part < 3 * HEADS) & (part % HEADS == iota((128, WIDTH), 1) // HEAD)
    return dot(columns, jnp.where(chosen, 1.0, 0.0).astype(bf16))


def rolled(a, distance, axis):
    return pltpu.roll(a, distance % a.shape[axis], axis)


def iota(shape, axis):
    return lax.broadcasted_iota(jnp.int32, shape, axis)


def before_taps(ext, late, weights):
    here, back = ext[8 : 8 + LENGTH], ext[7 : 7 + LENGTH]
    late[8:] = weights[1:2] * here + weights[0:1] * back
    return weights[3:4] * here + weights[2:3] * back + late[6 : 6 + LENGTH]


def earlier_taps(last, taps):
    total = taps[0] * last + taps[1] * rolled(last, -1, 0) + taps[2] * rolled(last, -2, 0)
    return jnp.where(iota(last.shape, 0) < EDGE, total, 0.0)


def own_taps(first, taps):
    return taps[3] * first + taps[2] * rolled(first, 1, 0) + taps[1] * rolled(first, 2, 0)


def rounded(a):
    return a.astype(bf16).astype(f32)


def fetch(pairs, sems):
    copies = [pltpu.make_async_copy(there, here, sems.at[i]) for i, (there, here) in enumerate(pairs)]
    for copy in copies:
        copy.start()
    return copies


def summary_kernel(
    x_at, bc_at, cx_at, cbc_at, step_at, decay_at, z_at, gain_at, skip_at,
    message_ref, act_ref, bc_act_ref, cum_ref, first_x_ref, first_bc_ref, taps_x_ref, taps_bc_ref,
    step_ref, z_ref, gain_ref, skip_row_ref,
    ext_x, ext_bc, late_x, late_bc, x_ref, bc_ref, decay_ref, skip_ref, sems,
):
    copies = fetch(
        [
            (decay_at, decay_ref), (step_at, step_ref), (cx_at, taps_x_ref),
            (cbc_at, taps_bc_ref), (bc_at, bc_ref), (x_at, x_ref),
            (z_at, z_ref), (gain_at, gain_ref), (skip_at, skip_ref),
        ],
        sems,
    )
    copies[0].wait()
    copies[1].wait()
    upto = jnp.where(iota((LENGTH, LENGTH), 0) <= iota((LENGTH, LENGTH), 1), 1.0, 0.0).astype(bf16)
    sums = dot(jnp.concatenate([p.astype(f32) for p in parts3(decay_ref[...])], axis=0).astype(bf16), upto)
    cum = sums[0:8] + (sums[8:16] + sums[16:24])
    cum_ref[...] = cum
    last = cum[:, LENGTH - 1 : LENGTH]
    factor = step_ref[...] * jnp.exp(last - cum)
    inside = jnp.where(iota((HEADS, LENGTH), 1) < EDGE, 0.0, factor)
    factor_spread = spread_heads(part_columns(inside))
    for copy in copies[2:6]:
        copy.wait()
    ext_x[0:8] = jnp.zeros((8, WIDTH), f32)
    ext_bc[0:8] = jnp.zeros((8, 2 * STATE), f32)
    ext_x[8:] = x_ref[...].astype(f32)
    ext_bc[8:] = bc_ref[...].astype(f32)
    late_bc[0:8] = jnp.zeros((8, 2 * STATE), f32)
    late_x[0:8] = jnp.zeros((8, WIDTH), f32)
    sums = before_taps(ext_bc, late_bc, taps_bc_ref)
    first_bc_ref[...] = sums[0:8]
    bc_act = silu(sums).astype(bf16)
    bc_act_ref[...] = bc_act
    sums = before_taps(ext_x, late_x, taps_x_ref)
    first_x_ref[...] = sums[0:8]
    act = silu(sums).astype(bf16)
    act_ref[...] = act

    weighted = (act.astype(f32) * factor_spread).astype(bf16)
    b_rows = bc_act[:, :STATE].astype(f32)
    summary = dot(b_rows.T.astype(bf16), weighted)

    total = jnp.broadcast_to(jnp.exp(last), (HEADS, 128))
    lane = iota((HEADS, 128), 1)
    lead = step_ref[:, :128] * jnp.exp(jnp.where(lane < EDGE, -cum[:, :128], 0.0))
    scalars = jnp.where(lane < HEAD, lead, total)
    high, middle, _ = (p.astype(f32) for p in parts3(scalars))
    tap_high, tap_middle, _ = (p.astype(f32) for p in parts3(taps_x_ref[...]))
    low_lanes = iota((HEAD, 128), 1) < HEAD
    few = iota((8, 128), 1) < HEAD
    row = iota((8, 128), 0)
    b_first = rolled(ext_bc[8:16, :STATE], 3, 0)
    bc_last = rolled(ext_bc[LENGTH : LENGTH + 8], 3, 0)
    for h in range(HEADS):
        lanes = slice(128 * (h // 2), 128 * (h // 2 + 1))
        even = h % 2 == 0

        def side_by_side(left, right, where):
            if even:
                return jnp.where(where, left, rolled(right, HEAD, 1))
            return jnp.where(where, rolled(left, HEAD, 1), right)

        message_ref[h, 0:HEAD] = side_by_side(summary[:HEAD, lanes], summary[HEAD:, lanes], low_lanes).astype(bf16)
        x_edges = side_by_side(ext_x[8:16, lanes], rolled(ext_x[LENGTH : LENGTH + 8, lanes], 3, 0), few)
        tile = jnp.where(row < 3, x_edges, b_first)
        tile = jnp.where(row == 6, high[h : h + 1], jnp.where(row == 7, middle[h : h + 1], tile))
        other = bc_last[:, :STATE]
        for at, (part, k) in enumerate(((tap_high, 0), (tap_high, 2), (tap_middle, 0), (tap_middle, 2))):
            pair = side_by_side(part[k : k + 1, lanes], part[k + 1 : k + 2, lanes], few[0:1])
            other = jnp.where(row == 3 + at, pair, other)
        c_row = bc_last[h : h + 1, STATE:] if h < EDGE else jnp.zeros((1, STATE), f32)
        other = jnp.where(row == 7, c_row, other)
        message_ref[h, HEAD:] = jnp.concatenate([tile, other], axis=0).astype(bf16)

    for copy in copies[6:]:
        copy.wait()
    head_at = iota((1, WIDTH), 1) // HEAD
    skip = jnp.zeros((1, WIDTH), f32)
    for h in range(HEADS):
        skip = jnp.where(head_at == h, skip_ref[h], skip)
    skip_row_ref[...] = skip


def within_kernel(
    act_ref, bc_act_ref, cum_ref, step_ref, skip_row_ref, z_ref, after_ref,
    local_ref, gate_ref, lead_ref, gate_first_ref,
):
    skip = skip_row_ref[...]
    cum = cum_ref[...]
    cum_columns = columns_of(cum)
    act = act_ref[...].astype(f32)
    step = step_ref[...]
    inside = jnp.where(iota((HEADS, LENGTH), 1) < EDGE, 0.0, step)
    scaled = (act * spread_heads(part_columns(inside))).astype(bf16)
    early = iota((HEADS, 128), 1) < 8
    lead = jnp.where(early, step[:, :128] * jnp.exp(jnp.where(early, -cum[:, :128], 0.0)), 0.0)
    lead_ref[...] = spread_heads(part_columns(lead)[0:16])[0:8]
    cum_spread = spread_heads(part_columns(jnp.exp(cum)))
    gate = silu(z_ref[...].astype(f32))
    gate_first_ref[...] = gate[0:8] * skip
    gate_ref[...] = gate * cum_spread
    b_rows = bc_act_ref[:, :STATE]
    c_rows = bc_act_ref[:, STATE:]
    skipped = jnp.where(iota((LENGTH, WIDTH), 0) < EDGE, 0.0, skip * act)
    t_at = lax.broadcasted_iota(jnp.int32, (BLOCK, BLOCK), 0)
    s_at = lax.broadcasted_iota(jnp.int32, (BLOCK, BLOCK), 1)
    causal = t_at >= s_at
    low_lanes = lax.broadcasted_iota(jnp.int32, (BLOCK, 128), 1) < HEAD
    for block in range(LENGTH // BLOCK):
        rows = slice(block * BLOCK, (block + 1) * BLOCK)
        scores = lax.dot_general(
            c_rows[rows], b_rows[: (block + 1) * BLOCK], (((1,), (1,)), ((), ())), preferred_element_type=f32
        )
        for pair in range(HEADS // 2):
            lanes = slice(128 * pair, 128 * (pair + 1))
            mixing = []
            for h in (2 * pair, 2 * pair + 1):
                here = cum_columns[rows, h : h + 1]
                tiles = []
                for other in range(block + 1):
                    columns = slice(other * BLOCK, (other + 1) * BLOCK)
                    spread = here - cum[h : h + 1, columns]
                    if other == block:
                        spread = jnp.where(causal, spread, -jnp.inf)
                    tiles.append((scores[:, columns] * jnp.exp(spread)).astype(bf16))
                mixing.append(tiles[0] if block == 0 else jnp.concatenate(tiles, axis=1))
            sums = dot(jnp.concatenate(mixing, axis=0), scaled[: (block + 1) * BLOCK, lanes])
            within = jnp.where(low_lanes, sums[:BLOCK], sums[BLOCK:])
            local_ref[rows, lanes] = (within + skipped[rows, lanes]) * gate[rows, lanes]


def all_lanes(row):
    return jnp.where(iota((1, 128), 1) < HEAD, rolled(row, HEAD, 1), row)


def taps_of(tile):
    pairs = tile[3:5] + tile[5:7]
    return [pairs[0:1], rolled(pairs[0:1], HEAD, 1), pairs[1:2], rolled(pairs[1:2], HEAD, 1)]


def edge_rows(tile, before, before_last, scalars, taps_x, taps_b):
    row = iota((8, 128), 0)
    lane = iota((8, 128), 1)
    sums = own_taps(jnp.where(row < EDGE, tile, 0.0), taps_x)
    sums_b = own_taps(jnp.where(row < EDGE, rolled(tile, -EDGE, 0), 0.0), taps_b)
    if before is not None:
        sums = sums + earlier_taps(jnp.where(row < EDGE, rolled(before, HEAD, 1), 0.0), taps_x)
        sums_b = sums_b + earlier_taps(jnp.where(row < EDGE, before_last, 0.0), taps_b)
    factor = jnp.sum(jnp.where(lane == row, scalars, 0.0), axis=1, keepdims=True)
    weighted = rounded(silu(sums)) * factor
    weighted = jnp.where((row < EDGE) & (lane < HEAD), weighted, 0.0)
    return weighted, jnp.where(row < EDGE, rounded(silu(sums_b)), 0.0)


def edge_states(entries):
    zeros = jnp.zeros((HEAD - 8 * len(entries), 128), f32)
    pad = [zeros] if zeros.shape[0] else []
    weighted = jnp.concatenate([e[0] for e in entries] + pad, axis=0)
    weighted = jnp.concatenate([weighted, rolled(weighted, HEAD, 1)], axis=0)
    b_rows = jnp.concatenate([e[1] for e in entries] + pad + [jnp.zeros((HEAD, 128), f32)], axis=0).T
    left = jnp.where(iota((HEAD, 128), 1) < HEAD, b_rows[:HEAD], rolled(b_rows[HEAD:], HEAD, 1)).astype(bf16)
    owner = (iota((128, 128), 0) % HEAD) // 8
    return [dot(left, jnp.where(owner == e, weighted, 0.0).astype(bf16)) for e in range(len(entries))]


def prefix_kernel(message_ref, taps_ref, prefix_ref, scale_ref, edge_ref, total_ref):
    tiles = [message_ref[m, HEAD:].astype(f32) for m in range(GROUP)]
    scalars = [t[6:7] + t[7:8] for t in tiles]
    decays = [all_lanes(s) for s in scalars]
    taps_x = taps_of(tiles[0][8:])
    taps_b = [taps_ref[k : k + 1, :STATE] for k in range(4)]
    entries = [
        edge_rows(tiles[m][:8], tiles[m - 1][:8], tiles[m - 1][8:], scalars[m], taps_x, taps_b) for m in range(1, GROUP)
    ]
    edges = edge_states(entries)
    state = message_ref[0, 0:HEAD].astype(f32)
    scale = jnp.ones((1, 128), f32)
    for m in range(1, GROUP):
        prefix_ref[m] = state
        scale_ref[m] = jnp.broadcast_to(scale, (8, 128))
        edge_ref[m] = edges[m - 1]
        state = decays[m] * (state + edges[m - 1]) + message_ref[m, 0:HEAD].astype(f32)
        scale = decays[m] * scale
    total_ref[0:HEAD] = state.astype(bf16)
    lane = iota((1, 128), 1)
    high, middle, _ = (p.astype(f32) for p in parts3(jnp.where(lane < HEAD, scalars[0], decays[0] * scale)))
    row = iota((8, 128), 0)
    first, last = tiles[0][:8], tiles[GROUP - 1]
    tile = jnp.where((row < EDGE) & (iota((8, 128), 1) >= HEAD), last[:8], first)
    tile = jnp.where(row == 6, high, jnp.where(row == 7, middle, tile))
    total_ref[HEAD:] = jnp.concatenate([tile, last[8:]], axis=0).astype(bf16)


def joined_kernel(lead_ref, total_ref, swapped_ref, taps_ref, joined_ref, own_ref):
    zeroth = lax.axis_index("seq") // GROUP == 0
    total, swapped = total_ref[...].astype(f32), swapped_ref[...].astype(f32)
    first, second = jnp.where(zeroth, total, swapped), jnp.where(zeroth, swapped, total)
    taps_x = taps_of(total[HEAD + 8 :])
    taps_b = [taps_ref[k : k + 1, :STATE] for k in range(4)]
    tiles = [first[HEAD:], second[HEAD:]]
    scalars = [t[6:7] + t[7:8] for t in tiles]
    edges = edge_states(
        [
            edge_rows(tiles[0][:8], None, None, scalars[0], taps_x, taps_b),
            edge_rows(tiles[1][:8], tiles[0][:8], tiles[0][8:], scalars[1], taps_x, taps_b),
        ]
    )
    state = all_lanes(scalars[0]) * edges[0] + first[:HEAD]
    state = all_lanes(scalars[1]) * (state + edges[1]) + second[:HEAD]
    joined_ref[0:HEAD] = state.astype(bf16)
    joined_ref[HEAD:] = tiles[1].astype(bf16)
    own_ref[...] = total_ref[...]


def entered(message_ref, taps_ref, near, crossed, third):
    own = message_ref[0, HEAD:].astype(f32)
    before = near[HEAD:] if third is None else jnp.where(third, crossed[HEAD:], near[HEAD:])
    taps_x = taps_of(own[8:])
    taps_b = [taps_ref[k : k + 1, :STATE] for k in range(4)]
    scalars = [t[6:7] + t[7:8] for t in (near[HEAD:], own)]
    edge, last = (None, None) if crossed is None else (crossed[HEAD : HEAD + 8], crossed[HEAD + 8 :])
    edges = edge_states(
        [
            edge_rows(near[HEAD : HEAD + 8], edge, last, scalars[0], taps_x, taps_b),
            edge_rows(own[:8], before[:8], before[8:], scalars[1], taps_x, taps_b),
        ]
    )
    if crossed is None:
        entering = all_lanes(scalars[0]) * edges[0] + near[:HEAD]
    else:
        entering = all_lanes(scalars[0]) * (crossed[:HEAD] + edges[0]) + near[:HEAD]
        entering = jnp.where(third, crossed[:HEAD], entering)
    return jnp.concatenate([entering + edges[1], before], axis=0)


def early_kernel(own_ref, message_ref, taps_ref, swapped_ref, early_ref):
    second = lax.axis_index("seq") // GROUP == 1
    near = jnp.where(second, swapped_ref[...].astype(f32), 0.0)
    early_ref[...] = entered(message_ref, taps_ref, near, None, None)


def entering_kernel(
    message_ref, taps_ref, prefix_ref, scale_ref, edge_ref, early_ref, crossed_ref, passed_ref, state_ref, entered_ref
):
    group = lax.axis_index("seq") // GROUP

    @pl.when(group < 2)
    def _():
        entered_ref[...] = early_ref[...]

    @pl.when(group >= 2)
    def _():
        crossed, near = crossed_ref[...].astype(f32), passed_ref[...].astype(f32)
        entered_ref[...] = entered(message_ref, taps_ref, near, crossed, group == 2)

    own = message_ref[0, HEAD:].astype(f32)
    entering = entered_ref[0:HEAD]
    state_ref[0, 0:HEAD] = entering.astype(bf16)
    state_ref[0, HEAD:] = entered_ref[HEAD:].astype(bf16)
    after_first = all_lanes(own[6:7] + own[7:8]) * entering
    for m in range(1, GROUP):
        state = prefix_ref[m] + scale_ref[m, 0:1] * after_first + edge_ref[m]
        state_ref[m, 0:HEAD] = state.astype(bf16)
        state_ref[m, HEAD:] = message_ref[m - 1, HEAD:]


def output_kernel(
    state_ref, bc_act_ref, first_x_ref, first_bc_ref, taps_x_ref, taps_bc_ref, lead_ref, gate_first_ref,
    local_ref, gate_ref, gain_ref, weight_ref, share_ref,
):
    row = iota((8, 128), 0)
    few = iota((8, 128), 1) < HEAD
    low_lanes = iota((HEAD, 128), 1) < HEAD
    tiles = [state_ref[h, HEAD:].astype(f32) for h in range(HEADS)]

    last_x = jnp.concatenate(
        [jnp.where(few, rolled(tiles[h][:8], HEAD, 1), tiles[h + 1][:8]) for h in range(0, HEADS, 2)], axis=1
    )
    last_c = jnp.zeros((8, 128), f32)
    for h in range(EDGE):
        last_c = jnp.where(row == h, tiles[h][15:16], last_c)
    last_bc = jnp.concatenate([tiles[0][8:], last_c], axis=1)
    last_x = jnp.where(iota((8, WIDTH), 0) < EDGE, last_x, 0.0)
    last_bc = jnp.where(iota((8, 2 * STATE), 0) < EDGE, last_bc, 0.0)
    taps_x = [taps_x_ref[k : k + 1] for k in range(4)]
    taps_bc = [taps_bc_ref[k : k + 1] for k in range(4)]
    act = rounded(silu(first_x_ref[...] + earlier_taps(last_x, taps_x)))
    bc_act = rounded(silu(first_bc_ref[...] + earlier_taps(last_bc, taps_bc)))
    b_first, c_first = bc_act[:, :STATE], bc_act[:, STATE:]
    lead = rounded(jnp.where(iota((8, WIDTH), 0) < EDGE, act * lead_ref[...], 0.0))

    pairs = []
    for pair in range(HEADS // 2):
        even = state_ref[2 * pair, 0:HEAD].astype(f32)
        odd = state_ref[2 * pair + 1, 0:HEAD].astype(f32)
        top = jnp.where(low_lanes, even, rolled(odd, HEAD, 1))
        bottom = jnp.where(low_lanes, rolled(even, HEAD, 1), odd)
        pairs.append(jnp.concatenate([top, bottom], axis=0))
    states = jnp.concatenate(pairs, axis=1)
    states = states.astype(bf16)
    c_rows = jnp.concatenate([c_first, bc_act_ref[:, STATE:].astype(f32)[8:]], axis=0).astype(bf16)
    gated = local_ref[...] + gate_ref[...] * dot(c_rows, states)
    ahead = jnp.zeros((8, WIDTH), f32)
    for s in range(1, EDGE):
        score = jnp.sum(c_first * b_first[s : s + 1], axis=1, keepdims=True)
        ahead = ahead + jnp.where(iota((8, WIDTH), 0) < s, score * lead[s : s + 1], 0.0)
    skipped = jnp.where(iota((8, WIDTH), 0) < EDGE, gate_first_ref[...] * act, 0.0)
    gated = jnp.concatenate([gated[0:8] + (skipped - gate_ref[0:8] * ahead), gated[8:]], axis=0)

    squares = jnp.sum(gated * gated, axis=1, keepdims=True)
    scaled = (gated * gain_ref[...]).astype(bf16)
    lane = iota((BLOCK, 128), 1)
    wide = jnp.zeros((BLOCK, 128), f32)
    for block in range(LENGTH // BLOCK):
        wide = jnp.where(lane == block, squares[block * BLOCK : (block + 1) * BLOCK], wide)
    high, middle, low = (p.astype(f32) for p in parts3(wide.T[0:8]))
    extra = jnp.where(row < 3, high, jnp.where(row < 6, rolled(middle, 3, 0), 0.0))
    extra = jnp.concatenate([extra, jnp.where(row < 3, low, 0.0)], axis=0).astype(bf16)
    for pair in range(SHARES // 2):
        product = dot(scaled, weight_ref[:, 256 * pair : 256 * (pair + 1)]).astype(bf16)
        share_ref[2 * pair, 0:LENGTH] = product[:, :128]
        share_ref[2 * pair, LENGTH:] = extra
        share_ref[2 * pair + 1, 0:LENGTH] = product[:, 128:]
        share_ref[2 * pair + 1, LENGTH:] = extra


def sum_kernel(share_ref, out_ref):
    total = share_ref[0].astype(f32)
    for d in range(1, SHARES):
        total = total + share_ref[d].astype(f32)
    extra = total[LENGTH:]
    for block in range(LENGTH // BLOCK):
        rows = slice(block * BLOCK, (block + 1) * BLOCK)
        squares = extra[block : block + 1] + (extra[block + 3 : block + 4] + extra[block + 8 : block + 9])
        scale = lax.rsqrt(squares / INNER + 1e-05)
        column = jnp.broadcast_to(scale, (128, 128)).T
        out_ref[rows] = (total[rows] * column).astype(bf16)


HERE = pl.BlockSpec(memory_space=pltpu.VMEM)
THERE = pl.BlockSpec(memory_space=pltpu.HBM)


def stay(a):
    return pltpu.with_memory_space_constraint(a, pltpu.HBM)


def call(kernel, outs, *args, specs=None, scratch=(), flops=1e8, transcendentals=0):
    return pl.pallas_call(
        kernel,
        out_shape=[jax.ShapeDtypeStruct(s, d) for s, d in outs],
        in_specs=specs or [HERE] * len(args),
        out_specs=[HERE] * len(outs),
        scratch_shapes=list(scratch),
        compiler_params=pltpu.CompilerParams(vmem_limit_bytes=32 * 1024 * 1024),
        cost_estimate=pl.CostEstimate(
            flops=int(flops), bytes_accessed=2_000_000, transcendentals=int(transcendentals)
        ),
    )(*(stay(a) if spec is THERE else a for a, spec in zip(args, specs or [HERE] * len(args))))


def shards(
    inner_x, gate_z, bc_input, conv_inner, conv_bc, step_size, log_decay, skip_gain, norm_gain, out_weight
):
    message, act, bc_act, cum, first_x, first_bc, taps_x, taps_bc, step, z, gain, skip = call(
        summary_kernel,
        [
            ((HEADS, HEAD + EXTRA, 128), bf16), ((LENGTH, WIDTH), bf16), ((LENGTH, 2 * STATE), bf16),
            ((HEADS, LENGTH), f32), ((8, WIDTH), f32), ((8, 2 * STATE), f32), ((4, WIDTH), f32), ((4, 2 * STATE), f32),
            ((HEADS, LENGTH), f32), ((LENGTH, WIDTH), bf16), ((1, WIDTH), f32), ((1, WIDTH), f32),
        ],
        inner_x, bc_input, conv_inner, conv_bc, step_size, log_decay, gate_z, norm_gain[None, :], skip_gain,
        specs=[THERE] * 9,
        scratch=[
            pltpu.VMEM((LENGTH + 8, WIDTH), f32), pltpu.VMEM((LENGTH + 8, 2 * STATE), f32),
            pltpu.VMEM((LENGTH + 8, WIDTH), f32), pltpu.VMEM((LENGTH + 8, 2 * STATE), f32),
            pltpu.VMEM((LENGTH, WIDTH), bf16), pltpu.VMEM((LENGTH, 2 * STATE), bf16),
            pltpu.VMEM((HEADS, LENGTH), f32), pltpu.SMEM((HEADS,), f32),
            pltpu.SemaphoreType.DMA((9,)),
        ],
    )
    groups = [list(range(i, i + GROUP)) for i in range(0, BLOCKS, GROUP)]
    message = lax.all_to_all(message, "seq", 0, 0, tiled=True, axis_index_groups=groups)
    prefix, scale, edge, total = call(
        prefix_kernel,
        [((GROUP, HEAD, 128), f32), ((GROUP, 8, 128), f32), ((GROUP, HEAD, 128), f32), ((HEAD + EXTRA, 128), bf16)],
        message, taps_bc,
    )
    def later(a, distance, first, last):
        return lax.ppermute(a, "seq", [(i, i + distance * GROUP) for i in range(first * GROUP, (last + 1) * GROUP)])

    def permuted(a, *ways):
        return lax.ppermute(a, "seq", [(i + f * GROUP, i + t * GROUP) for f, t in ways for i in range(GROUP)])

    swapped = permuted(total, (0, 1), (1, 0))
    local, gate, lead, gate_first = call(
        within_kernel,
        [((LENGTH, WIDTH), f32), ((LENGTH, WIDTH), f32), ((8, WIDTH), f32), ((8, WIDTH), f32)],
        act, bc_act, cum, step, skip, z, total,
        flops=2e9, transcendentals=1.2e6,
    )
    joined, own = call(
        joined_kernel,
        [((HEAD + EXTRA, 128), bf16), ((HEAD + EXTRA, 128), bf16)],
        lead, total, swapped, taps_bc,
    )
    crossed, passed = permuted(joined, (1, 2), (0, 3)), permuted(own, (2, 3))
    (early,) = call(early_kernel, [((HEAD + EXTRA, 128), f32)], own, message, taps_bc, swapped)
    (state,) = call(
        entering_kernel,
        [((GROUP, HEAD + EXTRA, 128), bf16)],
        message, taps_bc, prefix, scale, edge, early, crossed, passed,
        scratch=[pltpu.VMEM((HEAD + EXTRA, 128), f32)],
    )
    state = lax.all_to_all(state, "seq", 0, 0, tiled=True, axis_index_groups=groups)
    (share,) = call(
        output_kernel,
        [((SHARES, LENGTH + EXTRA, 128), bf16)],
        state, bc_act, first_x, first_bc, taps_x, taps_bc, lead, gate_first, local, gate, gain, out_weight,
        flops=9e8,
    )
    share = lax.all_to_all(share, "tp", 0, 0, tiled=True)
    (mixed,) = call(sum_kernel, [((LENGTH, 128), bf16)], share)
    return mixed


def solution(mesh):
    in_specs = (
        P("seq", "tp"),
        P("seq", "tp"),
        P("seq", None),
        P(None, "tp"),
        P(),
        P("tp", "seq"),
        P("tp", "seq"),
        P("tp"),
        P("tp"),
        P("tp", None),
    )
    return jax.shard_map(shards, mesh=mesh, in_specs=in_specs, out_specs=P("seq", "tp"), check_vma=False)
```

```python
import jax
import jax.numpy as jnp
from jax import lax
from jax.experimental import pallas as pl
from jax.experimental.pallas import tpu as pltpu
from jax.sharding import PartitionSpec as P

INNER = 8192
HEADS = 8
HEAD = 64
WIDTH = HEADS * HEAD
STATE = 128
LENGTH = 384
BLOCK = 128
BLOCKS = 32
GROUP = 8
SHARES = 16
EDGE = 3
EXTRA = 16

f32 = jnp.float32
bf16 = jnp.bfloat16


def parts3(a):
    high = a.astype(bf16)
    rest = a - high.astype(f32)
    middle = rest.astype(bf16)
    low = (rest - middle.astype(f32)).astype(bf16)
    return high, middle, low


def silu(a):
    return a * jax.nn.sigmoid(a)


def dot(a, b):
    return lax.dot_general(a, b, (((1,), (0,)), ((), ())), preferred_element_type=f32)


def columns_of(rows):
    padded = jnp.concatenate([rows, jnp.zeros((128 - rows.shape[0], rows.shape[1]), f32)], axis=0)
    return padded.T


def part_columns(rows):
    return columns_of(jnp.concatenate([p.astype(f32) for p in parts3(rows)], axis=0)).astype(bf16)


def spread_heads(columns):
    part = iota((128, WIDTH), 0)
    chosen = (part < 3 * HEADS) & (part % HEADS == iota((128, WIDTH), 1) // HEAD)
    return dot(columns, jnp.where(chosen, 1.0, 0.0).astype(bf16))


def rolled(a, distance, axis):
    return pltpu.roll(a, distance % a.shape[axis], axis)


def iota(shape, axis):
    return lax.broadcasted_iota(jnp.int32, shape, axis)


def before_taps(ext, late, weights):
    here, back = ext[8 : 8 + LENGTH], ext[7 : 7 + LENGTH]
    late[8:] = weights[1:2] * here + weights[0:1] * back
    return weights[3:4] * here + weights[2:3] * back + late[6 : 6 + LENGTH]


def earlier_taps(last, taps):
    total = taps[0] * last + taps[1] * rolled(last, -1, 0) + taps[2] * rolled(last, -2, 0)
    return jnp.where(iota(last.shape, 0) < EDGE, total, 0.0)


def own_taps(first, taps):
    return taps[3] * first + taps[2] * rolled(first, 1, 0) + taps[1] * rolled(first, 2, 0)


def rounded(a):
    return a.astype(bf16).astype(f32)


def fetch(pairs, sems):
    copies = [pltpu.make_async_copy(there, here, sems.at[i]) for i, (there, here) in enumerate(pairs)]
    for copy in copies:
        copy.start()
    return copies


def summary_kernel(
    x_at, bc_at, cx_at, cbc_at, step_at, decay_at, z_at, gain_at, skip_at,
    message_ref, act_ref, bc_act_ref, cum_ref, first_x_ref, first_bc_ref, taps_x_ref, taps_bc_ref,
    step_ref, z_ref, gain_ref, skip_row_ref,
    ext_x, ext_bc, late_x, late_bc, x_ref, bc_ref, decay_ref, skip_ref, sems,
):
    copies = fetch(
        [
            (decay_at, decay_ref), (step_at, step_ref), (cx_at, taps_x_ref),
            (cbc_at, taps_bc_ref), (bc_at, bc_ref), (x_at, x_ref),
            (z_at, z_ref), (gain_at, gain_ref), (skip_at, skip_ref),
        ],
        sems,
    )
    copies[0].wait()
    copies[1].wait()
    upto = jnp.where(iota((LENGTH, LENGTH), 0) <= iota((LENGTH, LENGTH), 1), 1.0, 0.0).astype(bf16)
    sums = dot(jnp.concatenate([p.astype(f32) for p in parts3(decay_ref[...])], axis=0).astype(bf16), upto)
    cum = sums[0:8] + (sums[8:16] + sums[16:24])
    cum_ref[...] = cum
    last = cum[:, LENGTH - 1 : LENGTH]
    factor = step_ref[...] * jnp.exp(last - cum)
    inside = jnp.where(iota((HEADS, LENGTH), 1) < EDGE, 0.0, factor)
    factor_spread = spread_heads(part_columns(inside))
    for copy in copies[2:6]:
        copy.wait()
    ext_x[0:8] = jnp.zeros((8, WIDTH), f32)
    ext_bc[0:8] = jnp.zeros((8, 2 * STATE), f32)
    ext_x[8:] = x_ref[...].astype(f32)
    ext_bc[8:] = bc_ref[...].astype(f32)
    late_bc[0:8] = jnp.zeros((8, 2 * STATE), f32)
    late_x[0:8] = jnp.zeros((8, WIDTH), f32)
    sums = before_taps(ext_bc, late_bc, taps_bc_ref)
    first_bc_ref[...] = sums[0:8]
    bc_act = silu(sums).astype(bf16)
    bc_act_ref[...] = bc_act
    sums = before_taps(ext_x, late_x, taps_x_ref)
    first_x_ref[...] = sums[0:8]
    act = silu(sums).astype(bf16)
    act_ref[...] = act

    weighted = (act.astype(f32) * factor_spread).astype(bf16)
    b_rows = bc_act[:, :STATE].astype(f32)
    summary = dot(b_rows.T.astype(bf16), weighted)

    total = jnp.broadcast_to(jnp.exp(last), (HEADS, 128))
    lane = iota((HEADS, 128), 1)
    lead = step_ref[:, :128] * jnp.exp(jnp.where(lane < EDGE, -cum[:, :128], 0.0))
    scalars = jnp.where(lane < HEAD, lead, total)
    high, middle, _ = (p.astype(f32) for p in parts3(scalars))
    tap_high, tap_middle, _ = (p.astype(f32) for p in parts3(taps_x_ref[...]))
    low_lanes = iota((HEAD, 128), 1) < HEAD
    few = iota((8, 128), 1) < HEAD
    row = iota((8, 128), 0)
    b_first = rolled(ext_bc[8:16, :STATE], 3, 0)
    bc_last = rolled(ext_bc[LENGTH : LENGTH + 8], 3, 0)
    for h in range(HEADS):
        lanes = slice(128 * (h // 2), 128 * (h // 2 + 1))
        even = h % 2 == 0

        def side_by_side(left, right, where):
            if even:
                return jnp.where(where, left, rolled(right, HEAD, 1))
            return jnp.where(where, rolled(left, HEAD, 1), right)

        message_ref[h, 0:HEAD] = side_by_side(summary[:HEAD, lanes], summary[HEAD:, lanes], low_lanes).astype(bf16)
        x_edges = side_by_side(ext_x[8:16, lanes], rolled(ext_x[LENGTH : LENGTH + 8, lanes], 3, 0), few)
        tile = jnp.where(row < 3, x_edges, b_first)
        tile = jnp.where(row == 6, high[h : h + 1], jnp.where(row == 7, middle[h : h + 1], tile))
        other = bc_last[:, :STATE]
        for at, (part, k) in enumerate(((tap_high, 0), (tap_high, 2), (tap_middle, 0), (tap_middle, 2))):
            pair = side_by_side(part[k : k + 1, lanes], part[k + 1 : k + 2, lanes], few[0:1])
            other = jnp.where(row == 3 + at, pair, other)
        c_row = bc_last[h : h + 1, STATE:] if h < EDGE else jnp.zeros((1, STATE), f32)
        other = jnp.where(row == 7, c_row, other)
        message_ref[h, HEAD:] = jnp.concatenate([tile, other], axis=0).astype(bf16)

    for copy in copies[6:]:
        copy.wait()
    head_at = iota((1, WIDTH), 1) // HEAD
    skip = jnp.zeros((1, WIDTH), f32)
    for h in range(HEADS):
        skip = jnp.where(head_at == h, skip_ref[h], skip)
    skip_row_ref[...] = skip


def within_kernel(
    act_ref, bc_act_ref, cum_ref, step_ref, skip_row_ref, z_ref, after_ref,
    local_ref, gate_ref, lead_ref, gate_first_ref,
):
    skip = skip_row_ref[...]
    cum = cum_ref[...]
    cum_columns = columns_of(cum)
    act = act_ref[...].astype(f32)
    step = step_ref[...]
    inside = jnp.where(iota((HEADS, LENGTH), 1) < EDGE, 0.0, step)
    scaled = (act * spread_heads(part_columns(inside))).astype(bf16)
    early = iota((HEADS, 128), 1) < 8
    lead = jnp.where(early, step[:, :128] * jnp.exp(jnp.where(early, -cum[:, :128], 0.0)), 0.0)
    lead_ref[...] = spread_heads(part_columns(lead)[0:16])[0:8]
    cum_spread = spread_heads(part_columns(jnp.exp(cum)))
    gate = silu(z_ref[...].astype(f32))
    gate_first_ref[...] = gate[0:8] * skip
    gate_ref[...] = gate * cum_spread
    b_rows = bc_act_ref[:, :STATE]
    c_rows = bc_act_ref[:, STATE:]
    skipped = jnp.where(iota((LENGTH, WIDTH), 0) < EDGE, 0.0, skip * act)
    t_at = lax.broadcasted_iota(jnp.int32, (BLOCK, BLOCK), 0)
    s_at = lax.broadcasted_iota(jnp.int32, (BLOCK, BLOCK), 1)
    causal = t_at >= s_at
    low_lanes = lax.broadcasted_iota(jnp.int32, (BLOCK, 128), 1) < HEAD
    for block in range(LENGTH // BLOCK):
        rows = slice(block * BLOCK, (block + 1) * BLOCK)
        scores = lax.dot_general(
            c_rows[rows], b_rows[: (block + 1) * BLOCK], (((1,), (1,)), ((), ())), preferred_element_type=f32
        )
        for pair in range(HEADS // 2):
            lanes = slice(128 * pair, 128 * (pair + 1))
            mixing = []
            for h in (2 * pair, 2 * pair + 1):
                here = cum_columns[rows, h : h + 1]
                tiles = []
                for other in range(block + 1):
                    columns = slice(other * BLOCK, (other + 1) * BLOCK)
                    spread = here - cum[h : h + 1, columns]
                    if other == block:
                        spread = jnp.where(causal, spread, -jnp.inf)
                    tiles.append((scores[:, columns] * jnp.exp(spread)).astype(bf16))
                mixing.append(tiles[0] if block == 0 else jnp.concatenate(tiles, axis=1))
            sums = dot(jnp.concatenate(mixing, axis=0), scaled[: (block + 1) * BLOCK, lanes])
            within = jnp.where(low_lanes, sums[:BLOCK], sums[BLOCK:])
            local_ref[rows, lanes] = (within + skipped[rows, lanes]) * gate[rows, lanes]


def all_lanes(row):
    return jnp.where(iota((1, 128), 1) < HEAD, rolled(row, HEAD, 1), row)


def taps_of(tile):
    pairs = tile[3:5] + tile[5:7]
    return [pairs[0:1], rolled(pairs[0:1], HEAD, 1), pairs[1:2], rolled(pairs[1:2], HEAD, 1)]


def edge_rows(tile, before, before_last, scalars, taps_x, taps_b):
    row = iota((8, 128), 0)
    lane = iota((8, 128), 1)
    sums = own_taps(jnp.where(row < EDGE, tile, 0.0), taps_x)
    sums_b = own_taps(jnp.where(row < EDGE, rolled(tile, -EDGE, 0), 0.0), taps_b)
    if before is not None:
        sums = sums + earlier_taps(jnp.where(row < EDGE, rolled(before, HEAD, 1), 0.0), taps_x)
        sums_b = sums_b + earlier_taps(jnp.where(row < EDGE, before_last, 0.0), taps_b)
    factor = jnp.sum(jnp.where(lane == row, scalars, 0.0), axis=1, keepdims=True)
    weighted = rounded(silu(sums)) * factor
    weighted = jnp.where((row < EDGE) & (lane < HEAD), weighted, 0.0)
    return weighted, jnp.where(row < EDGE, rounded(silu(sums_b)), 0.0)


def edge_states(entries):
    zeros = jnp.zeros((HEAD - 8 * len(entries), 128), f32)
    pad = [zeros] if zeros.shape[0] else []
    weighted = jnp.concatenate([e[0] for e in entries] + pad, axis=0)
    weighted = jnp.concatenate([weighted, rolled(weighted, HEAD, 1)], axis=0)
    b_rows = jnp.concatenate([e[1] for e in entries] + pad + [jnp.zeros((HEAD, 128), f32)], axis=0).T
    left = jnp.where(iota((HEAD, 128), 1) < HEAD, b_rows[:HEAD], rolled(b_rows[HEAD:], HEAD, 1)).astype(bf16)
    owner = (iota((128, 128), 0) % HEAD) // 8
    return [dot(left, jnp.where(owner == e, weighted, 0.0).astype(bf16)) for e in range(len(entries))]


def prefix_kernel(message_ref, taps_ref, prefix_ref, scale_ref, edge_ref, total_ref):
    tiles = [message_ref[m, HEAD:].astype(f32) for m in range(GROUP)]
    scalars = [t[6:7] + t[7:8] for t in tiles]
    decays = [all_lanes(s) for s in scalars]
    taps_x = taps_of(tiles[0][8:])
    taps_b = [taps_ref[k : k + 1, :STATE] for k in range(4)]
    entries = [
        edge_rows(tiles[m][:8], tiles[m - 1][:8], tiles[m - 1][8:], scalars[m], taps_x, taps_b) for m in range(1, GROUP)
    ]
    edges = edge_states(entries)
    state = message_ref[0, 0:HEAD].astype(f32)
    scale = jnp.ones((1, 128), f32)
    for m in range(1, GROUP):
        prefix_ref[m] = state
        scale_ref[m] = jnp.broadcast_to(scale, (8, 128))
        edge_ref[m] = edges[m - 1]
        state = decays[m] * (state + edges[m - 1]) + message_ref[m, 0:HEAD].astype(f32)
        scale = decays[m] * scale
    total_ref[0:HEAD] = state.astype(bf16)
    lane = iota((1, 128), 1)
    high, middle, _ = (p.astype(f32) for p in parts3(jnp.where(lane < HEAD, scalars[0], decays[0] * scale)))
    row = iota((8, 128), 0)
    first, last = tiles[0][:8], tiles[GROUP - 1]
    tile = jnp.where((row < EDGE) & (iota((8, 128), 1) >= HEAD), last[:8], first)
    tile = jnp.where(row == 6, high, jnp.where(row == 7, middle, tile))
    total_ref[HEAD:] = jnp.concatenate([tile, last[8:]], axis=0).astype(bf16)


def joined_kernel(lead_ref, total_ref, swapped_ref, taps_ref, joined_ref, own_ref):
    zeroth = lax.axis_index("seq") // GROUP == 0
    total, swapped = total_ref[...].astype(f32), swapped_ref[...].astype(f32)
    first, second = jnp.where(zeroth, total, swapped), jnp.where(zeroth, swapped, total)
    taps_x = taps_of(total[HEAD + 8 :])
    taps_b = [taps_ref[k : k + 1, :STATE] for k in range(4)]
    tiles = [first[HEAD:], second[HEAD:]]
    scalars = [t[6:7] + t[7:8] for t in tiles]
    edges = edge_states(
        [
            edge_rows(tiles[0][:8], None, None, scalars[0], taps_x, taps_b),
            edge_rows(tiles[1][:8], tiles[0][:8], tiles[0][8:], scalars[1], taps_x, taps_b),
        ]
    )
    state = all_lanes(scalars[0]) * edges[0] + first[:HEAD]
    state = all_lanes(scalars[1]) * (state + edges[1]) + second[:HEAD]
    joined_ref[0:HEAD] = state.astype(bf16)
    joined_ref[HEAD:] = tiles[1].astype(bf16)
    own_ref[...] = total_ref[...]


def entered(message_ref, taps_ref, near, crossed, third):
    own = message_ref[0, HEAD:].astype(f32)
    before = near[HEAD:] if third is None else jnp.where(third, crossed[HEAD:], near[HEAD:])
    taps_x = taps_of(own[8:])
    taps_b = [taps_ref[k : k + 1, :STATE] for k in range(4)]
    scalars = [t[6:7] + t[7:8] for t in (near[HEAD:], own)]
    edge, last = (None, None) if crossed is None else (crossed[HEAD : HEAD + 8], crossed[HEAD + 8 :])
    edges = edge_states(
        [
            edge_rows(near[HEAD : HEAD + 8], edge, last, scalars[0], taps_x, taps_b),
            edge_rows(own[:8], before[:8], before[8:], scalars[1], taps_x, taps_b),
        ]
    )
    if crossed is None:
        entering = all_lanes(scalars[0]) * edges[0] + near[:HEAD]
    else:
        entering = all_lanes(scalars[0]) * (crossed[:HEAD] + edges[0]) + near[:HEAD]
        entering = jnp.where(third, crossed[:HEAD], entering)
    return jnp.concatenate([entering + edges[1], before], axis=0)


def early_kernel(own_ref, message_ref, taps_ref, swapped_ref, early_ref):
    second = lax.axis_index("seq") // GROUP == 1
    near = jnp.where(second, swapped_ref[...].astype(f32), 0.0)
    early_ref[...] = entered(message_ref, taps_ref, near, None, None)


def entering_kernel(
    message_ref, taps_ref, prefix_ref, scale_ref, edge_ref, early_ref, crossed_ref, passed_ref, state_ref, entered_ref
):
    group = lax.axis_index("seq") // GROUP

    @pl.when(group < 2)
    def _():
        entered_ref[...] = early_ref[...]

    @pl.when(group >= 2)
    def _():
        crossed, near = crossed_ref[...].astype(f32), passed_ref[...].astype(f32)
        entered_ref[...] = entered(message_ref, taps_ref, near, crossed, group == 2)

    own = message_ref[0, HEAD:].astype(f32)
    entering = entered_ref[0:HEAD]
    state_ref[0, 0:HEAD] = entering.astype(bf16)
    state_ref[0, HEAD:] = entered_ref[HEAD:].astype(bf16)
    after_first = all_lanes(own[6:7] + own[7:8]) * entering
    for m in range(1, GROUP):
        state = prefix_ref[m] + scale_ref[m, 0:1] * after_first + edge_ref[m]
        state_ref[m, 0:HEAD] = state.astype(bf16)
        state_ref[m, HEAD:] = message_ref[m - 1, HEAD:]


def output_kernel(
    state_ref, bc_act_ref, first_x_ref, first_bc_ref, taps_x_ref, taps_bc_ref, lead_ref, gate_first_ref,
    local_ref, gate_ref, gain_ref, weight_ref, share_ref,
):
    row = iota((8, 128), 0)
    few = iota((8, 128), 1) < HEAD
    low_lanes = iota((HEAD, 128), 1) < HEAD
    tiles = [state_ref[h, HEAD:].astype(f32) for h in range(HEADS)]

    last_x = jnp.concatenate(
        [jnp.where(few, rolled(tiles[h][:8], HEAD, 1), tiles[h + 1][:8]) for h in range(0, HEADS, 2)], axis=1
    )
    last_c = jnp.zeros((8, 128), f32)
    for h in range(EDGE):
        last_c = jnp.where(row == h, tiles[h][15:16], last_c)
    last_bc = jnp.concatenate([tiles[0][8:], last_c], axis=1)
    last_x = jnp.where(iota((8, WIDTH), 0) < EDGE, last_x, 0.0)
    last_bc = jnp.where(iota((8, 2 * STATE), 0) < EDGE, last_bc, 0.0)
    taps_x = [taps_x_ref[k : k + 1] for k in range(4)]
    taps_bc = [taps_bc_ref[k : k + 1] for k in range(4)]
    act = rounded(silu(first_x_ref[...] + earlier_taps(last_x, taps_x)))
    bc_act = rounded(silu(first_bc_ref[...] + earlier_taps(last_bc, taps_bc)))
    b_first, c_first = bc_act[:, :STATE], bc_act[:, STATE:]
    lead = rounded(jnp.where(iota((8, WIDTH), 0) < EDGE, act * lead_ref[...], 0.0))

    pairs = []
    for pair in range(HEADS // 2):
        even = state_ref[2 * pair, 0:HEAD].astype(f32)
        odd = state_ref[2 * pair + 1, 0:HEAD].astype(f32)
        top = jnp.where(low_lanes, even, rolled(odd, HEAD, 1))
        bottom = jnp.where(low_lanes, rolled(even, HEAD, 1), odd)
        pairs.append(jnp.concatenate([top, bottom], axis=0))
    states = jnp.concatenate(pairs, axis=1)
    states = states.astype(bf16)
    c_rows = jnp.concatenate([c_first, bc_act_ref[:, STATE:].astype(f32)[8:]], axis=0).astype(bf16)
    gated = local_ref[...] + gate_ref[...] * dot(c_rows, states)
    ahead = jnp.zeros((8, WIDTH), f32)
    for s in range(1, EDGE):
        score = jnp.sum(c_first * b_first[s : s + 1], axis=1, keepdims=True)
        ahead = ahead + jnp.where(iota((8, WIDTH), 0) < s, score * lead[s : s + 1], 0.0)
    skipped = jnp.where(iota((8, WIDTH), 0) < EDGE, gate_first_ref[...] * act, 0.0)
    gated = jnp.concatenate([gated[0:8] + (skipped - gate_ref[0:8] * ahead), gated[8:]], axis=0)

    squares = jnp.sum(gated * gated, axis=1, keepdims=True)
    scaled = (gated * gain_ref[...]).astype(bf16)
    lane = iota((BLOCK, 128), 1)
    wide = jnp.zeros((BLOCK, 128), f32)
    for block in range(LENGTH // BLOCK):
        wide = jnp.where(lane == block, squares[block * BLOCK : (block + 1) * BLOCK], wide)
    high, middle, low = (p.astype(f32) for p in parts3(wide.T[0:8]))
    extra = jnp.where(row < 3, high, jnp.where(row < 6, rolled(middle, 3, 0), 0.0))
    extra = jnp.concatenate([extra, jnp.where(row < 3, low, 0.0)], axis=0).astype(bf16)
    for four in range(SHARES // 4):
        product = dot(scaled, weight_ref[:, 512 * four : 512 * (four + 1)]).astype(bf16)
        for k in range(4):
            share_ref[4 * four + k, 0:LENGTH] = product[:, 128 * k : 128 * (k + 1)]
            share_ref[4 * four + k, LENGTH:] = extra


def sum_kernel(share_ref, out_ref):
    total = share_ref[0].astype(f32)
    for d in range(1, SHARES):
        total = total + share_ref[d].astype(f32)
    extra = total[LENGTH:]
    for block in range(LENGTH // BLOCK):
        rows = slice(block * BLOCK, (block + 1) * BLOCK)
        squares = extra[block : block + 1] + (extra[block + 3 : block + 4] + extra[block + 8 : block + 9])
        scale = lax.rsqrt(squares / INNER + 1e-05)
        column = jnp.broadcast_to(scale, (128, 128)).T
        out_ref[rows] = (total[rows] * column).astype(bf16)


HERE = pl.BlockSpec(memory_space=pltpu.VMEM)
THERE = pl.BlockSpec(memory_space=pltpu.HBM)


def stay(a):
    return pltpu.with_memory_space_constraint(a, pltpu.HBM)


def call(kernel, outs, *args, specs=None, scratch=(), flops=1e8, transcendentals=0):
    return pl.pallas_call(
        kernel,
        out_shape=[jax.ShapeDtypeStruct(s, d) for s, d in outs],
        in_specs=specs or [HERE] * len(args),
        out_specs=[HERE] * len(outs),
        scratch_shapes=list(scratch),
        compiler_params=pltpu.CompilerParams(vmem_limit_bytes=32 * 1024 * 1024),
        cost_estimate=pl.CostEstimate(
            flops=int(flops), bytes_accessed=2_000_000, transcendentals=int(transcendentals)
        ),
    )(*(stay(a) if spec is THERE else a for a, spec in zip(args, specs or [HERE] * len(args))))


def shards(
    inner_x, gate_z, bc_input, conv_inner, conv_bc, step_size, log_decay, skip_gain, norm_gain, out_weight
):
    message, act, bc_act, cum, first_x, first_bc, taps_x, taps_bc, step, z, gain, skip = call(
        summary_kernel,
        [
            ((HEADS, HEAD + EXTRA, 128), bf16), ((LENGTH, WIDTH), bf16), ((LENGTH, 2 * STATE), bf16),
            ((HEADS, LENGTH), f32), ((8, WIDTH), f32), ((8, 2 * STATE), f32), ((4, WIDTH), f32), ((4, 2 * STATE), f32),
            ((HEADS, LENGTH), f32), ((LENGTH, WIDTH), bf16), ((1, WIDTH), f32), ((1, WIDTH), f32),
        ],
        inner_x, bc_input, conv_inner, conv_bc, step_size, log_decay, gate_z, norm_gain[None, :], skip_gain,
        specs=[THERE] * 9,
        scratch=[
            pltpu.VMEM((LENGTH + 8, WIDTH), f32), pltpu.VMEM((LENGTH + 8, 2 * STATE), f32),
            pltpu.VMEM((LENGTH + 8, WIDTH), f32), pltpu.VMEM((LENGTH + 8, 2 * STATE), f32),
            pltpu.VMEM((LENGTH, WIDTH), bf16), pltpu.VMEM((LENGTH, 2 * STATE), bf16),
            pltpu.VMEM((HEADS, LENGTH), f32), pltpu.SMEM((HEADS,), f32),
            pltpu.SemaphoreType.DMA((9,)),
        ],
    )
    groups = [list(range(i, i + GROUP)) for i in range(0, BLOCKS, GROUP)]
    message = lax.all_to_all(message, "seq", 0, 0, tiled=True, axis_index_groups=groups)
    prefix, scale, edge, total = call(
        prefix_kernel,
        [((GROUP, HEAD, 128), f32), ((GROUP, 8, 128), f32), ((GROUP, HEAD, 128), f32), ((HEAD + EXTRA, 128), bf16)],
        message, taps_bc,
    )
    def later(a, distance, first, last):
        return lax.ppermute(a, "seq", [(i, i + distance * GROUP) for i in range(first * GROUP, (last + 1) * GROUP)])

    def permuted(a, *ways):
        return lax.ppermute(a, "seq", [(i + f * GROUP, i + t * GROUP) for f, t in ways for i in range(GROUP)])

    swapped = permuted(total, (0, 1), (1, 0))
    local, gate, lead, gate_first = call(
        within_kernel,
        [((LENGTH, WIDTH), f32), ((LENGTH, WIDTH), f32), ((8, WIDTH), f32), ((8, WIDTH), f32)],
        act, bc_act, cum, step, skip, z, total,
        flops=2e9, transcendentals=1.2e6,
    )
    joined, own = call(
        joined_kernel,
        [((HEAD + EXTRA, 128), bf16), ((HEAD + EXTRA, 128), bf16)],
        lead, total, swapped, taps_bc,
    )
    crossed, passed = permuted(joined, (1, 2), (0, 3)), permuted(own, (2, 3))
    (early,) = call(early_kernel, [((HEAD + EXTRA, 128), f32)], own, message, taps_bc, swapped)
    (state,) = call(
        entering_kernel,
        [((GROUP, HEAD + EXTRA, 128), bf16)],
        message, taps_bc, prefix, scale, edge, early, crossed, passed,
        scratch=[pltpu.VMEM((HEAD + EXTRA, 128), f32)],
    )
    state = lax.all_to_all(state, "seq", 0, 0, tiled=True, axis_index_groups=groups)
    (share,) = call(
        output_kernel,
        [((SHARES, LENGTH + EXTRA, 128), bf16)],
        state, bc_act, first_x, first_bc, taps_x, taps_bc, lead, gate_first, local, gate, gain, out_weight,
        flops=9e8,
    )
    share = lax.all_to_all(share, "tp", 0, 0, tiled=True)
    (mixed,) = call(sum_kernel, [((LENGTH, 128), bf16)], share)
    return mixed


def solution(mesh):
    in_specs = (
        P("seq", "tp"),
        P("seq", "tp"),
        P("seq", None),
        P(None, "tp"),
        P(),
        P("tp", "seq"),
        P("tp", "seq"),
        P("tp"),
        P("tp"),
        P("tp", None),
    )
    return jax.shard_map(shards, mesh=mesh, in_specs=in_specs, out_specs=P("seq", "tp"), check_vma=False)
```

```python
import jax
import jax.numpy as jnp
from jax import lax
from jax.experimental import pallas as pl
from jax.experimental.pallas import tpu as pltpu
from jax.sharding import PartitionSpec as P

INNER = 8192
HEADS = 8
HEAD = 64
WIDTH = HEADS * HEAD
STATE = 128
LENGTH = 384
BLOCK = 128
BLOCKS = 32
GROUP = 8
SHARES = 16
EDGE = 3
EXTRA = 16

f32 = jnp.float32
bf16 = jnp.bfloat16


def parts3(a):
    high = a.astype(bf16)
    rest = a - high.astype(f32)
    middle = rest.astype(bf16)
    low = (rest - middle.astype(f32)).astype(bf16)
    return high, middle, low


def silu(a):
    return a * jax.nn.sigmoid(a)


def dot(a, b):
    return lax.dot_general(a, b, (((1,), (0,)), ((), ())), preferred_element_type=f32)


def columns_of(rows):
    padded = jnp.concatenate([rows, jnp.zeros((128 - rows.shape[0], rows.shape[1]), f32)], axis=0)
    return padded.T


def part_columns(rows):
    return columns_of(jnp.concatenate([p.astype(f32) for p in parts3(rows)], axis=0)).astype(bf16)


def spread_heads(columns):
    part = iota((128, WIDTH), 0)
    chosen = (part < 3 * HEADS) & (part % HEADS == iota((128, WIDTH), 1) // HEAD)
    return dot(columns, jnp.where(chosen, 1.0, 0.0).astype(bf16))


def rolled(a, distance, axis):
    return pltpu.roll(a, distance % a.shape[axis], axis)


def iota(shape, axis):
    return lax.broadcasted_iota(jnp.int32, shape, axis)


def before_taps(ext, late, weights):
    here, back = ext[8 : 8 + LENGTH], ext[7 : 7 + LENGTH]
    late[8:] = weights[1:2] * here + weights[0:1] * back
    return weights[3:4] * here + weights[2:3] * back + late[6 : 6 + LENGTH]


def earlier_taps(last, taps):
    total = taps[0] * last + taps[1] * rolled(last, -1, 0) + taps[2] * rolled(last, -2, 0)
    return jnp.where(iota(last.shape, 0) < EDGE, total, 0.0)


def own_taps(first, taps):
    return taps[3] * first + taps[2] * rolled(first, 1, 0) + taps[1] * rolled(first, 2, 0)


def rounded(a):
    return a.astype(bf16).astype(f32)


def fetch(pairs, sems):
    copies = [pltpu.make_async_copy(there, here, sems.at[i]) for i, (there, here) in enumerate(pairs)]
    for copy in copies:
        copy.start()
    return copies


def summary_kernel(
    x_at, bc_at, cx_at, cbc_at, step_at, decay_at, z_at, gain_at, skip_at,
    message_ref, act_ref, bc_act_ref, cum_ref, first_x_ref, first_bc_ref, taps_x_ref, taps_bc_ref,
    step_ref, z_ref, gain_ref, skip_row_ref,
    ext_x, ext_bc, late_x, late_bc, x_ref, bc_ref, decay_ref, skip_ref, sems,
):
    copies = fetch(
        [
            (decay_at, decay_ref), (step_at, step_ref), (cx_at, taps_x_ref),
            (cbc_at, taps_bc_ref), (bc_at, bc_ref), (x_at, x_ref),
            (z_at, z_ref), (gain_at, gain_ref), (skip_at, skip_ref),
        ],
        sems,
    )
    copies[0].wait()
    copies[1].wait()
    upto = jnp.where(iota((LENGTH, LENGTH), 0) <= iota((LENGTH, LENGTH), 1), 1.0, 0.0).astype(bf16)
    sums = dot(jnp.concatenate([p.astype(f32) for p in parts3(decay_ref[...])], axis=0).astype(bf16), upto)
    cum = sums[0:8] + (sums[8:16] + sums[16:24])
    cum_ref[...] = cum
    last = cum[:, LENGTH - 1 : LENGTH]
    factor = step_ref[...] * jnp.exp(last - cum)
    inside = jnp.where(iota((HEADS, LENGTH), 1) < EDGE, 0.0, factor)
    factor_spread = spread_heads(part_columns(inside))
    for copy in copies[2:6]:
        copy.wait()
    ext_x[0:8] = jnp.zeros((8, WIDTH), f32)
    ext_bc[0:8] = jnp.zeros((8, 2 * STATE), f32)
    ext_x[8:] = x_ref[...].astype(f32)
    ext_bc[8:] = bc_ref[...].astype(f32)
    late_bc[0:8] = jnp.zeros((8, 2 * STATE), f32)
    late_x[0:8] = jnp.zeros((8, WIDTH), f32)
    sums = before_taps(ext_bc, late_bc, taps_bc_ref)
    first_bc_ref[...] = sums[0:8]
    bc_act = silu(sums).astype(bf16)
    bc_act_ref[...] = bc_act
    sums = before_taps(ext_x, late_x, taps_x_ref)
    first_x_ref[...] = sums[0:8]
    act = silu(sums).astype(bf16)
    act_ref[...] = act

    weighted = (act.astype(f32) * factor_spread).astype(bf16)
    b_rows = bc_act[:, :STATE].astype(f32)
    summary = dot(b_rows.T.astype(bf16), weighted)

    total = jnp.broadcast_to(jnp.exp(last), (HEADS, 128))
    lane = iota((HEADS, 128), 1)
    lead = step_ref[:, :128] * jnp.exp(jnp.where(lane < EDGE, -cum[:, :128], 0.0))
    scalars = jnp.where(lane < HEAD, lead, total)
    high, middle, _ = (p.astype(f32) for p in parts3(scalars))
    tap_high, tap_middle, _ = (p.astype(f32) for p in parts3(taps_x_ref[...]))
    low_lanes = iota((HEAD, 128), 1) < HEAD
    few = iota((8, 128), 1) < HEAD
    row = iota((8, 128), 0)
    b_first = rolled(ext_bc[8:16, :STATE], 3, 0)
    bc_last = rolled(ext_bc[LENGTH : LENGTH + 8], 3, 0)
    for h in range(HEADS):
        lanes = slice(128 * (h // 2), 128 * (h // 2 + 1))
        even = h % 2 == 0

        def side_by_side(left, right, where):
            if even:
                return jnp.where(where, left, rolled(right, HEAD, 1))
            return jnp.where(where, rolled(left, HEAD, 1), right)

        message_ref[h, 0:HEAD] = side_by_side(summary[:HEAD, lanes], summary[HEAD:, lanes], low_lanes).astype(bf16)
        x_edges = side_by_side(ext_x[8:16, lanes], rolled(ext_x[LENGTH : LENGTH + 8, lanes], 3, 0), few)
        tile = jnp.where(row < 3, x_edges, b_first)
        tile = jnp.where(row == 6, high[h : h + 1], jnp.where(row == 7, middle[h : h + 1], tile))
        other = bc_last[:, :STATE]
        for at, (part, k) in enumerate(((tap_high, 0), (tap_high, 2), (tap_middle, 0), (tap_middle, 2))):
            pair = side_by_side(part[k : k + 1, lanes], part[k + 1 : k + 2, lanes], few[0:1])
            other = jnp.where(row == 3 + at, pair, other)
        c_row = bc_last[h : h + 1, STATE:] if h < EDGE else jnp.zeros((1, STATE), f32)
        other = jnp.where(row == 7, c_row, other)
        message_ref[h, HEAD:] = jnp.concatenate([tile, other], axis=0).astype(bf16)

    for copy in copies[6:]:
        copy.wait()
    head_at = iota((1, WIDTH), 1) // HEAD
    skip = jnp.zeros((1, WIDTH), f32)
    for h in range(HEADS):
        skip = jnp.where(head_at == h, skip_ref[h], skip)
    skip_row_ref[...] = skip


def within_kernel(
    act_ref, bc_act_ref, cum_ref, step_ref, skip_row_ref, z_ref, after_ref,
    local_ref, gate_ref, lead_ref, gate_first_ref,
):
    skip = skip_row_ref[...]
    cum = cum_ref[...]
    cum_columns = columns_of(cum)
    act = act_ref[...].astype(f32)
    step = step_ref[...]
    inside = jnp.where(iota((HEADS, LENGTH), 1) < EDGE, 0.0, step)
    scaled = (act * spread_heads(part_columns(inside))).astype(bf16)
    early = iota((HEADS, 128), 1) < 8
    lead = jnp.where(early, step[:, :128] * jnp.exp(jnp.where(early, -cum[:, :128], 0.0)), 0.0)
    lead_ref[...] = spread_heads(part_columns(lead)[0:16])[0:8]
    cum_spread = spread_heads(part_columns(jnp.exp(cum)))
    gate = silu(z_ref[...].astype(f32))
    gate_first_ref[...] = gate[0:8] * skip
    gate_ref[...] = gate * cum_spread
    b_rows = bc_act_ref[:, :STATE]
    c_rows = bc_act_ref[:, STATE:]
    skipped = jnp.where(iota((LENGTH, WIDTH), 0) < EDGE, 0.0, skip * act)
    t_at = lax.broadcasted_iota(jnp.int32, (BLOCK, BLOCK), 0)
    s_at = lax.broadcasted_iota(jnp.int32, (BLOCK, BLOCK), 1)
    causal = t_at >= s_at
    low_lanes = lax.broadcasted_iota(jnp.int32, (BLOCK, 128), 1) < HEAD
    for block in range(LENGTH // BLOCK):
        rows = slice(block * BLOCK, (block + 1) * BLOCK)
        scores = lax.dot_general(
            c_rows[rows], b_rows[: (block + 1) * BLOCK], (((1,), (1,)), ((), ())), preferred_element_type=f32
        )
        for pair in range(HEADS // 2):
            lanes = slice(128 * pair, 128 * (pair + 1))
            mixing = []
            for h in (2 * pair, 2 * pair + 1):
                here = cum_columns[rows, h : h + 1]
                tiles = []
                for other in range(block + 1):
                    columns = slice(other * BLOCK, (other + 1) * BLOCK)
                    spread = here - cum[h : h + 1, columns]
                    if other == block:
                        spread = jnp.where(causal, spread, -jnp.inf)
                    tiles.append((scores[:, columns] * jnp.exp(spread)).astype(bf16))
                mixing.append(tiles[0] if block == 0 else jnp.concatenate(tiles, axis=1))
            sums = dot(jnp.concatenate(mixing, axis=0), scaled[: (block + 1) * BLOCK, lanes])
            within = jnp.where(low_lanes, sums[:BLOCK], sums[BLOCK:])
            local_ref[rows, lanes] = (within + skipped[rows, lanes]) * gate[rows, lanes]


def all_lanes(row):
    return jnp.where(iota((1, 128), 1) < HEAD, rolled(row, HEAD, 1), row)


def taps_of(tile):
    pairs = tile[3:5] + tile[5:7]
    return [pairs[0:1], rolled(pairs[0:1], HEAD, 1), pairs[1:2], rolled(pairs[1:2], HEAD, 1)]


def edge_rows(tile, before, before_last, scalars, taps_x, taps_b):
    row = iota((8, 128), 0)
    lane = iota((8, 128), 1)
    sums = own_taps(jnp.where(row < EDGE, tile, 0.0), taps_x)
    sums_b = own_taps(jnp.where(row < EDGE, rolled(tile, -EDGE, 0), 0.0), taps_b)
    if before is not None:
        sums = sums + earlier_taps(jnp.where(row < EDGE, rolled(before, HEAD, 1), 0.0), taps_x)
        sums_b = sums_b + earlier_taps(jnp.where(row < EDGE, before_last, 0.0), taps_b)
    factor = jnp.sum(jnp.where(lane == row, scalars, 0.0), axis=1, keepdims=True)
    weighted = rounded(silu(sums)) * factor
    weighted = jnp.where((row < EDGE) & (lane < HEAD), weighted, 0.0)
    return weighted, jnp.where(row < EDGE, rounded(silu(sums_b)), 0.0)


def edge_states(entries):
    zeros = jnp.zeros((HEAD - 8 * len(entries), 128), f32)
    pad = [zeros] if zeros.shape[0] else []
    weighted = jnp.concatenate([e[0] for e in entries] + pad, axis=0)
    weighted = jnp.concatenate([weighted, rolled(weighted, HEAD, 1)], axis=0)
    b_rows = jnp.concatenate([e[1] for e in entries] + pad + [jnp.zeros((HEAD, 128), f32)], axis=0).T
    left = jnp.where(iota((HEAD, 128), 1) < HEAD, b_rows[:HEAD], rolled(b_rows[HEAD:], HEAD, 1)).astype(bf16)
    owner = (iota((128, 128), 0) % HEAD) // 8
    return [dot(left, jnp.where(owner == e, weighted, 0.0).astype(bf16)) for e in range(len(entries))]


def prefix_kernel(message_ref, taps_ref, prefix_ref, scale_ref, edge_ref, total_ref):
    tiles = [message_ref[m, HEAD:].astype(f32) for m in range(GROUP)]
    scalars = [t[6:7] + t[7:8] for t in tiles]
    decays = [all_lanes(s) for s in scalars]
    taps_x = taps_of(tiles[0][8:])
    taps_b = [taps_ref[k : k + 1, :STATE] for k in range(4)]
    entries = [
        edge_rows(tiles[m][:8], tiles[m - 1][:8], tiles[m - 1][8:], scalars[m], taps_x, taps_b) for m in range(1, GROUP)
    ]
    edges = edge_states(entries)
    state = message_ref[0, 0:HEAD].astype(f32)
    scale = jnp.ones((1, 128), f32)
    for m in range(1, GROUP):
        prefix_ref[m] = state
        scale_ref[m] = jnp.broadcast_to(scale, (8, 128))
        edge_ref[m] = edges[m - 1]
        state = decays[m] * (state + edges[m - 1]) + message_ref[m, 0:HEAD].astype(f32)
        scale = decays[m] * scale
    total_ref[0:HEAD] = state.astype(bf16)
    lane = iota((1, 128), 1)
    high, middle, _ = (p.astype(f32) for p in parts3(jnp.where(lane < HEAD, scalars[0], decays[0] * scale)))
    row = iota((8, 128), 0)
    first, last = tiles[0][:8], tiles[GROUP - 1]
    tile = jnp.where((row < EDGE) & (iota((8, 128), 1) >= HEAD), last[:8], first)
    tile = jnp.where(row == 6, high, jnp.where(row == 7, middle, tile))
    total_ref[HEAD:] = jnp.concatenate([tile, last[8:]], axis=0).astype(bf16)


def joined_kernel(lead_ref, total_ref, swapped_ref, taps_ref, joined_ref, own_ref):
    zeroth = lax.axis_index("seq") // GROUP == 0
    total, swapped = total_ref[...].astype(f32), swapped_ref[...].astype(f32)
    first, second = jnp.where(zeroth, total, swapped), jnp.where(zeroth, swapped, total)
    taps_x = taps_of(total[HEAD + 8 :])
    taps_b = [taps_ref[k : k + 1, :STATE] for k in range(4)]
    tiles = [first[HEAD:], second[HEAD:]]
    scalars = [t[6:7] + t[7:8] for t in tiles]
    edges = edge_states(
        [
            edge_rows(tiles[0][:8], None, None, scalars[0], taps_x, taps_b),
            edge_rows(tiles[1][:8], tiles[0][:8], tiles[0][8:], scalars[1], taps_x, taps_b),
        ]
    )
    state = all_lanes(scalars[0]) * edges[0] + first[:HEAD]
    state = all_lanes(scalars[1]) * (state + edges[1]) + second[:HEAD]
    joined_ref[0:HEAD] = state.astype(bf16)
    joined_ref[HEAD:] = tiles[1].astype(bf16)
    own_ref[...] = total_ref[...]


def entered(message_ref, taps_ref, near, crossed, third):
    own = message_ref[0, HEAD:].astype(f32)
    before = near[HEAD:] if third is None else jnp.where(third, crossed[HEAD:], near[HEAD:])
    taps_x = taps_of(own[8:])
    taps_b = [taps_ref[k : k + 1, :STATE] for k in range(4)]
    scalars = [t[6:7] + t[7:8] for t in (near[HEAD:], own)]
    edge, last = (None, None) if crossed is None else (crossed[HEAD : HEAD + 8], crossed[HEAD + 8 :])
    edges = edge_states(
        [
            edge_rows(near[HEAD : HEAD + 8], edge, last, scalars[0], taps_x, taps_b),
            edge_rows(own[:8], before[:8], before[8:], scalars[1], taps_x, taps_b),
        ]
    )
    if crossed is None:
        entering = all_lanes(scalars[0]) * edges[0] + near[:HEAD]
    else:
        entering = all_lanes(scalars[0]) * (crossed[:HEAD] + edges[0]) + near[:HEAD]
        entering = jnp.where(third, crossed[:HEAD], entering)
    return jnp.concatenate([entering + edges[1], before], axis=0)


def early_kernel(own_ref, message_ref, taps_ref, swapped_ref, early_ref):
    second = lax.axis_index("seq") // GROUP == 1
    near = jnp.where(second, swapped_ref[...].astype(f32), 0.0)
    early_ref[...] = entered(message_ref, taps_ref, near, None, None)


def entering_kernel(
    message_ref, taps_ref, prefix_ref, scale_ref, edge_ref, early_ref, crossed_ref, passed_ref, state_ref, entered_ref
):
    group = lax.axis_index("seq") // GROUP

    @pl.when(group < 2)
    def _():
        entered_ref[...] = early_ref[...]

    @pl.when(group >= 2)
    def _():
        crossed, near = crossed_ref[...].astype(f32), passed_ref[...].astype(f32)
        entered_ref[...] = entered(message_ref, taps_ref, near, crossed, group == 2)

    own = message_ref[0, HEAD:].astype(f32)
    entering = entered_ref[0:HEAD]
    state_ref[0, 0:HEAD] = entering.astype(bf16)
    state_ref[0, HEAD:] = entered_ref[HEAD:].astype(bf16)
    after_first = all_lanes(own[6:7] + own[7:8]) * entering
    for m in range(1, GROUP):
        state = prefix_ref[m] + scale_ref[m, 0:1] * after_first + edge_ref[m]
        state_ref[m, 0:HEAD] = state.astype(bf16)
        state_ref[m, HEAD:] = message_ref[m - 1, HEAD:]


def output_kernel(
    state_ref, bc_act_ref, first_x_ref, first_bc_ref, taps_x_ref, taps_bc_ref, lead_ref, gate_first_ref,
    local_ref, gate_ref, gain_ref, weight_ref, share_ref,
):
    row = iota((8, 128), 0)
    few = iota((8, 128), 1) < HEAD
    low_lanes = iota((HEAD, 128), 1) < HEAD
    tiles = [state_ref[h, HEAD:].astype(f32) for h in range(HEADS)]

    last_x = jnp.concatenate(
        [jnp.where(few, rolled(tiles[h][:8], HEAD, 1), tiles[h + 1][:8]) for h in range(0, HEADS, 2)], axis=1
    )
    last_c = jnp.zeros((8, 128), f32)
    for h in range(EDGE):
        last_c = jnp.where(row == h, tiles[h][15:16], last_c)
    last_bc = jnp.concatenate([tiles[0][8:], last_c], axis=1)
    last_x = jnp.where(iota((8, WIDTH), 0) < EDGE, last_x, 0.0)
    last_bc = jnp.where(iota((8, 2 * STATE), 0) < EDGE, last_bc, 0.0)
    taps_x = [taps_x_ref[k : k + 1] for k in range(4)]
    taps_bc = [taps_bc_ref[k : k + 1] for k in range(4)]
    act = rounded(silu(first_x_ref[...] + earlier_taps(last_x, taps_x)))
    bc_act = rounded(silu(first_bc_ref[...] + earlier_taps(last_bc, taps_bc)))
    b_first, c_first = bc_act[:, :STATE], bc_act[:, STATE:]
    lead = rounded(jnp.where(iota((8, WIDTH), 0) < EDGE, act * lead_ref[...], 0.0))

    pairs = []
    for pair in range(HEADS // 2):
        even = state_ref[2 * pair, 0:HEAD].astype(f32)
        odd = state_ref[2 * pair + 1, 0:HEAD].astype(f32)
        top = jnp.where(low_lanes, even, rolled(odd, HEAD, 1))
        bottom = jnp.where(low_lanes, rolled(even, HEAD, 1), odd)
        pairs.append(jnp.concatenate([top, bottom], axis=0))
    states = jnp.concatenate(pairs, axis=1)
    states = states.astype(bf16)
    c_rows = jnp.concatenate([c_first, bc_act_ref[:, STATE:].astype(f32)[8:]], axis=0).astype(bf16)
    gated = local_ref[...] + gate_ref[...] * dot(c_rows, states)
    ahead = jnp.zeros((8, WIDTH), f32)
    for s in range(1, EDGE):
        score = jnp.sum(c_first * b_first[s : s + 1], axis=1, keepdims=True)
        ahead = ahead + jnp.where(iota((8, WIDTH), 0) < s, score * lead[s : s + 1], 0.0)
    skipped = jnp.where(iota((8, WIDTH), 0) < EDGE, gate_first_ref[...] * act, 0.0)
    gated = jnp.concatenate([gated[0:8] + (skipped - gate_ref[0:8] * ahead), gated[8:]], axis=0)

    squares = jnp.sum(gated * gated, axis=1, keepdims=True)
    scaled = (gated * gain_ref[...]).astype(bf16)
    lane = iota((BLOCK, 128), 1)
    wide = jnp.zeros((BLOCK, 128), f32)
    for block in range(LENGTH // BLOCK):
        wide = jnp.where(lane == block, squares[block * BLOCK : (block + 1) * BLOCK], wide)
    high, middle, low = (p.astype(f32) for p in parts3(wide.T[0:8]))
    extra = jnp.where(row < 3, high, jnp.where(row < 6, rolled(middle, 3, 0), 0.0))
    extra = jnp.concatenate([extra, jnp.where(row < 3, low, 0.0)], axis=0).astype(bf16)
    for pair in range(SHARES // 2):
        product = dot(scaled, weight_ref[:, 256 * pair : 256 * (pair + 1)]).astype(bf16)
        share_ref[2 * pair, 0:LENGTH] = product[:, :128]
        share_ref[2 * pair, LENGTH:] = extra
        share_ref[2 * pair + 1, 0:LENGTH] = product[:, 128:]
        share_ref[2 * pair + 1, LENGTH:] = extra


def sum_kernel(share_ref, out_ref):
    def summed(rows):
        parts = [share_ref[d, rows].astype(f32) for d in range(SHARES)]
        while len(parts) > 1:
            parts = [x + y for x, y in zip(parts[::2], parts[1::2])]
        return parts[0]

    extra = summed(slice(LENGTH, LENGTH + EXTRA))
    for block in range(LENGTH // BLOCK):
        squares = extra[block : block + 1] + (extra[block + 3 : block + 4] + extra[block + 8 : block + 9])
        scale = lax.rsqrt(squares / INNER + 1e-05)
        column = jnp.broadcast_to(scale, (128, 128)).T
        rows = slice(block * BLOCK, (block + 1) * BLOCK)
        out_ref[rows] = (summed(rows) * column).astype(bf16)


HERE = pl.BlockSpec(memory_space=pltpu.VMEM)
THERE = pl.BlockSpec(memory_space=pltpu.HBM)


def stay(a):
    return pltpu.with_memory_space_constraint(a, pltpu.HBM)


def call(kernel, outs, *args, specs=None, scratch=(), flops=1e8, transcendentals=0):
    return pl.pallas_call(
        kernel,
        out_shape=[jax.ShapeDtypeStruct(s, d) for s, d in outs],
        in_specs=specs or [HERE] * len(args),
        out_specs=[HERE] * len(outs),
        scratch_shapes=list(scratch),
        compiler_params=pltpu.CompilerParams(vmem_limit_bytes=32 * 1024 * 1024),
        cost_estimate=pl.CostEstimate(
            flops=int(flops), bytes_accessed=2_000_000, transcendentals=int(transcendentals)
        ),
    )(*(stay(a) if spec is THERE else a for a, spec in zip(args, specs or [HERE] * len(args))))


def shards(
    inner_x, gate_z, bc_input, conv_inner, conv_bc, step_size, log_decay, skip_gain, norm_gain, out_weight
):
    message, act, bc_act, cum, first_x, first_bc, taps_x, taps_bc, step, z, gain, skip = call(
        summary_kernel,
        [
            ((HEADS, HEAD + EXTRA, 128), bf16), ((LENGTH, WIDTH), bf16), ((LENGTH, 2 * STATE), bf16),
            ((HEADS, LENGTH), f32), ((8, WIDTH), f32), ((8, 2 * STATE), f32), ((4, WIDTH), f32), ((4, 2 * STATE), f32),
            ((HEADS, LENGTH), f32), ((LENGTH, WIDTH), bf16), ((1, WIDTH), f32), ((1, WIDTH), f32),
        ],
        inner_x, bc_input, conv_inner, conv_bc, step_size, log_decay, gate_z, norm_gain[None, :], skip_gain,
        specs=[THERE] * 9,
        scratch=[
            pltpu.VMEM((LENGTH + 8, WIDTH), f32), pltpu.VMEM((LENGTH + 8, 2 * STATE), f32),
            pltpu.VMEM((LENGTH + 8, WIDTH), f32), pltpu.VMEM((LENGTH + 8, 2 * STATE), f32),
            pltpu.VMEM((LENGTH, WIDTH), bf16), pltpu.VMEM((LENGTH, 2 * STATE), bf16),
            pltpu.VMEM((HEADS, LENGTH), f32), pltpu.SMEM((HEADS,), f32),
            pltpu.SemaphoreType.DMA((9,)),
        ],
    )
    groups = [list(range(i, i + GROUP)) for i in range(0, BLOCKS, GROUP)]
    message = lax.all_to_all(message, "seq", 0, 0, tiled=True, axis_index_groups=groups)
    prefix, scale, edge, total = call(
        prefix_kernel,
        [((GROUP, HEAD, 128), f32), ((GROUP, 8, 128), f32), ((GROUP, HEAD, 128), f32), ((HEAD + EXTRA, 128), bf16)],
        message, taps_bc,
    )
    def later(a, distance, first, last):
        return lax.ppermute(a, "seq", [(i, i + distance * GROUP) for i in range(first * GROUP, (last + 1) * GROUP)])

    def permuted(a, *ways):
        return lax.ppermute(a, "seq", [(i + f * GROUP, i + t * GROUP) for f, t in ways for i in range(GROUP)])

    swapped = permuted(total, (0, 1), (1, 0))
    local, gate, lead, gate_first = call(
        within_kernel,
        [((LENGTH, WIDTH), f32), ((LENGTH, WIDTH), f32), ((8, WIDTH), f32), ((8, WIDTH), f32)],
        act, bc_act, cum, step, skip, z, total,
        flops=2e9, transcendentals=1.2e6,
    )
    joined, own = call(
        joined_kernel,
        [((HEAD + EXTRA, 128), bf16), ((HEAD + EXTRA, 128), bf16)],
        lead, total, swapped, taps_bc,
    )
    crossed, passed = permuted(joined, (1, 2), (0, 3)), permuted(own, (2, 3))
    (early,) = call(early_kernel, [((HEAD + EXTRA, 128), f32)], own, message, taps_bc, swapped)
    (state,) = call(
        entering_kernel,
        [((GROUP, HEAD + EXTRA, 128), bf16)],
        message, taps_bc, prefix, scale, edge, early, crossed, passed,
        scratch=[pltpu.VMEM((HEAD + EXTRA, 128), f32)],
    )
    state = lax.all_to_all(state, "seq", 0, 0, tiled=True, axis_index_groups=groups)
    (share,) = call(
        output_kernel,
        [((SHARES, LENGTH + EXTRA, 128), bf16)],
        state, bc_act, first_x, first_bc, taps_x, taps_bc, lead, gate_first, local, gate, gain, out_weight,
        flops=9e8,
    )
    share = lax.all_to_all(share, "tp", 0, 0, tiled=True)
    (mixed,) = call(sum_kernel, [((LENGTH, 128), bf16)], share)
    return mixed


def solution(mesh):
    in_specs = (
        P("seq", "tp"),
        P("seq", "tp"),
        P("seq", None),
        P(None, "tp"),
        P(),
        P("tp", "seq"),
        P("tp", "seq"),
        P("tp"),
        P("tp"),
        P("tp", None),
    )
    return jax.shard_map(shards, mesh=mesh, in_specs=in_specs, out_specs=P("seq", "tp"), check_vma=False)
```
